32 devices in a mesh: samples: 4 (over z), rows: 8 (over y, x, core).
Axes of the slice: x: 2, y: 2, z: 4, core: 2. Of those that a mesh axis runs over, the one named last changes fastest.
Arguments:
- x_big: bfloat16 [112, 4, 48, 16384], P('samples', None, None, 'rows'), may hold values from -6 to 6
- x_small: bfloat16 [8, 4, 48, 4096], P('samples', None, None, 'rows'), may hold values from -6 to 6
- spec_weight: bfloat16 [256, 4, 48, 48], P('rows'), may hold values from -0.4375 to 0.4375
- lin_weight: bfloat16 [4, 48, 48], replicated, may hold values from -0.4375 to 0.4375
- lin_bias: bfloat16 [4, 48], replicated, may hold values from -3 to 3
- grad_big: bfloat16 [112, 4, 48, 16384], P('samples', None, None, 'rows'), may hold values from -6 to 6
- grad_small: bfloat16 [8, 4, 48, 4096], P('samples', None, None, 'rows'), may hold values from -6 to 6
Outputs:
- out_big: bfloat16 [112, 4, 48, 16384], P('samples', None, None, 'rows')
- out_small: bfloat16 [8, 4, 48, 4096], P('samples', None, None, 'rows')
- dx_big: float32 [112, 4, 48, 16384], P('samples', None, None, 'rows')
- dx_small: float32 [8, 4, 48, 4096], P('samples', None, None, 'rows')
- d_spec_weight: float32 [256, 4, 48, 48], P('rows')
- d_lin_weight: float32 [4, 48, 48], replicated
- d_lin_bias: float32 [4, 48], replicated
The draws below stay inside these ranges and needn't reach their ends.
All inputs are finite; a program needn't handle non-finite values.
Results may differ from the reference program's by a relative error of at most 0.014.
Values may be sent and summed in bfloat16 or wider, within the bound.
A program may use at most 384 MiB of HBM per device.

```python
import math
import jax
import jax.numpy as jnp
from jax import lax

C = 48
MX = 16
N1 = 128
N2 = 64
NB = 112
NS = 8


def shard_levels(key, shape, shards, low, largest):
    def one(dim, shards_of):
        steps = jax.random.uniform(jax.random.fold_in(jax.random.fold_in(key, 6), dim), (shards_of,), jnp.float32, low / len(shards), largest / len(shards))
        return jnp.repeat(jnp.exp(steps), shape[dim] // shards_of).reshape((-1,) + (1,) * (len(shape) - dim - 1))

    level = one(*shards[0])
    for cut in shards[1:]:
        level = level * one(*cut)
    return level


def scatter_about(rng, dims, scale, reach, split=(), kind=jnp.bfloat16):
    entries = jax.random.normal(rng, dims, jnp.float32) * scale
    if len(split) > 0:
        entries = shard_levels(rng, dims, split, -0.22, 0.18) * entries
    return jnp.clip(entries, min=-reach, max=reach).astype(kind)


def setup_inputs(seed: int = 0) -> dict:
    key_list = jax.random.split(jax.random.key(seed), 8)
    return {
        "x_big": scatter_about(key_list[0], (NB, 4, C, N1 * N1), 1.0, 6.0, ((0, 4), (3, 8))),
        "x_small": scatter_about(key_list[1], (NS, 4, C, N2 * N2), 1.0, 6.0, ((0, 4), (3, 8))),
        "spec_weight": scatter_about(key_list[2], (MX * MX, 4, C, C), (4 * C) ** -0.5, 0.4375, ((0, 8),)),
        "lin_weight": scatter_about(key_list[3], (4, C, C), (4 * C) ** -0.5, 0.4375),
        "lin_bias": scatter_about(key_list[4], (4, C), 0.5, 3.0),
        "grad_big": scatter_about(key_list[5], (NB, 4, C, N1 * N1), 1.0, 6.0, ((0, 4), (3, 8))),
        "grad_small": scatter_about(key_list[6], (NS, 4, C, N2 * N2), 1.0, 6.0, ((0, 4), (3, 8))),
    }


@jax.custom_vjp
def low(v):
    return lax.optimization_barrier(v.astype(jnp.bfloat16)).astype(jnp.float32)

@jax.custom_vjp
def low_back(v):
    return v

def low_keep(v):
    return (low(v), None)

def low_pass(kept, grad):
    return (grad,)

def back_keep(v):
    return (v, None)

def back_low(kept, grad):
    return (low(grad),)
low.defvjp(low_keep, low_pass)
low_back.defvjp(back_keep, back_low)

def kept_freqs(mode_ids, grid_side):
    return jnp.where(mode_ids < MX // 2, mode_ids, grid_side - MX + mode_ids)

def trig_pair(phases, grid_side):
    angles = phases.astype(jnp.float32) * (2.0 * math.pi / grid_side)
    return (low(jnp.cos(angles)), low(jnp.sin(angles)))

def combine(leading, second, sign_flip, axis_at):
    left_parts = [lax.index_in_dim(leading, blade_id, axis_at, keepdims=False) for blade_id in range(4)]
    right_parts = [lax.index_in_dim(second, blade_id, axis_at, keepdims=False) for blade_id in range(4)]
    return jnp.stack([left_parts[0] + sign_flip * right_parts[3], left_parts[1] + sign_flip * right_parts[2], left_parts[2] - sign_flip * right_parts[1], left_parts[3] - sign_flip * right_parts[0]], axis=axis_at)

def build_kernel(weights):
    rows_list = []
    for source in range(4):
        blocks = []
        for target in range(4):
            blade_id = source ^ target
            block_part = weights[..., blade_id, :, :]
            if blade_id >> 1 & source & 1:
                block_part = -block_part
            blocks.append(block_part)
        rows_list.append(jnp.concatenate(blocks, axis=-1))
    return jnp.concatenate(rows_list, axis=-2)

def precise(pattern, operand, factor):
    return jnp.einsum(pattern, operand, factor, precision=lax.Precision.HIGHEST)

def clifford_layer(grid_field, spec_weight, lin_weight, lin_bias):
    grid_side = grid_field.shape[-1]
    comp_width = 4 * C
    mode_ids = jnp.arange(MX, dtype=jnp.int32)
    cell_ids = jnp.arange(grid_side, dtype=jnp.int32)
    cos_table, sin_table = trig_pair(cell_ids[:, None] * kept_freqs(mode_ids, grid_side)[None, :] % grid_side, grid_side)
    column = combine(precise('bchw,wk->bchk', grid_field, cos_table), precise('bchw,wk->bchk', grid_field, sin_table), 1.0, 0)
    column = low(low_back(column * (1.0 / grid_side)))
    spectrum = combine(precise('bchk,ha->bcak', column, cos_table), precise('bchk,ha->bcak', column, sin_table), 1.0, 0)
    spectrum = low(low_back(spectrum)).transpose(2, 3, 0, 1).reshape(MX * MX, comp_width)
    mixed_modes = precise('mi,mio->mo', spectrum, build_kernel(spec_weight))
    mixed_modes = low(low_back(mixed_modes)).reshape(MX, MX, 4, C).transpose(2, 3, 0, 1)
    back_rows = combine(precise('bcak,ha->bchk', mixed_modes, cos_table), precise('bcak,ha->bchk', mixed_modes, sin_table), -1.0, 0)
    back_rows = low(low_back(back_rows * (1.0 / MX)))
    spectral = combine(precise('bchk,wk->bchw', back_rows, cos_table), precise('bchk,wk->bchw', back_rows, sin_table), -1.0, 0)
    flat_field = grid_field.reshape(comp_width, grid_side, grid_side)
    linear = precise('ihw,io->ohw', flat_field, build_kernel(lin_weight)) + lin_bias.reshape(comp_width)[:, None, None]
    before = low_back(spectral.reshape(comp_width, grid_side, grid_side) + linear)
    return (flat_field + jax.nn.gelu(before)).reshape(grid_field.shape)

def reference(x_big, x_small, spec_weight, lin_weight, lin_bias, grad_big, grad_small):
    weights = (spec_weight.astype(jnp.float32), lin_weight.astype(jnp.float32), lin_bias.astype(jnp.float32))
    zero_grads = tuple((jnp.zeros_like(weight_one) for weight_one in weights))

    def run_group(totals, fields, cotangents, grid_side):

        def sample_step(running_sums, inputs_pair):
            grid_field, cotangent = inputs_pair
            square = (4, C, grid_side, grid_side)
            result, pullback = jax.vjp(clifford_layer, grid_field.astype(jnp.float32).reshape(square), *weights)
            pulled = pullback(cotangent.astype(jnp.float32).reshape(square))
            running_sums = tuple((running + update for running, update in zip(running_sums, pulled[1:])))
            return (running_sums, (result.astype(jnp.bfloat16).reshape(grid_field.shape), pulled[0].reshape(grid_field.shape)))
        return lax.scan(sample_step, totals, (fields, cotangents))
    totals, (out_big, dx_big) = run_group(zero_grads, x_big, grad_big, N1)
    totals, (out_small, dx_small) = run_group(totals, x_small, grad_small, N2)
    return (out_big, out_small, dx_big, dx_small, totals[0], totals[1], totals[2])
```

```python
import math

import jax
import jax.numpy as jnp
import ml_dtypes
import numpy as np
from jax import lax
from jax.experimental import pallas as pl
from jax.experimental.pallas import tpu as pltpu
from jax.sharding import PartitionSpec as P

C = 48
MX = 16
N1 = 128
N2 = 64
W = 4 * C
MODES = MX * MX
BF = jnp.bfloat16
F32 = jnp.float32


def trig(side):
    a = np.arange(MX)
    freq = np.where(a < MX // 2, a, side - MX + a)
    phase = (np.arange(side)[:, None] * freq[None, :]) % side
    angle = phase.astype(np.float32) * np.float32(2.0 * math.pi / side)
    cos = np.cos(angle).astype(ml_dtypes.bfloat16).astype(np.float32)
    sin = np.sin(angle).astype(ml_dtypes.bfloat16).astype(np.float32)
    return cos, sin


def low(table):
    return table.astype(ml_dtypes.bfloat16)


class Geometry:
    def __init__(self, side, n):
        self.side = side
        self.rows = side // n
        self.cells = self.rows * side
        self.group = min(8, self.rows)
        self.ngroups = self.rows // self.group
        self.npairs = self.rows // 2
        self.qlanes = max(128, self.npairs * 64)
        self.hk = self.ngroups * 128
        cos, sin = trig(side)
        eye = np.eye(MX, dtype=np.float32)

        first = np.zeros((self.group, side, 256), np.float32)
        for h in range(self.group):
            first[h, :, h * MX : (h + 1) * MX] = cos
            first[h, :, 128 + h * MX : 128 + (h + 1) * MX] = sin
        self.first = low(first.reshape(self.group * side, 256))

        second = np.zeros((n, MX, MX, 2, self.ngroups, 128), np.float32)
        inverse = np.zeros((n, MX, MX, 2, self.qlanes), np.float32)
        for r in range(n):
            for h in range(self.rows):
                c, s = cos[r * self.rows + h], sin[r * self.rows + h]
                ce, se = c[:, None, None] * eye, s[:, None, None] * eye
                g, lane = h // self.group, (h % self.group) * MX
                second[r, :, :, 0, g, lane : lane + MX] = ce
                second[r, :, :, 1, g, lane : lane + MX] = se
                lane = h * 2 * MX
                inverse[r, :, :, 0, lane : lane + MX] = ce
                inverse[r, :, :, 0, lane + MX : lane + 2 * MX] = -se
                inverse[r, :, :, 1, lane : lane + MX] = -se
                inverse[r, :, :, 1, lane + MX : lane + 2 * MX] = -ce
        self.second = low(second.reshape(n, MODES, 2 * self.hk))
        self.inverse = low(inverse.reshape(n, MODES, 2 * self.qlanes))

        spread = np.zeros((4, 2, MX, 4, side), np.float32)
        for h in range(4):
            spread[h, 0, :, h] = cos.T
            spread[h, 1, :, h] = sin.T
        self.spread = low(spread.reshape(128, 4 * side))
        if self.npairs == 1:
            self.spread = self.spread[:, : 2 * side]
        self.pair_spread = low(spread.reshape(128, 4 * side))[:64, : 2 * side]


def turn(v):
    return jnp.concatenate([v[3 * C :], v[2 * C : 3 * C], -v[C : 2 * C], -v[:C]], axis=0)


def dot(a, b, dims=((1,), (0,))):
    return lax.dot_general(a, b, (dims, ((), ())), preferred_element_type=F32)


def forward_pair(geo, get, first, second, scale, keep=None):
    width = geo.group * geo.side
    parts = []
    for g in range(geo.ngroups):
        y = dot(get(g * width, width), first)
        if keep is not None:
            keep(y[:W] + y[W:])
        parts.append(y)
    stacked = []
    for s in range(2):
        cols = []
        for y in parts:
            col = y[W * s : W * s + W, :128] + turn(y[W * s : W * s + W, 128:])
            cols.append((col * scale).astype(BF))
        col = jnp.concatenate(cols, axis=1) if len(cols) > 1 else cols[0]
        stacked.append(jnp.concatenate([col, turn(col)], axis=1))
    a, b = stacked
    both = jnp.concatenate([a[:128], b[:128], a[128:], b[128:]], axis=0)
    return dot(second, both, ((1,), (1,)))


def inverse_pair(geo, modes, inverse, scale):
    uv = dot(modes, inverse, ((0,), (0,)))
    result = []
    for s in range(2):
        part = jnp.concatenate(
            [uv[128 * s : 128 * s + 128], uv[256 + 64 * s : 320 + 64 * s]], axis=0
        )
        q = part[:, : geo.qlanes] + turn(part[:, geo.qlanes :])
        result.append((q * scale).astype(BF))
    return result


def build_kernel(weights):
    rows_list = []
    for source in range(4):
        blocks = []
        for target in range(4):
            blade_id = source ^ target
            block_part = weights[..., blade_id, :, :]
            if blade_id >> 1 & source & 1:
                block_part = -block_part
            blocks.append(block_part)
        rows_list.append(jnp.concatenate(blocks, axis=-1))
    return jnp.concatenate(rows_list, axis=-2)


def fold_kernel(kernel_grad):
    blades = []
    for blade_id in range(4):
        summed = None
        for source in range(4):
            target = source ^ blade_id
            block_part = kernel_grad[
                ..., source * C : (source + 1) * C, target * C : (target + 1) * C
            ]
            if blade_id >> 1 & source & 1:
                block_part = -block_part
            summed = block_part if summed is None else summed + block_part
        blades.append(summed)
    return jnp.stack(blades, axis=-3)


def expand_tables():
    dup = np.concatenate([np.arange(192), np.arange(128, 192)])
    place = np.zeros((4, C, 4, 256), np.float32)
    for p in range(4):
        for q in range(4):
            sign = -1.0 if (p >> 1) & q & 1 else 1.0
            full = np.zeros((C, 192), np.float32)
            o = p ^ q
            full[:, o * C : (o + 1) * C] = sign * np.eye(C)
            place[p, :, q] = full[:, dup]
    return low(place.reshape(4, C, 1024))


class Plan:
    def __init__(self, mesh, nbig, nsmall):
        self.n = mesh.shape["rows"]
        self.own = MODES // self.n
        self.per = max(1, 16 // self.own)
        self.big = Geometry(N1, self.n)
        self.small = Geometry(N2, self.n)
        self.nbig, self.nsmall = nbig, nsmall
        assert nbig % (2 * self.per) == 0 and nsmall % 2 == 0 and nsmall // 2 <= self.per
        self.steps = nbig // (2 * self.per)
        self.block = self.per * self.own
        self.total = (self.steps + 1) * self.block
        self.slots = -(-(self.total // self.own) // 8) * 8


def wide(i, last):
    return jnp.minimum(i, last)


def params(**kw):
    return pltpu.CompilerParams(vmem_limit_bytes=56 * 1024 * 1024, **kw)


def const_spec(shape):
    return pl.BlockSpec(shape, lambda i, r: (0,) * len(shape))


def device_spec(shape):
    return pl.BlockSpec((None,) + shape, lambda i, r: (r[0],) + (0,) * len(shape))


def field_specs(plan):
    big, small = plan.big, plan.small
    last = plan.steps - 1
    return (
        pl.BlockSpec((2 * plan.per, 4, C, big.cells), lambda i, r: (wide(i, last), 0, 0, 0)),
        pl.BlockSpec((plan.nsmall, 4, C, small.cells), lambda i, r: (0, 0, 0, 0)),
    )


def mode_spec(plan):
    return pl.BlockSpec((plan.n, plan.block, 2 * W), lambda i, r: (0, i, 0))


def store_modes(plan, ref, pair, z):
    z = z.reshape(plan.n, plan.own, 2 * W).astype(BF)
    ref[:, pair * plan.own : (pair + 1) * plan.own, :] = z


def load_modes(plan, ref, pair):
    return ref[:, pair * plan.own : (pair + 1) * plan.own, :].reshape(MODES, 2 * W)


def cost(flops, moved):
    return pl.CostEstimate(flops=flops, bytes_accessed=moved, transcendentals=0)


def spectra(plan, rank, x_big, x_small):
    def body(r, xb, xs, fb, sb, fs, ss, z):
        i = pl.program_id(0)

        def run(x, geo, first, second, count):
            for pair in range(count):
                def get(start, width):
                    part = x[2 * pair : 2 * pair + 2, :, :, start : start + width]
                    return part.reshape(2 * W, width)

                out = forward_pair(geo, get, first[...], second[...], 1.0 / geo.side)
                store_modes(plan, z, pair, out)

        @pl.when(i < plan.steps)
        def _():
            run(xb, plan.big, fb, sb, plan.per)

        @pl.when(i == plan.steps)
        def _():
            if plan.nsmall // 2 < plan.per:
                z[...] = jnp.zeros_like(z)
            run(xs, plan.small, fs, ss, plan.nsmall // 2)

    big, small = plan.big, plan.small
    return pl.pallas_call(
        body,
        grid_spec=pltpu.PrefetchScalarGridSpec(
            num_scalar_prefetch=1,
            grid=(plan.steps + 1,),
            in_specs=[
                *field_specs(plan),
                const_spec(big.first.shape),
                device_spec(big.second.shape[1:]),
                const_spec(small.first.shape),
                device_spec(small.second.shape[1:]),
            ],
            out_specs=mode_spec(plan),
        ),
        out_shape=jax.ShapeDtypeStruct((plan.n, plan.total, 2 * W), BF),
        compiler_params=params(),
        name="spectra",
    )(rank, x_big, x_small, big.first, big.second, small.first, small.second)


def cells_pass(plan, rank, x_big, x_small, g_big, g_small, modes, lin, lin_t, bias):
    k0 = math.sqrt(2.0 / math.pi)
    k1 = k0 * 0.044715

    def body(r, xb, xs, gb, gs, m, fb, sb, vb, eb, fs, ss, vs, es, kk, kt, bias_ref,
             ob, os_, pb, ps, z, lin_acc, y_acc, grad_b, grad_s):
        i = pl.program_id(0)

        @pl.when(i == 0)
        def _():
            lin_acc[...] = jnp.zeros_like(lin_acc)
            y_acc[...] = jnp.zeros_like(y_acc)

        def run(x, g, o, d, geo, first, second, inverse, spread, scratch, count):
            wide_cells = 2 * geo.side
            lane = lax.broadcasted_iota(jnp.int32, (W, 128), 1)
            for pair in range(count):
                qs = inverse_pair(geo, load_modes(plan, m, pair), inverse[...], 1.0 / MX)
                for s in range(2):
                    at = 2 * pair + s
                    for p in range(geo.npairs):
                        lo = p * wide_cells
                        q = qs[s][:, 128 * (p // 2) : 128 * (p // 2) + 128]
                        xv = x[at, :, :, lo : lo + wide_cells].reshape(W, wide_cells)
                        if p % 2 == 0:
                            tail = jnp.where(lane < 64, q, kt[:, 128:256])
                            rhs = [xv[:128], spread[...], xv[128:]]
                        else:
                            tail = jnp.where(lane >= 64, q, kt[:, 256:384])
                            rhs = [xv[:128], xv[128:], spread[...]]
                        lhs = jnp.concatenate([kt[:, :128], tail], axis=1)
                        a = dot(lhs, jnp.concatenate(rhs, axis=0)) + bias_ref[...]
                        a2 = a * a
                        t = jnp.tanh(a * (k0 + k1 * a2))
                        h = 0.5 + 0.5 * t
                        o[at, :, :, lo : lo + wide_cells] = (
                            (xv.astype(F32) + a * h).astype(BF).reshape(4, C, wide_cells)
                        )
                        slope = h + (a * (2.0 * k0 + 6.0 * k1 * a2)) * (h - h * h)
                        gv = g[at, :, :, lo : lo + wide_cells].reshape(W, wide_cells).astype(F32)
                        pre = (gv * slope).astype(BF)
                        scratch[s * W : s * W + W, lo : lo + wide_cells] = pre
                        d[at, :, :, lo : lo + wide_cells] = (
                            (gv + dot(kk[...], pre)).astype(BF).reshape(4, C, wide_cells)
                        )
                    xa = x[at, :, :, :].reshape(W, geo.cells)
                    lin_acc[...] += dot(xa, scratch[s * W : s * W + W, :], ((1,), (1,)))

                def keep(y):
                    y_acc[...] += y

                out = forward_pair(
                    geo, lambda start, width: scratch[:, start : start + width],
                    first[...], second[...], 1.0, keep,
                )
                store_modes(plan, z, pair, out)

        @pl.when(i < plan.steps)
        def _():
            run(xb, gb, ob, pb, plan.big, fb, sb, vb, eb, grad_b, plan.per)

        @pl.when(i == plan.steps)
        def _():
            if plan.nsmall // 2 < plan.per:
                z[...] = jnp.zeros_like(z)
            run(xs, gs, os_, ps, plan.small, fs, ss, vs, es, grad_s, plan.nsmall // 2)

    big, small = plan.big, plan.small
    tables = []
    specs = []
    for geo in (big, small):
        tables += [geo.first, geo.second, geo.inverse, geo.pair_spread]
        specs += [
            const_spec(geo.first.shape),
            device_spec(geo.second.shape[1:]),
            device_spec(geo.inverse.shape[1:]),
            const_spec(geo.pair_spread.shape),
        ]
    return pl.pallas_call(
        body,
        grid_spec=pltpu.PrefetchScalarGridSpec(
            num_scalar_prefetch=1,
            grid=(plan.steps + 1,),
            in_specs=[
                *field_specs(plan),
                *field_specs(plan),
                mode_spec(plan),
                *specs,
                const_spec(lin.shape),
                const_spec(lin_t.shape),
                const_spec(bias.shape),
            ],
            out_specs=[
                *field_specs(plan),
                *field_specs(plan),
                mode_spec(plan),
                const_spec((W, W)),
                const_spec((W, 256)),
            ],
            scratch_shapes=[
                pltpu.VMEM((2 * W, big.cells), BF),
                pltpu.VMEM((2 * W, small.cells), BF),
            ],
        ),
        out_shape=[
            jax.ShapeDtypeStruct(x_big.shape, BF),
            jax.ShapeDtypeStruct(x_small.shape, BF),
            jax.ShapeDtypeStruct(x_big.shape, BF),
            jax.ShapeDtypeStruct(x_small.shape, BF),
            jax.ShapeDtypeStruct((plan.n, plan.total, 2 * W), BF),
            jax.ShapeDtypeStruct((W, W), F32),
            jax.ShapeDtypeStruct((W, 256), F32),
        ],
        compiler_params=params(),
        name="cells",
    )(rank, x_big, x_small, g_big, g_small, modes, *tables, lin, lin_t, bias)


def input_grads(plan, rank, part_big, part_small, modes):
    def body(r, pb, ps, m, vb, eb, vs, es, db, ds):
        i = pl.program_id(0)

        def run(part, d, geo, inverse, spread, count):
            span = spread.shape[1]
            for pair in range(count):
                qs = inverse_pair(geo, load_modes(plan, m, pair), inverse[...], 1.0)
                q = jnp.concatenate(qs, axis=0) * jnp.asarray(1.0 / geo.side, BF)
                for j in range(geo.cells // span):
                    v = dot(q[:, 128 * j : 128 * j + 128], spread[...])
                    at = (slice(2 * pair, 2 * pair + 2), slice(None), slice(None),
                          slice(j * span, (j + 1) * span))
                    d[at] = part[at].astype(F32) + v.reshape(2, 4, C, span)

        @pl.when(i < plan.steps)
        def _():
            run(pb, db, plan.big, vb, eb, plan.per)

        @pl.when(i == plan.steps)
        def _():
            run(ps, ds, plan.small, vs, es, plan.nsmall // 2)

    tables = []
    specs = []
    for geo in (plan.big, plan.small):
        tables += [geo.inverse, geo.spread]
        specs += [device_spec(geo.inverse.shape[1:]), const_spec(geo.spread.shape)]
    return pl.pallas_call(
        body,
        grid_spec=pltpu.PrefetchScalarGridSpec(
            num_scalar_prefetch=1,
            grid=(plan.steps + 1,),
            in_specs=[*field_specs(plan), mode_spec(plan), *specs],
            out_specs=[*field_specs(plan)],
        ),
        out_shape=[
            jax.ShapeDtypeStruct(part_big.shape, F32),
            jax.ShapeDtypeStruct(part_small.shape, F32),
        ],
        compiler_params=params(),
        name="input_grads",
    )(rank, part_big, part_small, modes, *tables)


def lanes(acc, count):
    return jnp.concatenate([acc[t, :count, :] for t in range(3)], axis=1)


def mix_rows(plan, acc, kernel, scale, dims):
    lane = lax.broadcasted_iota(jnp.int32, (plan.slots, 128), 1)
    low_half = lane < 64

    def one(m):
        rows = pl.ds(m, plan.slots, stride=plan.own)
        first, second, third = (acc[t, rows, :] * scale for t in range(3))
        a = jnp.concatenate([first, jnp.where(low_half, third, 0.0)], axis=1)
        b = jnp.concatenate([second, jnp.where(low_half, 0.0, third)], axis=1)
        lhs = jnp.concatenate([a, b], axis=0).astype(BF)
        res = dot(lhs, kernel[m], dims)
        ra, rb = res[: plan.slots], res[plan.slots :]
        acc[0, rows, :] = ra[:, :128]
        acc[1, rows, :] = rb[:, :128]
        acc[2, rows, :] = jnp.where(low_half, ra[:, 128:], rb[:, 128:])

    unroll = 4

    @pl.loop(0, plan.own // unroll)
    def _(j):
        for u in range(unroll):
            one(j * unroll + u)


def exchange(plan, body, collective_id, name, operands, extra_out):
    n, own, total = plan.n, plan.own, plan.total
    half = n // 2
    block = (total, 2 * W)
    nin = len(operands)
    nout = 1 + len(extra_out)

    def kernel(*refs):
        part = refs[0]
        result = refs[nin]
        (acc, sib_in, sib_sum, peer_in, s_sib, r_sib, s_peer, r_peer,
         s_out, r_out, s_fwd, r_fwd) = refs[nin + nout :]
        me = lax.axis_index("rows")
        chip, core = me // 2, me % 2
        other = chip * 2 + (1 - core)

        def peer(d):
            return lax.rem(chip + d, half)

        def source(d):
            return lax.rem(chip + half - d, half)

        barrier = pltpu.get_barrier_semaphore()
        pl.semaphore_signal(barrier, inc=1, device_id={"rows": other})
        for d in range(1, half):
            pl.semaphore_signal(barrier, inc=1, device_id={"rows": peer(d) * 2 + core})
        pl.semaphore_wait(barrier, half)

        def to_sibling(d):
            return pltpu.make_async_remote_copy(
                src_ref=part.at[peer(d) * 2 + (1 - core)],
                dst_ref=sib_in.at[d],
                send_sem=s_sib.at[d],
                recv_sem=r_sib.at[d],
                device_id={"rows": other},
            )

        def to_peer(d):
            return pltpu.make_async_remote_copy(
                src_ref=sib_sum.at[d],
                dst_ref=peer_in.at[d],
                send_sem=s_peer.at[d],
                recv_sem=r_peer.at[d],
                device_id={"rows": peer(d) * 2 + core},
            )

        order = list(range(1, half)) + [0]
        for d in order:
            to_sibling(d).start()
        for d in range(1, half):
            to_sibling(d).wait_recv()
            mine = part[peer(d) * 2 + core].astype(F32)
            sib_sum[d] = (mine + sib_in[d].astype(F32)).astype(BF)
            to_peer(d).start()
        finish = body(plan, refs[1:nin], refs[nin + 1 : nin + nout], acc)
        to_sibling(0).wait_recv()
        summed = part[me].astype(F32) + sib_in[0].astype(F32)
        for d in range(1, half):
            to_peer(d).wait_recv()
            summed = summed + peer_in[d].astype(F32)
        for t in range(3):
            acc[t, :total, :] = summed[:, 128 * t : 128 * t + 128]
        if plan.slots * own > total:
            acc[:, total:, :] = jnp.zeros((3, plan.slots * own - total, 128), F32)
        finish()
        result[me] = lanes(acc, total).astype(BF)

        def out_to(d):
            return pltpu.make_async_remote_copy(
                src_ref=result.at[me],
                dst_ref=result.at[me],
                send_sem=s_out.at[d],
                recv_sem=r_out.at[d],
                device_id={"rows": other if d == 0 else peer(d) * 2 + core},
            )

        def forward(d):
            at = source(d) * 2 + core
            return pltpu.make_async_remote_copy(
                src_ref=result.at[at],
                dst_ref=result.at[at],
                send_sem=s_fwd.at[d],
                recv_sem=r_fwd.at[d],
                device_id={"rows": other},
            )

        for d in order:
            out_to(d).start()
        for d in range(1, half):
            out_to(d).wait_recv()
            forward(d).start()
        out_to(0).wait_recv()
        for d in range(1, half):
            forward(d).wait_recv()
            forward(d).wait_send()
            out_to(d).wait_send()
            to_peer(d).wait_send()
        out_to(0).wait_send()
        for d in range(half):
            to_sibling(d).wait_send()

    vmem = pl.BlockSpec(memory_space=pltpu.VMEM)
    dma = pltpu.SemaphoreType.DMA((half,))
    return pl.pallas_call(
        kernel,
        in_specs=[vmem] * nin,
        out_specs=[vmem] * nout,
        out_shape=[jax.ShapeDtypeStruct((n,) + block, BF), *extra_out],
        scratch_shapes=[
            pltpu.VMEM((3, plan.slots * own, 128), F32),
            pltpu.VMEM((half,) + block, BF),
            pltpu.VMEM((half,) + block, BF),
            pltpu.VMEM((half,) + block, BF),
            *[dma] * 8,
        ],
        compiler_params=params(collective_id=collective_id, has_side_effects=True),
        name=name,
    )(*operands)


def forward_modes(plan, operands, outs, acc):
    place, weights = operands
    kernel, spectrum = outs
    flat = [weights[:, p].reshape(plan.own * C, C) for p in range(4)]
    for q in range(4):
        rows = None
        for p in range(4):
            term = dot(flat[p], place[p, :, 256 * q : 256 * q + 256])
            rows = term if rows is None else rows + term
        kernel[:, C * q : C * q + C, :] = rows.astype(BF).reshape(plan.own, C, 256)
    kernel[:, W:, :] = kernel[:, 128:W, :]

    def finish():
        spectrum[...] = lanes(acc, plan.total).astype(BF)
        mix_rows(plan, acc, kernel, 1.0, ((1,), (0,)))

    return finish


def backward_modes(plan, operands, outs, acc):
    (kernel,) = operands
    (grad,) = outs

    def finish():
        grad[...] = (lanes(acc, plan.total) * (1.0 / MX)).astype(BF)
        mix_rows(plan, acc, kernel, 1.0 / MX, ((1,), (1,)))

    return finish


def on_device(plan, x_big, x_small, spec_weight, lin_weight, lin_bias, grad_big, grad_small):
    rank = lax.axis_index("rows").reshape(1)
    lin = build_kernel(lin_weight)
    lin_t = lin.T
    zero = jnp.zeros((W, 64), BF)
    lin_t = jnp.concatenate([lin_t[:, :128], zero, lin_t[:, 128:], lin_t[:, 128:], zero], axis=1)
    bias = lin_bias.astype(F32).reshape(W, 1)

    block = (plan.total, 2 * W)
    part = spectra(plan, rank, x_big, x_small)
    modes, kernel, spectrum = exchange(
        plan, forward_modes, 1, "mix_modes",
        (part, jnp.asarray(expand_tables()), spec_weight),
        (
            jax.ShapeDtypeStruct((plan.own, 256, 256), BF),
            jax.ShapeDtypeStruct(block, BF),
        ),
    )
    out_big, out_small, part_big, part_small, part, lin_grad, columns = cells_pass(
        plan, rank, x_big, x_small, grad_big, grad_small, modes, lin, lin_t, bias
    )
    bias_grad = columns[:, :128:MX].sum(axis=1)
    lin_grads = lax.psum((fold_kernel(lin_grad), bias_grad.reshape(4, C)), ("samples", "rows"))
    modes, mode_grad = exchange(
        plan, backward_modes, 2, "mix_grads", (part, kernel),
        (jax.ShapeDtypeStruct(block, BF),),
    )

    def samples(v):
        v = v.reshape(plan.total // plan.own, plan.own, 2 * W)
        a = jnp.concatenate([v[..., :128], v[..., 256:320]], axis=-1)
        b = jnp.concatenate([v[..., 128:256], v[..., 320:]], axis=-1)
        return jnp.concatenate([a, b], axis=0)

    kernel_grad = jnp.einsum(
        "smi,smo->mio", samples(spectrum), samples(mode_grad), preferred_element_type=F32
    )
    spec_grad = lax.psum(fold_kernel(kernel_grad).astype(BF), "samples").astype(F32)
    dx_big, dx_small = input_grads(plan, rank, part_big, part_small, modes)
    return out_big, out_small, dx_big, dx_small, spec_grad, lin_grads[0], lin_grads[1]


def solution(mesh):
    fields = P("samples", None, None, "rows")
    spec = P("rows", None, None, None)

    def run(x_big, x_small, *rest):
        count = mesh.shape["samples"]
        plan = Plan(mesh, x_big.shape[0] // count, x_small.shape[0] // count)

        def local(*args):
            return on_device(plan, *args)

        return jax.shard_map(
            local,
            mesh=mesh,
            in_specs=(fields, fields, spec, P(), P(), fields, fields),
            out_specs=(fields, fields, fields, fields, spec, P(), P()),
            check_vma=False,
        )(x_big, x_small, *rest)

    return run
```

```python
import math

import jax
import jax.numpy as jnp
import ml_dtypes
import numpy as np
from jax import lax
from jax.experimental import pallas as pl
from jax.experimental.pallas import tpu as pltpu
from jax.sharding import PartitionSpec as P

C = 48
MX = 16
N1 = 128
N2 = 64
W = 4 * C
MODES = MX * MX
BF = jnp.bfloat16
F32 = jnp.float32


def trig(side):
    a = np.arange(MX)
    freq = np.where(a < MX // 2, a, side - MX + a)
    phase = (np.arange(side)[:, None] * freq[None, :]) % side
    angle = phase.astype(np.float32) * np.float32(2.0 * math.pi / side)
    cos = np.cos(angle).astype(ml_dtypes.bfloat16).astype(np.float32)
    sin = np.sin(angle).astype(ml_dtypes.bfloat16).astype(np.float32)
    return cos, sin


def low(table):
    return table.astype(ml_dtypes.bfloat16)


class Geometry:
    def __init__(self, side, n):
        self.side = side
        self.rows = side // n
        self.cells = self.rows * side
        self.group = min(8, self.rows)
        self.ngroups = self.rows // self.group
        self.npairs = self.rows // 2
        self.qlanes = max(128, self.npairs * 64)
        self.hk = self.ngroups * 128
        cos, sin = trig(side)
        eye = np.eye(MX, dtype=np.float32)

        first = np.zeros((self.group, side, 256), np.float32)
        for h in range(self.group):
            first[h, :, h * MX : (h + 1) * MX] = cos
            first[h, :, 128 + h * MX : 128 + (h + 1) * MX] = sin
        self.first = low(first.reshape(self.group * side, 256))

        second = np.zeros((n, MX, MX, 2, self.ngroups, 128), np.float32)
        inverse = np.zeros((n, MX, MX, 2, self.qlanes), np.float32)
        for r in range(n):
            for h in range(self.rows):
                c, s = cos[r * self.rows + h], sin[r * self.rows + h]
                ce, se = c[:, None, None] * eye, s[:, None, None] * eye
                g, lane = h // self.group, (h % self.group) * MX
                second[r, :, :, 0, g, lane : lane + MX] = ce
                second[r, :, :, 1, g, lane : lane + MX] = se
                lane = h * 2 * MX
                inverse[r, :, :, 0, lane : lane + MX] = ce
                inverse[r, :, :, 0, lane + MX : lane + 2 * MX] = -se
                inverse[r, :, :, 1, lane : lane + MX] = -se
                inverse[r, :, :, 1, lane + MX : lane + 2 * MX] = -ce
        self.second = low(second.reshape(n, MODES, 2 * self.hk))
        inverse[..., MX : self.rows * 2 * MX : 2 * MX] = 0.0
        self.inverse = low(inverse.reshape(n, MODES, 2 * self.qlanes))

        spread = np.zeros((4, 2, MX, 4, side), np.float32)
        for h in range(4):
            spread[h, 0, :, h] = cos.T
            spread[h, 1, :, h] = sin.T
        self.spread = low(spread.reshape(128, 4 * side))
        if self.npairs == 1:
            self.spread = self.spread[:, : 2 * side]
        for h in range(4):
            spread[h, 1, 0, h] = 1.0
        self.pair_spread = low(spread.reshape(128, 4 * side))[:64, : 2 * side]


def turn(v):
    return jnp.concatenate([v[3 * C :], v[2 * C : 3 * C], -v[C : 2 * C], -v[:C]], axis=0)


def dot(a, b, dims=((1,), (0,))):
    return lax.dot_general(a, b, (dims, ((), ())), preferred_element_type=F32)


def forward_pair(geo, get, first, second, scale, keep=None):
    width = geo.group * geo.side
    parts = []
    for g in range(geo.ngroups):
        y = dot(get(g * width, width), first)
        if keep is not None:
            keep(y[:W] + y[W:])
        parts.append(y)
    stacked = []
    for s in range(2):
        cols = []
        for y in parts:
            col = y[W * s : W * s + W, :128] + turn(y[W * s : W * s + W, 128:])
            cols.append((col * scale).astype(BF))
        col = jnp.concatenate(cols, axis=1) if len(cols) > 1 else cols[0]
        stacked.append(jnp.concatenate([col, turn(col)], axis=1))
    a, b = stacked
    both = jnp.concatenate([a[:128], b[:128], a[128:], b[128:]], axis=0)
    return dot(second, both, ((1,), (1,)))


def inverse_pair(geo, modes, inverse, scale):
    uv = dot(modes, inverse, ((0,), (0,)))
    result = []
    for s in range(2):
        part = jnp.concatenate(
            [uv[128 * s : 128 * s + 128], uv[256 + 64 * s : 320 + 64 * s]], axis=0
        )
        q = part[:, : geo.qlanes] + turn(part[:, geo.qlanes :])
        result.append((q * scale).astype(BF))
    return result


def build_kernel(weights):
    rows_list = []
    for source in range(4):
        blocks = []
        for target in range(4):
            blade_id = source ^ target
            block_part = weights[..., blade_id, :, :]
            if blade_id >> 1 & source & 1:
                block_part = -block_part
            blocks.append(block_part)
        rows_list.append(jnp.concatenate(blocks, axis=-1))
    return jnp.concatenate(rows_list, axis=-2)


def fold_kernel(kernel_grad):
    blades = []
    for blade_id in range(4):
        summed = None
        for source in range(4):
            target = source ^ blade_id
            block_part = kernel_grad[
                ..., source * C : (source + 1) * C, target * C : (target + 1) * C
            ]
            if blade_id >> 1 & source & 1:
                block_part = -block_part
            summed = block_part if summed is None else summed + block_part
        blades.append(summed)
    return jnp.stack(blades, axis=-3)


def fold_tables():
    dup = np.concatenate([np.arange(192), np.arange(128, 192)])
    pick = np.zeros((192, 4, 128), np.float32)
    move = np.zeros((192, 4, 192), np.float32)
    for q in range(4):
        pick[q * C : q * C + C, q, :C] = np.eye(C)
        for p in range(4):
            sign = -1.0 if (p >> 1) & q & 1 else 1.0
            o = p ^ q
            move[o * C : o * C + C, q, p * C : p * C + C] = sign * np.eye(C)
    return (
        low(pick[dup].reshape(256, 512)),
        low(move[dup][:, :, dup].reshape(256, 1024)),
        move.transpose(1, 0, 2).copy(),
    )


def expand_tables():
    dup = np.concatenate([np.arange(192), np.arange(128, 192)])
    place = np.zeros((4, C, 4, 256), np.float32)
    for p in range(4):
        for q in range(4):
            sign = -1.0 if (p >> 1) & q & 1 else 1.0
            full = np.zeros((C, 192), np.float32)
            o = p ^ q
            full[:, o * C : (o + 1) * C] = sign * np.eye(C)
            place[p, :, q] = full[:, dup]
    return low(place.reshape(4, C, 1024))


class Plan:
    def __init__(self, mesh, nbig, nsmall):
        self.n = mesh.shape["rows"]
        self.nz = mesh.shape["samples"]
        self.own = MODES // self.n
        self.per = max(1, 16 // self.own)
        self.big = Geometry(N1, self.n)
        self.small = Geometry(N2, self.n)
        self.nbig, self.nsmall = nbig, nsmall
        assert nbig % (2 * self.per) == 0 and nsmall % 2 == 0 and nsmall // 2 <= self.per
        self.steps = nbig // (2 * self.per)
        self.count = self.steps + 1
        self.block = self.per * self.own
        self.total = self.count * self.block
        self.chunks = next(c for c in (3, 2, 1) if self.count % c == 0)
        self.span = self.count // self.chunks
        self.crow = self.span * self.block
        self.half = self.crow // 2
        self.slots = -(-(self.span * self.per) // 8) * 8
        self.acc_rows = self.slots * self.own
        self.chips = self.n // 2
        bits = list(range(1, self.n.bit_length() - 1))
        self.orders = (bits, bits[::-1])
        self.levels = len(bits)
        self.wrows = self.own // 2 * C
        self.zrows = -(-self.wrows // (16 * self.nz)) * 16

    def mask(self, h, idx):
        m = 0
        for t, b in enumerate(self.orders[h]):
            if idx >> (self.levels - 1 - t) & 1:
                m |= 1 << b
        return m


def wide(i, last):
    return jnp.minimum(i, last)


def params(**kw):
    return pltpu.CompilerParams(vmem_limit_bytes=56 * 1024 * 1024, **kw)


def const_spec(shape):
    return pl.BlockSpec(shape, lambda i, r: (0,) * len(shape))


def device_spec(shape):
    return pl.BlockSpec((None,) + shape, lambda i, r: (r[0],) + (0,) * len(shape))


def field_specs(plan):
    big, small = plan.big, plan.small
    last = plan.steps - 1
    return (
        pl.BlockSpec((2 * plan.per, 4, C, big.cells), lambda i, r: (wide(i, last), 0, 0, 0)),
        pl.BlockSpec((plan.nsmall, 4, C, small.cells), lambda i, r: (0, 0, 0, 0)),
    )


def mode_spec(plan):
    return pl.BlockSpec((plan.n, plan.block, 2 * W), lambda i, r: (0, i, 0))


def store_modes(plan, ref, pair, z):
    z = z.reshape(plan.n, plan.own, 2 * W).astype(BF)
    ref[:, pair * plan.own : (pair + 1) * plan.own, :] = z


def load_modes(plan, ref, pair):
    return ref[:, pair * plan.own : (pair + 1) * plan.own, :].reshape(MODES, 2 * W)


def cost(flops, moved):
    return pl.CostEstimate(flops=flops, bytes_accessed=moved, transcendentals=0)


def flip(index, mask):
    result = index
    for b in range(mask.bit_length()):
        if mask >> b & 1:
            bit = lax.rem(lax.div(index, 1 << b), 2)
            result = result + (1 - 2 * bit) * (1 << b)
    return result


def tiles(v):
    return [v[:, 128 * t : 128 * t + 128] for t in range(v.shape[1] // 128)]


def sample_rows(first, second, third):
    lane = lax.broadcasted_iota(jnp.int32, third.shape, 1)
    a = jnp.concatenate([first, jnp.where(lane < 64, third, 0.0)], axis=1)
    b = jnp.concatenate([second, jnp.where(lane < 64, 0.0, third)], axis=1)
    return jnp.concatenate([a, b], axis=0)


def pair_tiles(a, b):
    lane = lax.broadcasted_iota(jnp.int32, (a.shape[0], 128), 1)
    return a[:, :128], b[:, :128], jnp.where(lane < 64, a[:, 128:], b[:, 128:])


def remote(src, dst, send, recv, device):
    return pltpu.make_async_remote_copy(
        src_ref=src, dst_ref=dst, send_sem=send, recv_sem=recv, device_id=device
    )


class Exchange:
    SCRATCH = 16

    @staticmethod
    def scratch(plan):
        n, chips, width = plan.n, plan.chips, 2 * W
        dma = pltpu.SemaphoreType.DMA
        part = (plan.chunks, 2)
        return [
            pltpu.VMEM((chips, plan.total, width), BF),
            pltpu.VMEM((2, chips, plan.chunks * plan.half, width), BF),
            pltpu.VMEM((2, chips, plan.chunks * plan.half, width), BF),
            pltpu.VMEM((chips, 2, plan.total, width), BF),
            pltpu.VMEM((3, plan.acc_rows, 128), F32),
            pltpu.VMEM((3, plan.acc_rows, 128), F32),
            dma((plan.chunks,)),
            dma((plan.chunks,)),
            dma(part + (plan.levels,)),
            dma(part + (plan.levels,)),
            dma(part + (chips,)),
            dma(part + (chips,)),
            dma(part + (chips,)),
            dma(part + (chips,)),
            dma((plan.chunks,)),
            pltpu.VMEM((plan.own, 256, 256), BF),
        ]

    def __init__(self, plan, part, out, refs):
        self.plan, self.part, self.out = plan, part, out
        (self.sib, self.sums, self.lev, self.res, self.acc, self.mixed,
         self.sib_s, self.sib_r, self.lev_s, self.lev_r, self.ag_s, self.ag_r,
         self.fw_s, self.fw_r, self.out_s, self.kernel) = refs
        self.me = lax.axis_index("rows")
        self.core = lax.rem(self.me, 2)

    def partners(self):
        return [flip(self.me, 1 << b) for b in range(self.plan.n.bit_length() - 1)]

    def to_sibling(self, c):
        rows = pl.ds(c * self.plan.crow, self.plan.crow)
        return remote(
            self.part.at[:, 1 - self.core, rows, :], self.sib.at[:, rows, :],
            self.sib_s.at[c], self.sib_r.at[c], {"rows": flip(self.me, 1)},
        )

    def level(self, c, h, t):
        plan = self.plan
        count = plan.chips >> (t + 1)
        rows = pl.ds(c * plan.half, plan.half)
        at = plan.chips - 2 * count
        return remote(
            self.sums.at[h, pl.ds(count, count), rows, :],
            self.lev.at[h, pl.ds(at, count), rows, :],
            self.lev_s.at[c, h, t], self.lev_r.at[c, h, t],
            {"rows": flip(self.me, 1 << plan.orders[h][t])},
        )

    def rows(self, c, h):
        return pl.ds(c * self.plan.crow + h * self.plan.half, self.plan.half)

    def block(self, c, h, owner):
        return self.res.at[lax.div(owner, 2), lax.rem(owner, 2), self.rows(c, h), :]

    def gather(self, c, h, u, idx):
        plan = self.plan
        sem = (1 << u) - 1 + idx
        ref = self.block(c, h, flip(self.me, plan.mask(h, idx)))
        return remote(
            ref, ref, self.ag_s.at[c, h, sem], self.ag_r.at[c, h, sem],
            {"rows": flip(self.me, 1 << plan.orders[h][plan.levels - 1 - u])},
        )

    def forward(self, c, h, idx):
        ref = self.block(c, h, flip(self.me, self.plan.mask(h, idx)))
        return remote(
            ref, ref, self.fw_s.at[c, h, idx], self.fw_r.at[c, h, idx],
            {"rows": flip(self.me, 1)},
        )

    def store(self, c):
        rows = pl.ds(c * self.plan.crow, self.plan.crow)
        return pltpu.make_async_copy(
            self.res.at[:, :, rows, :], self.out.at[:, :, rows, :], self.out_s.at[c]
        )

    def begin(self, c):
        self.to_sibling(c).start()

    def add_sibling(self, c):
        plan = self.plan
        self.to_sibling(c).wait_recv()
        for far in (1, 0):
            for h in range(2):
                span = plan.chips // 2
                for idx in range(far * span, far * span + span):
                    owner = flip(self.me, plan.mask(h, idx))
                    chip = lax.div(owner, 2)
                    rows = self.rows(c, h)
                    v = self.part[chip, self.core, rows, :].astype(F32)
                    v = v + self.sib[chip, rows, :].astype(F32)
                    self.sums[h, idx, pl.ds(c * plan.half, plan.half), :] = v.astype(BF)
                if far:
                    self.level(c, h, 0).start()

    def next_level(self, c, t):
        plan = self.plan
        rows = pl.ds(c * plan.half, plan.half)
        count = plan.chips >> t
        at = plan.chips - 2 * count
        for h in range(2):
            self.level(c, h, t - 1).wait_recv()
            for idx in reversed(range(count)):
                v = self.sums[h, idx, rows, :].astype(F32)
                v = v + self.lev[h, at + idx, rows, :].astype(F32)
                self.sums[h, idx, rows, :] = v.astype(BF)
                if idx == count // 2:
                    self.level(c, h, t).start()

    def finish_sum(self, c, scale):
        plan = self.plan
        rows = pl.ds(c * plan.half, plan.half)
        for h in range(2):
            self.level(c, h, plan.levels - 1).wait_recv()
            v = self.sums[h, 0, rows, :].astype(F32)
            v = (v + self.lev[h, plan.chips - 2, rows, :].astype(F32)) * scale
            for t, tile in enumerate(tiles(v)):
                self.acc[t, h * plan.half : (h + 1) * plan.half, :] = tile

    def mix(self, c, dims):
        plan = self.plan

        def one(m):
            rows = pl.ds(m, plan.slots, stride=plan.own)
            lhs = sample_rows(*(self.acc[t, rows, :] for t in range(3))).astype(BF)
            res = dot(lhs, self.kernel[m], dims)
            for t, tile in enumerate(pair_tiles(res[: plan.slots], res[plan.slots :])):
                self.mixed[t, rows, :] = tile

        unroll = 8

        @pl.loop(0, plan.own // unroll)
        def _(j):
            for u in range(unroll):
                one(j * unroll + u)

        result = jnp.concatenate([self.mixed[t, : plan.crow, :] for t in range(3)], axis=1)
        self.res[lax.div(self.me, 2), self.core, pl.ds(c * plan.crow, plan.crow), :] = (
            result.astype(BF)
        )
        for h in range(2):
            self.gather(c, h, 0, 0).start()
            self.forward(c, h, 0).start()

    def spread(self, c, u):
        for h in range(2):
            got = 1 << (u - 1)
            for idx in range(got):
                self.gather(c, h, u - 1, idx).wait_recv()
            if u < self.plan.levels:
                for idx in reversed(range(2 * got)):
                    self.gather(c, h, u, idx).start()
            for idx in range(got, 2 * got):
                self.forward(c, h, idx).start()

    def close(self, c):
        for h in range(2):
            for idx in range(self.plan.chips):
                self.forward(c, h, idx).wait_recv()
        self.store(c).start()

    def drain(self):
        plan = self.plan
        for c in range(plan.chunks):
            self.to_sibling(c).wait_send()
            for h in range(2):
                for t in range(plan.levels):
                    self.level(c, h, t).wait_send()
                for u in range(plan.levels):
                    for idx in range(1 << u):
                        self.gather(c, h, u, idx).wait_send()
                for idx in range(plan.chips):
                    self.forward(c, h, idx).wait_send()
            self.store(c).wait()

    def clear(self):
        plan = self.plan
        if plan.acc_rows > plan.crow:
            rest = plan.acc_rows - plan.crow
            self.acc[:, plan.crow :, :] = jnp.zeros((3, rest, 128), F32)

    def tasks(self, c, total):
        plan = self.plan
        todo = [lambda: self.begin(c), lambda: self.add_sibling(c)]
        todo += [lambda t=t: self.next_level(c, t) for t in range(1, plan.levels)]
        todo += [lambda: total(c)]
        todo += [lambda u=u: self.spread(c, u) for u in range(1, plan.levels + 1)]
        todo += [lambda: self.close(c)]
        return todo


def greet(devices):
    barrier = pltpu.get_barrier_semaphore()
    for device in devices:
        pl.semaphore_signal(barrier, inc=1, device_id=device)
    pl.semaphore_wait(barrier, len(devices))


def build_modes(plan, place, weights, kernel):
    flat = [weights[:, p].reshape(plan.own * C, C) for p in range(4)]
    for q in range(4):
        rows = None
        for p in range(4):
            term = dot(flat[p], place[p, :, 256 * q : 256 * q + 256])
            rows = term if rows is None else rows + term
        kernel[:, C * q : C * q + C, :] = rows.astype(BF).reshape(plan.own, C, 256)
    kernel[:, W:, :] = kernel[:, 128:W, :]


def plain_fields(plan):
    big, small = plan.big, plan.small
    last = plan.steps - 1
    return [
        pl.BlockSpec((2 * plan.per, 4, C, big.cells), lambda i: (wide(i, last), 0, 0, 0)),
        pl.BlockSpec((plan.nsmall, 4, C, small.cells), lambda i: (0, 0, 0, 0)),
    ]


def fixed(shape):
    return pl.BlockSpec(shape, lambda i: (0,) * len(shape))


ANYWHERE = pl.BlockSpec(memory_space=pl.ANY)


def forward_kernel(plan, x_big, x_small, spec_weight):
    big, small = plan.big, plan.small

    def kernel(xb, xs, fb, fs, place, weights, sb_all, ss_all, out, kernel_out, spectrum,
               part, sb, ss, table_sem, *refs):
        i = pl.program_id(0)
        ex = Exchange(plan, part, out, refs)
        loads = [
            pltpu.make_async_copy(sb_all.at[ex.me], sb, table_sem.at[0]),
            pltpu.make_async_copy(ss_all.at[ex.me], ss, table_sem.at[1]),
        ]
        keep = pltpu.make_async_copy(ex.kernel, kernel_out, table_sem.at[2])

        @pl.when(i == 0)
        def _():
            for load in loads:
                load.start()
            greet([{"rows": d} for d in ex.partners()])
            ex.clear()
            for load in loads:
                load.wait()

        def run(x, geo, first, second, count):
            parts = []
            for pair in range(count):
                def get(start, width):
                    v = x[2 * pair : 2 * pair + 2, :, :, start : start + width]
                    return v.reshape(2 * W, width)

                z = forward_pair(geo, get, first[...], second[...], 1.0 / geo.side)
                parts.append(z.reshape(plan.chips, 2, plan.own, 2 * W))
            parts += [jnp.zeros_like(parts[0])] * (plan.per - count)
            z = jnp.concatenate(parts, axis=2) if plan.per > 1 else parts[0]
            rows = pl.ds(pl.multiple_of(i * plan.block, 16), plan.block)
            part[:, :, rows, :] = z.astype(BF)

        @pl.when(i < plan.steps)
        def _():
            run(xb, big, fb, sb, plan.per)

        @pl.when(i == plan.steps)
        def _():
            run(xs, small, fs, ss, plan.nsmall // 2)

        def total(c):
            ex.finish_sum(c, 1.0)
            spectrum[pl.ds(c * plan.crow, plan.crow), :] = jnp.concatenate(
                [ex.acc[t, : plan.crow, :] for t in range(3)], axis=1
            ).astype(BF)
            ex.mix(c, ((1,), (0,)))

        def prepare():
            build_modes(plan, place, weights, ex.kernel)
            keep.start()

        starts = [(c + 1) * plan.span - 1 for c in range(plan.chunks)]
        schedule(plan, ex, i, total, starts, 2, [(starts[0], prepare)])

        @pl.when(i == plan.steps)
        def _():
            ex.drain()
            keep.wait()

    return pl.pallas_call(
        kernel,
        grid=(plan.count,),
        in_specs=[
            *plain_fields(plan),
            fixed(big.first.shape),
            fixed(small.first.shape),
            fixed((4, C, 1024)),
            fixed(spec_weight.shape),
            ANYWHERE,
            ANYWHERE,
        ],
        out_specs=[ANYWHERE, ANYWHERE, fixed((plan.total, 2 * W))],
        out_shape=[
            jax.ShapeDtypeStruct((plan.chips, 2, plan.total, 2 * W), BF),
            jax.ShapeDtypeStruct((plan.own, 256, 256), BF),
            jax.ShapeDtypeStruct((plan.total, 2 * W), BF),
        ],
        scratch_shapes=[
            pltpu.VMEM((plan.chips, 2, plan.total, 2 * W), BF),
            pltpu.VMEM(big.second.shape[1:], BF),
            pltpu.VMEM(small.second.shape[1:], BF),
            pltpu.SemaphoreType.DMA((3,)),
            *Exchange.scratch(plan),
        ],
        compiler_params=params(collective_id=1, has_side_effects=True),
        name="mode_forward",
    )(x_big, x_small, big.first, small.first, expand_tables(), spec_weight,
      big.second, small.second)


def schedule(plan, ex, i, total, starts, gap, hooks):
    last = plan.count - 1
    at = {}
    for c in range(plan.chunks):
        for k, task in enumerate(ex.tasks(c, total)):
            when = starts[c] + gap * k
            at.setdefault(min(when, last), []).append((when, c, task))
    for when, task in hooks:
        at.setdefault(min(when, last), []).append((when, -1, task))
    for step in sorted(at):
        @pl.when(i == step)
        def _(step=step):
            for _, _, task in sorted(at[step], key=lambda v: v[:2]):
                task()


def cells_pass(plan, rank, x_big, x_small, g_big, g_small, modes, lin_t, bias):
    k0 = math.sqrt(2.0 / math.pi)
    k1 = k0 * 0.044715

    def body(r, xb, xs, gb, gs, m, fb, sb, vb, eb, fs, ss, vs, es, kt, bias_ref,
             ob, os_, pb, ps, z, lin_acc, y_acc):
        i = pl.program_id(0)

        @pl.when(i == 0)
        def _():
            lin_acc[...] = jnp.zeros_like(lin_acc)
            y_acc[...] = jnp.zeros_like(y_acc)

        def run(x, g, o, d, geo, first, second, inverse, spread, count):
            wide_cells = 2 * geo.side
            lane = lax.broadcasted_iota(jnp.int32, (W, 128), 1)

            def main(at, q_all, p):
                lo = p * wide_cells
                cells = slice(lo, lo + wide_cells)
                q = q_all[:, 128 * (p // 2) : 128 * (p // 2) + 128]
                xv = x[at, :, :, cells].reshape(W, wide_cells)
                if p % 2 == 0:
                    tail = jnp.where(lane < 64, q, kt[:, 128:256])
                    rhs = [xv[:128], spread[...], xv[128:]]
                else:
                    tail = jnp.where(lane >= 64, q, kt[:, 256:384])
                    rhs = [xv[:128], xv[128:], spread[...]]
                lhs = jnp.concatenate([kt[:, :128], tail], axis=1)
                b = dot(lhs, jnp.concatenate(rhs, axis=0))
                s = b * b
                t = jnp.tanh(b * (2.0 * k0 + 8.0 * k1 * s))
                e = 1.0 + t
                o[at, :, :, cells] = (xv + (b * e).astype(BF)).reshape(4, C, wide_cells)
                slope = e * (0.5 + b * (k0 + 12.0 * k1 * s) * (1.0 - t))
                gv = g[at, :, :, cells].reshape(W, wide_cells)
                d[at, :, :, cells] = (gv * slope.astype(BF)).reshape(4, C, wide_cells)

            def weight_grad(at):
                xa = x[at, :, :, :].reshape(W, geo.cells)
                pa = d[at, :, :, :].reshape(W, geo.cells)
                lin_acc[...] += dot(xa, pa, ((1,), (1,)))

            def keep(y):
                y_acc[...] += y

            for pair in range(count):
                qs = inverse_pair(geo, load_modes(plan, m, pair), inverse[...], 0.5 / MX)
                for s in range(2):
                    q_all = qs[s] + jnp.concatenate([bias_ref[...]] * (geo.qlanes // 128), axis=1)
                    for p in range(geo.npairs):
                        main(2 * pair + s, q_all, p)
                    weight_grad(2 * pair + s)

                def get(start, width):
                    v = d[2 * pair : 2 * pair + 2, :, :, start : start + width]
                    return v.reshape(2 * W, width)

                out = forward_pair(geo, get, first[...], second[...], 1.0, keep)
                store_modes(plan, z, pair, out)

        @pl.when(i < plan.steps)
        def _():
            run(xb, gb, ob, pb, plan.big, fb, sb, vb, eb, plan.per)

        @pl.when(i == plan.steps)
        def _():
            if plan.nsmall // 2 < plan.per:
                z[...] = jnp.zeros_like(z)
            run(xs, gs, os_, ps, plan.small, fs, ss, vs, es, plan.nsmall // 2)

    big, small = plan.big, plan.small
    tables = []
    specs = []
    for geo in (big, small):
        tables += [geo.first, geo.second, geo.inverse, geo.pair_spread]
        specs += [
            const_spec(geo.first.shape),
            device_spec(geo.second.shape[1:]),
            device_spec(geo.inverse.shape[1:]),
            const_spec(geo.pair_spread.shape),
        ]
    return pl.pallas_call(
        body,
        grid_spec=pltpu.PrefetchScalarGridSpec(
            num_scalar_prefetch=1,
            grid=(plan.count,),
            in_specs=[
                *field_specs(plan),
                *field_specs(plan),
                mode_spec(plan),
                *specs,
                const_spec(lin_t.shape),
                const_spec(bias.shape),
            ],
            out_specs=[
                *field_specs(plan),
                *field_specs(plan),
                mode_spec(plan),
                const_spec((W, W)),
                const_spec((W, 256)),
            ],
        ),
        out_shape=[
            jax.ShapeDtypeStruct(x_big.shape, BF),
            jax.ShapeDtypeStruct(x_small.shape, BF),
            jax.ShapeDtypeStruct(x_big.shape, BF),
            jax.ShapeDtypeStruct(x_small.shape, BF),
            jax.ShapeDtypeStruct((plan.n, plan.total, 2 * W), BF),
            jax.ShapeDtypeStruct((W, W), F32),
            jax.ShapeDtypeStruct((W, 256), F32),
        ],
        compiler_params=params(),
        name="cells",
    )(rank, x_big, x_small, g_big, g_small, modes, *tables, lin_t, bias)


def backward_kernel(plan, part, p_big, p_small, g_big, g_small, kernel_all, spectrum, lin,
                    lin_grad, columns):
    big, small = plan.big, plan.small
    stages = plan.n.bit_length() - 1 + plan.nz.bit_length() - 1
    rows_bits = plan.n.bit_length() - 1
    pick_all, move_all, move_lin = fold_tables()
    zero_lanes = np.zeros((8, 256), np.float32)
    zero_lanes[0, : 128 : MX] = 1.0

    def kernel(pb, ps, gb, gs, kk, spec, lin_in, col_in, pick, move, shift, line, part_in, kernel_in,
               db, ds, out, weight_out, lin_out,
               part, sa, mb, dacc, send_z, recv_z, lin_buf, lin_recv,
               in_sem, zs, zr, ls, lr, *refs):
        i = pl.program_id(0)
        ex = Exchange(plan, part, out, refs)
        here = lax.axis_index("samples")
        loads = [
            pltpu.make_async_copy(part_in, part, in_sem.at[0]),
            pltpu.make_async_copy(kernel_in, ex.kernel, in_sem.at[1]),
        ]

        def z_peer(d):
            return lax.rem(here + d, plan.nz)

        def to_z(d):
            return remote(
                send_z.at[z_peer(d)], recv_z.at[d], zs.at[d], zr.at[d], {"samples": z_peer(d)}
            )

        def lin_partner(k):
            if k < rows_bits:
                return {"rows": flip(ex.me, 1 << k)}
            return {"samples": flip(here, 1 << (k - rows_bits))}

        def lin_step(k):
            return remote(lin_buf.at[k], lin_recv.at[k], ls.at[k], lr.at[k], lin_partner(k))

        @pl.when(i == 0)
        def _():
            for load in loads:
                load.start()
            greet([{"rows": d} for d in ex.partners()]
                  + [{"samples": z_peer(d)} for d in range(1, plan.nz)])
            ex.clear()
            folded = None
            for q in range(4):
                term = lax.dot_general(
                    lin_in[C * q : C * q + C, :], shift[q], (((1,), (0,)), ((), ())),
                    precision=lax.Precision.HIGHEST, preferred_element_type=F32,
                )
                folded = term if folded is None else folded + term
            lin_buf[0, :C, :] = folded
            lin_buf[0, C:, :] = lax.dot_general(
                line[...], col_in[...], (((1,), (1,)), ((), ())),
                precision=lax.Precision.HIGHEST, preferred_element_type=F32,
            )
            lin_step(0).start()
            sa[...] = jnp.zeros_like(sa)
            mb[...] = jnp.zeros_like(mb)
            dacc[...] = jnp.zeros_like(dacc)
            send_z[...] = jnp.zeros_like(send_z)
            for load in loads:
                load.wait()

        def run(p, g, d, geo, count):
            for at in range(2 * count):
                v = dot(kk[...], p[at, :, :, :].reshape(W, geo.cells))
                v = g[at, :, :, :].reshape(W, geo.cells) + v.astype(BF)
                d[at, :, :, :] = v.reshape(4, C, geo.cells)

        @pl.when(i < plan.steps)
        def _():
            run(pb, gb, db, big, plan.per)

        @pl.when(i == plan.steps)
        def _():
            run(ps, gs, ds, small, plan.nsmall // 2)

        def total(c):
            ex.finish_sum(c, 1.0 / MX)
            ex.mix(c, ((1,), (1,)))

        def weight_grad(c):
            crow = plan.crow
            grads = sample_rows(*(ex.acc[t, :crow, :] for t in range(3))).astype(BF)
            held = spec[pl.ds(c * crow, crow), :].astype(F32)
            spectra = sample_rows(*tiles(held)).astype(BF)
            for t, tile in enumerate(tiles(dot(spectra, pick[...]))):
                sa[t, 0, :crow, :] = tile[:crow]
                sa[t, 1, :crow, :] = tile[crow:]
            for t, tile in enumerate(tiles(dot(grads, move[...]))):
                mb[t, 0, :crow, :] = tile[:crow]
                mb[t, 1, :crow, :] = tile[crow:]

            def one(m):
                rows = pl.ds(m, plan.slots, stride=plan.own)
                left = [sa[q, s, rows, :] for q in range(4) for s in range(2)]
                right = [
                    jnp.concatenate([mb[2 * q, s, rows, :], mb[2 * q + 1, s, rows, :]], axis=1)
                    for q in range(4) for s in range(2)
                ]
                v = dot(
                    jnp.concatenate(left, axis=0).astype(BF),
                    jnp.concatenate(right, axis=0).astype(BF),
                    ((0,), (0,)),
                )
                dacc[m] += v[:C]

            unroll = 4

            @pl.loop(0, plan.own // unroll)
            def _(j):
                for u in range(unroll):
                    one(j * unroll + u)

        def send_weights():
            pairs = []
            for j in range(plan.own // 2):
                pairs.append(jnp.concatenate(pair_tiles(dacc[2 * j], dacc[2 * j + 1]), axis=1))
            rows = jnp.concatenate(pairs, axis=0).astype(BF)
            for z in range(plan.nz):
                lo = z * plan.zrows
                hi = min(lo + plan.zrows, plan.wrows)
                if hi > lo:
                    send_z[z, : hi - lo, :] = rows[lo:hi]
            for d in range(1, plan.nz):
                to_z(d).start()

        def sum_weights():
            v = send_z[here].astype(F32)
            for d in range(1, plan.nz):
                to_z(d).wait_recv()
                v = v + recv_z[d].astype(F32)
            weight_out[...] = v.astype(BF)

        def lin_next(k):
            lin_step(k).wait_recv()
            v = lin_buf[k] + lin_recv[k]
            if k + 1 < stages:
                lin_buf[k + 1] = v
                lin_step(k + 1).start()
            else:
                lin_out[...] = v

        def chunk_total(c):
            ex.finish_sum(c, 1.0 / MX)
            weight_grad(c)
            ex.mix(c, ((1,), (1,)))
            if c == plan.chunks - 1:
                send_weights()

        last = plan.count - 1
        hooks = [(2 * k + 1, lambda k=k: lin_next(k)) for k in range(stages)]
        hooks.append((4 * plan.count, sum_weights))
        starts = [c for c in range(plan.chunks)]
        schedule(plan, ex, i, chunk_total, starts, 2, hooks)

        @pl.when(i == last)
        def _():
            ex.drain()
            for d in range(1, plan.nz):
                to_z(d).wait_send()
            for k in range(stages):
                lin_step(k).wait_send()

    acc = plan.acc_rows
    dma = pltpu.SemaphoreType.DMA
    return pl.pallas_call(
        kernel,
        grid=(plan.count,),
        in_specs=[
            *plain_fields(plan),
            *plain_fields(plan),
            fixed((W, W)),
            fixed((plan.total, 2 * W)),
            fixed((W, W)),
            fixed((W, 256)),
            fixed(pick_all.shape),
            fixed(move_all.shape),
            fixed(move_lin.shape),
            fixed(zero_lanes.shape),
            ANYWHERE,
            ANYWHERE,
        ],
        out_specs=[
            *plain_fields(plan),
            ANYWHERE,
            fixed((plan.zrows, 2 * W)),
            fixed((C + 8, W)),
        ],
        out_shape=[
            jax.ShapeDtypeStruct(p_big.shape, BF),
            jax.ShapeDtypeStruct(p_small.shape, BF),
            jax.ShapeDtypeStruct((plan.chips, 2, plan.total, 2 * W), BF),
            jax.ShapeDtypeStruct((plan.zrows, 2 * W), BF),
            jax.ShapeDtypeStruct((C + 8, W), F32),
        ],
        scratch_shapes=[
            pltpu.VMEM((plan.chips, 2, plan.total, 2 * W), BF),
            pltpu.VMEM((4, 2, acc, 128), F32),
            pltpu.VMEM((8, 2, acc, 128), F32),
            pltpu.VMEM((plan.own, C, 256), F32),
            pltpu.VMEM((plan.nz, plan.zrows, 2 * W), BF),
            pltpu.VMEM((plan.nz, plan.zrows, 2 * W), BF),
            pltpu.VMEM((stages, C + 8, W), F32),
            pltpu.VMEM((stages, C + 8, W), F32),
            dma((2,)),
            dma((plan.nz,)),
            dma((plan.nz,)),
            dma((stages,)),
            dma((stages,)),
            *Exchange.scratch(plan),
        ],
        compiler_params=params(collective_id=2, has_side_effects=True),
        name="mode_backward",
    )(p_big, p_small, g_big, g_small, lin, spectrum, lin_grad, columns,
      pick_all, move_all, move_lin, zero_lanes, part, kernel_all)


def input_grads(plan, rank, part_big, part_small, modes):
    def body(r, pb, ps, m, vb, eb, vs, es, db, ds):
        i = pl.program_id(0)

        def run(part, d, geo, inverse, spread, count):
            span = spread.shape[1]
            for pair in range(count):
                qs = inverse_pair(geo, load_modes(plan, m, pair), inverse[...], 1.0)
                q = jnp.concatenate(qs, axis=0) * jnp.asarray(1.0 / geo.side, BF)
                for j in range(geo.cells // span):
                    v = dot(q[:, 128 * j : 128 * j + 128], spread[...])
                    at = (slice(2 * pair, 2 * pair + 2), slice(None), slice(None),
                          slice(j * span, (j + 1) * span))
                    d[at] = part[at].astype(F32) + v.reshape(2, 4, C, span)

        @pl.when(i < plan.steps)
        def _():
            run(pb, db, plan.big, vb, eb, plan.per)

        @pl.when(i == plan.steps)
        def _():
            run(ps, ds, plan.small, vs, es, plan.nsmall // 2)

    tables = []
    specs = []
    for geo in (plan.big, plan.small):
        tables += [geo.inverse, geo.spread]
        specs += [device_spec(geo.inverse.shape[1:]), const_spec(geo.spread.shape)]
    return pl.pallas_call(
        body,
        grid_spec=pltpu.PrefetchScalarGridSpec(
            num_scalar_prefetch=1,
            grid=(plan.steps + 1,),
            in_specs=[*field_specs(plan), mode_spec(plan), *specs],
            out_specs=[*field_specs(plan)],
        ),
        out_shape=[
            jax.ShapeDtypeStruct(part_big.shape, F32),
            jax.ShapeDtypeStruct(part_small.shape, F32),
        ],
        compiler_params=params(),
        name="input_grads",
    )(rank, part_big, part_small, modes, *tables)


def on_device(plan, x_big, x_small, spec_weight, lin_weight, lin_bias, grad_big, grad_small):
    rank = lax.axis_index("rows").reshape(1)
    lin = build_kernel(lin_weight)
    half = lin.T * jnp.asarray(0.5, BF)
    zero = jnp.zeros((W, 64), BF)
    half = jnp.concatenate([half[:, :128], zero, half[:, 128:], half[:, 128:], zero], axis=1)
    bias_lane = np.arange(128) % (2 * MX) == MX
    bias = lin_bias.reshape(W, 1) * jnp.asarray(0.5 * bias_lane, BF)

    whole = (plan.n, plan.total, 2 * W)
    modes, kernel, spectrum = forward_kernel(plan, x_big, x_small, spec_weight)
    out_big, out_small, pre_big, pre_small, part, lin_grad, columns = cells_pass(
        plan, rank, x_big, x_small, grad_big, grad_small, modes.reshape(whole), half, bias
    )
    part_big, part_small, modes, weight_part, lin_sum = backward_kernel(
        plan, part.reshape(plan.chips, 2, plan.total, 2 * W), pre_big, pre_small,
        grad_big, grad_small, kernel, spectrum, lin, lin_grad, columns,
    )
    here = lax.axis_index("samples")
    pieces = [weight_part]
    for d in range(1, plan.nz):
        pairs = [(z, (z + d) % plan.nz) for z in range(plan.nz)]
        pieces.append(lax.ppermute(weight_part, "samples", pairs))
    dx_big, dx_small = input_grads(plan, rank, part_big, part_small, modes.reshape(whole))
    order = lax.rem(here - jnp.arange(plan.nz) + plan.nz, plan.nz)
    rows = jnp.stack(pieces)[order].reshape(plan.nz * plan.zrows, 2 * W)
    rows = rows[: plan.wrows].reshape(plan.own // 2, C, 2 * W)
    even = jnp.concatenate([rows[..., :128], rows[..., 256:320]], axis=-1)
    odd = jnp.concatenate([rows[..., 128:256], rows[..., 320:]], axis=-1)
    spec_grad = jnp.stack([even, odd], axis=1).reshape(plan.own, C, 4, C)
    spec_grad = spec_grad.transpose(0, 2, 1, 3).astype(F32)
    lin_weight_grad = lin_sum[:C].reshape(C, 4, C).transpose(1, 0, 2)
    lin_bias_grad = lin_sum[C].reshape(4, C)
    return out_big, out_small, dx_big, dx_small, spec_grad, lin_weight_grad, lin_bias_grad


def solution(mesh):
    fields = P("samples", None, None, "rows")
    spec = P("rows", None, None, None)

    def run(x_big, x_small, *rest):
        count = mesh.shape["samples"]
        plan = Plan(mesh, x_big.shape[0] // count, x_small.shape[0] // count)

        def local(*args):
            return on_device(plan, *args)

        return jax.shard_map(
            local,
            mesh=mesh,
            in_specs=(fields, fields, spec, P(), P(), fields, fields),
            out_specs=(fields, fields, fields, fields, spec, P(), P()),
            check_vma=False,
        )(x_big, x_small, *rest)

    return run
```

```python
import math

import jax
import jax.numpy as jnp
import ml_dtypes
import numpy as np
from jax import lax
from jax.experimental import pallas as pl
from jax.experimental.pallas import tpu as pltpu
from jax.sharding import PartitionSpec as P

C = 48
MX = 16
N1 = 128
N2 = 64
W = 4 * C
MODES = MX * MX
BF = jnp.bfloat16
F32 = jnp.float32


def trig(side):
    a = np.arange(MX)
    freq = np.where(a < MX // 2, a, side - MX + a)
    phase = (np.arange(side)[:, None] * freq[None, :]) % side
    angle = phase.astype(np.float32) * np.float32(2.0 * math.pi / side)
    cos = np.cos(angle).astype(ml_dtypes.bfloat16).astype(np.float32)
    sin = np.sin(angle).astype(ml_dtypes.bfloat16).astype(np.float32)
    return cos, sin


def low(table):
    return table.astype(ml_dtypes.bfloat16)


class Geometry:
    def __init__(self, side, n):
        self.side = side
        self.rows = side // n
        self.cells = self.rows * side
        self.group = min(8, self.rows)
        self.ngroups = self.rows // self.group
        self.npairs = self.rows // 2
        self.qlanes = max(128, self.npairs * 64)
        self.hk = self.ngroups * 128
        cos, sin = trig(side)
        eye = np.eye(MX, dtype=np.float32)

        first = np.zeros((self.group, side, 256), np.float32)
        for h in range(self.group):
            first[h, :, h * MX : (h + 1) * MX] = cos
            first[h, :, 128 + h * MX : 128 + (h + 1) * MX] = sin
        self.first = low(first.reshape(self.group * side, 256))

        second = np.zeros((n, MX, MX, 2, self.ngroups, 128), np.float32)
        inverse = np.zeros((n, MX, MX, 2, self.qlanes), np.float32)
        for r in range(n):
            for h in range(self.rows):
                c, s = cos[r * self.rows + h], sin[r * self.rows + h]
                ce, se = c[:, None, None] * eye, s[:, None, None] * eye
                g, lane = h // self.group, (h % self.group) * MX
                second[r, :, :, 0, g, lane : lane + MX] = ce
                second[r, :, :, 1, g, lane : lane + MX] = se
                lane = h * 2 * MX
                inverse[r, :, :, 0, lane : lane + MX] = ce
                inverse[r, :, :, 0, lane + MX : lane + 2 * MX] = -se
                inverse[r, :, :, 1, lane : lane + MX] = -se
                inverse[r, :, :, 1, lane + MX : lane + 2 * MX] = -ce
        self.second = low(second.reshape(n, MODES, 2 * self.hk))
        inverse[..., MX : self.rows * 2 * MX : 2 * MX] = 0.0
        self.inverse = low(inverse.reshape(n, MODES, 2 * self.qlanes))

        spread = np.zeros((4, 2, MX, 4, side), np.float32)
        for h in range(4):
            spread[h, 0, :, h] = cos.T
            spread[h, 1, :, h] = sin.T
        self.spread = low(spread.reshape(128, 4 * side))
        if self.npairs == 1:
            self.spread = self.spread[:, : 2 * side]
        for h in range(4):
            spread[h, 1, 0, h] = 1.0
        self.pair_spread = low(spread.reshape(128, 4 * side))[:64, : 2 * side]


def turn(v):
    return jnp.concatenate([v[3 * C :], v[2 * C : 3 * C], -v[C : 2 * C], -v[:C]], axis=0)


def dot(a, b, dims=((1,), (0,))):
    return lax.dot_general(a, b, (dims, ((), ())), preferred_element_type=F32)


def forward_group(field, first, scale, keep=None):
    y = dot(field, first)
    grids = range(y.shape[0] // W)
    if keep is not None:
        keep(sum(y[W * s : W * s + W, :128] for s in grids))
    cols = []
    for s in grids:
        col = y[W * s : W * s + W, :128] + turn(y[W * s : W * s + W, 128:])
        cols.append((col * scale).astype(BF))
    return cols


def forward_rows(groups, second):
    stacked = []
    for s in range(2):
        cols = [cols[s] for cols in groups]
        stacked.append(jnp.concatenate(cols + [turn(col) for col in cols], axis=1))
    a, b = stacked
    both = jnp.concatenate([a[:128], b[:128], a[128:], b[128:]], axis=0)
    return dot(second, both, ((1,), (1,)))


def forward_grids(geo, get, first, second, scale):
    width = geo.group * geo.side
    groups = [forward_group(get(g * width, width), first, scale) for g in range(geo.ngroups)]
    return [
        forward_rows([cols[2 * k : 2 * k + 2] for cols in groups], second)
        for k in range(len(groups[0]) // 2)
    ]


def inverse_pair(geo, modes, inverse, scale):
    uv = dot(modes, inverse, ((0,), (0,)))
    result = []
    for s in range(2):
        part = jnp.concatenate(
            [uv[128 * s : 128 * s + 128], uv[256 + 64 * s : 320 + 64 * s]], axis=0
        )
        q = part[:, : geo.qlanes] + turn(part[:, geo.qlanes :])
        result.append((q * scale).astype(BF))
    return result


def fold_tables():
    dup = np.concatenate([np.arange(192), np.arange(128, 192)])
    pick = np.zeros((192, 4, 128), np.float32)
    move = np.zeros((192, 4, 192), np.float32)
    for q in range(4):
        pick[q * C : q * C + C, q, :C] = np.eye(C)
        for p in range(4):
            sign = -1.0 if (p >> 1) & q & 1 else 1.0
            o = p ^ q
            move[o * C : o * C + C, q, p * C : p * C + C] = sign * np.eye(C)
    return (
        low(pick[dup].reshape(256, 512)),
        low(move[dup][:, :, dup].reshape(256, 1024)),
        move.transpose(1, 0, 2).copy(),
    )


def expand_tables():
    dup = np.concatenate([np.arange(192), np.arange(128, 192)])
    place = np.zeros((4, C, 4, 256), np.float32)
    for p in range(4):
        for q in range(4):
            sign = -1.0 if (p >> 1) & q & 1 else 1.0
            full = np.zeros((C, 192), np.float32)
            o = p ^ q
            full[:, o * C : (o + 1) * C] = sign * np.eye(C)
            place[p, :, q] = full[:, dup]
    return low(place.reshape(W, 1024))


class Plan:
    def __init__(self, mesh, nbig, nsmall):
        self.n = mesh.shape["rows"]
        self.nz = mesh.shape["samples"]
        self.own = MODES // self.n
        self.per = max(1, 16 // self.own)
        self.big = Geometry(N1, self.n)
        self.small = Geometry(N2, self.n)
        self.nbig, self.nsmall = nbig, nsmall
        assert nbig % (2 * self.per) == 0 and nsmall % 2 == 0 and nsmall // 2 <= self.per
        self.steps = nbig // (2 * self.per)
        self.count = self.steps + 1
        self.wide_per = 2 * self.per if self.steps % 2 == 0 else self.per
        self.wide_steps = nbig // (2 * self.wide_per)
        self.block = self.per * self.own
        self.total = self.count * self.block
        self.chunks = next(c for c in (3, 2, 1) if self.count % c == 0)
        self.span = self.count // self.chunks
        self.crow = self.span * self.block
        self.half = self.crow // 2
        self.slots = -(-(self.span * self.per) // 8) * 8
        self.acc_rows = self.slots * self.own
        self.chips = self.n // 2
        bits = list(range(1, self.n.bit_length() - 1))
        self.orders = (bits, bits[::-1])
        self.levels = len(bits)
        self.wrows = self.own // 2 * C
        self.zrows = -(-self.wrows // (16 * self.nz)) * 16

    def mask(self, h, idx):
        m = 0
        for t, b in enumerate(self.orders[h]):
            if idx >> (self.levels - 1 - t) & 1:
                m |= 1 << b
        return m


def wide(i, last):
    return jnp.minimum(i, last)


def params(**kw):
    return pltpu.CompilerParams(vmem_limit_bytes=56 * 1024 * 1024, **kw)


def const_spec(shape):
    return pl.BlockSpec(shape, lambda i, r: (0,) * len(shape))


def device_spec(shape):
    return pl.BlockSpec((None,) + shape, lambda i, r: (r[0],) + (0,) * len(shape))


def field_specs(plan):
    big, small = plan.big, plan.small
    last = plan.steps - 1
    return (
        pl.BlockSpec((2 * plan.per, 4, C, big.cells), lambda i, r: (wide(i, last), 0, 0, 0)),
        pl.BlockSpec((plan.nsmall, 4, C, small.cells), lambda i, r: (0, 0, 0, 0)),
    )


def mode_spec(plan):
    return pl.BlockSpec((plan.n, plan.block, 2 * W), lambda i, r: (0, i, 0))


def store_modes(plan, ref, pair, z):
    z = z.reshape(plan.n, plan.own, 2 * W).astype(BF)
    ref[:, pair * plan.own : (pair + 1) * plan.own, :] = z


def load_modes(plan, ref, pair):
    return ref[:, pair * plan.own : (pair + 1) * plan.own, :].reshape(MODES, 2 * W)


def cost(flops, moved):
    return pl.CostEstimate(flops=flops, bytes_accessed=moved, transcendentals=0)


def flip(index, mask):
    result = index
    for b in range(mask.bit_length()):
        if mask >> b & 1:
            bit = lax.rem(lax.div(index, 1 << b), 2)
            result = result + (1 - 2 * bit) * (1 << b)
    return result


def tiles(v):
    return [v[:, 128 * t : 128 * t + 128] for t in range(v.shape[1] // 128)]


def sample_rows(first, second, third):
    lane = lax.broadcasted_iota(jnp.int32, third.shape, 1)
    a = jnp.concatenate([first, jnp.where(lane < 64, third, 0.0)], axis=1)
    b = jnp.concatenate([second, jnp.where(lane < 64, 0.0, third)], axis=1)
    return jnp.concatenate([a, b], axis=0)


def pair_tiles(a, b):
    lane = lax.broadcasted_iota(jnp.int32, (a.shape[0], 128), 1)
    return a[:, :128], b[:, :128], jnp.where(lane < 64, a[:, 128:], b[:, 128:])


def remote(src, dst, send, recv, device):
    return pltpu.make_async_remote_copy(
        src_ref=src, dst_ref=dst, send_sem=send, recv_sem=recv, device_id=device
    )


class Stream:
    def __init__(self, field, ring, sems, grids):
        self.field, self.ring, self.sems, self.grids = field, ring, sems, grids
        self.depth = ring.shape[0]

    @staticmethod
    def scratch(depth, grids, cells):
        return [pltpu.VMEM((depth, grids, 4, C, cells), BF), pltpu.SemaphoreType.DMA((depth,))]

    def slot(self, i):
        return self.ring.at[lax.rem(i, self.depth)]

    def copy(self, i, out=False):
        block = self.field.at[pl.ds(i * self.grids, self.grids)]
        sem = self.sems.at[lax.rem(i, self.depth)]
        if out:
            return pltpu.make_async_copy(self.slot(i), block, sem)
        return pltpu.make_async_copy(block, self.slot(i), sem)

    def read(self, i, count):
        @pl.when(i == 0)
        def _():
            for k in range(min(self.depth, count)):
                self.copy(jnp.int32(k)).start()

        self.copy(i).wait()
        return self.slot(i)

    def ahead(self, i, count):
        @pl.when(i + self.depth < count)
        def _():
            self.copy(i + self.depth).start()

    def reserve(self, i):
        @pl.when(i >= self.depth)
        def _():
            self.copy(i - self.depth, True).wait()

        return self.slot(i)

    def flush(self, count):
        for k in range(max(0, count - self.depth), count):
            self.copy(jnp.int32(k), True).wait()


class Exchange:
    SCRATCH = 16

    @staticmethod
    def scratch(plan):
        n, chips, width = plan.n, plan.chips, 2 * W
        dma = pltpu.SemaphoreType.DMA
        part = (plan.chunks, 2)
        return [
            pltpu.VMEM((chips, plan.total, width), BF),
            pltpu.VMEM((2, chips, plan.chunks * plan.half, width), BF),
            pltpu.VMEM((2, chips, plan.chunks * plan.half, width), BF),
            pltpu.VMEM((chips, 2, plan.total, width), BF),
            pltpu.VMEM((3, plan.acc_rows, 128), F32),
            pltpu.VMEM((3, plan.acc_rows, 128), F32),
            dma((plan.chunks,)),
            dma((plan.chunks,)),
            dma(part + (plan.levels,)),
            dma(part + (plan.levels,)),
            dma(part + (chips,)),
            dma(part + (chips,)),
            dma(part + (chips,)),
            dma(part + (chips,)),
            dma((plan.chunks,)),
            pltpu.VMEM((plan.own, 256, 256), BF),
        ]

    def __init__(self, plan, part, out, refs, origin=None):
        self.plan, self.part, self.out = plan, part, out
        self.origin = part if origin is None else origin
        (self.sib, self.sums, self.lev, self.res, self.acc, self.mixed,
         self.sib_s, self.sib_r, self.lev_s, self.lev_r, self.ag_s, self.ag_r,
         self.fw_s, self.fw_r, self.out_s, self.kernel) = refs
        self.me = lax.axis_index("rows")
        self.core = lax.rem(self.me, 2)

    def partners(self):
        return [flip(self.me, 1 << b) for b in range(self.plan.n.bit_length() - 1)]

    def to_sibling(self, c):
        rows = pl.ds(c * self.plan.crow, self.plan.crow)
        return remote(
            self.origin.at[:, 1 - self.core, rows, :], self.sib.at[:, rows, :],
            self.sib_s.at[c], self.sib_r.at[c], {"rows": flip(self.me, 1)},
        )

    def level(self, c, h, t):
        plan = self.plan
        count = plan.chips >> (t + 1)
        rows = pl.ds(c * plan.half, plan.half)
        at = plan.chips - 2 * count
        return remote(
            self.sums.at[h, pl.ds(count, count), rows, :],
            self.lev.at[h, pl.ds(at, count), rows, :],
            self.lev_s.at[c, h, t], self.lev_r.at[c, h, t],
            {"rows": flip(self.me, 1 << plan.orders[h][t])},
        )

    def rows(self, c, h):
        return pl.ds(c * self.plan.crow + h * self.plan.half, self.plan.half)

    def block(self, c, h, owner):
        return self.res.at[lax.div(owner, 2), lax.rem(owner, 2), self.rows(c, h), :]

    def gather(self, c, h, u, idx):
        plan = self.plan
        sem = (1 << u) - 1 + idx
        ref = self.block(c, h, flip(self.me, plan.mask(h, idx)))
        return remote(
            ref, ref, self.ag_s.at[c, h, sem], self.ag_r.at[c, h, sem],
            {"rows": flip(self.me, 1 << plan.orders[h][plan.levels - 1 - u])},
        )

    def forward(self, c, h, idx):
        ref = self.block(c, h, flip(self.me, self.plan.mask(h, idx)))
        return remote(
            ref, ref, self.fw_s.at[c, h, idx], self.fw_r.at[c, h, idx],
            {"rows": flip(self.me, 1)},
        )

    def store(self, c):
        rows = pl.ds(c * self.plan.crow, self.plan.crow)
        return pltpu.make_async_copy(
            self.res.at[:, :, rows, :], self.out.at[:, :, rows, :], self.out_s.at[c]
        )

    def begin(self, c):
        self.to_sibling(c).start()

    def add_sibling(self, c):
        plan = self.plan
        self.to_sibling(c).wait_recv()
        for far in (1, 0):
            for h in range(2):
                span = plan.chips // 2
                for idx in range(far * span, far * span + span):
                    owner = flip(self.me, plan.mask(h, idx))
                    chip = lax.div(owner, 2)
                    rows = self.rows(c, h)
                    v = self.part[chip, self.core, rows, :].astype(F32)
                    v = v + self.sib[chip, rows, :].astype(F32)
                    self.sums[h, idx, pl.ds(c * plan.half, plan.half), :] = v.astype(BF)
                if far:
                    self.level(c, h, 0).start()

    def next_level(self, c, t):
        plan = self.plan
        rows = pl.ds(c * plan.half, plan.half)
        count = plan.chips >> t
        at = plan.chips - 2 * count
        for h in range(2):
            self.level(c, h, t - 1).wait_recv()
            for idx in reversed(range(count)):
                v = self.sums[h, idx, rows, :].astype(F32)
                v = v + self.lev[h, at + idx, rows, :].astype(F32)
                self.sums[h, idx, rows, :] = v.astype(BF)
                if idx == count // 2:
                    self.level(c, h, t).start()

    def finish_sum(self, c, scale):
        plan = self.plan
        rows = pl.ds(c * plan.half, plan.half)
        for h in range(2):
            self.level(c, h, plan.levels - 1).wait_recv()
            v = self.sums[h, 0, rows, :].astype(F32)
            v = (v + self.lev[h, plan.chips - 2, rows, :].astype(F32)) * scale
            for t, tile in enumerate(tiles(v)):
                self.acc[t, h * plan.half : (h + 1) * plan.half, :] = tile

    def mix(self, c, dims):
        plan = self.plan

        def one(m):
            rows = pl.ds(m, plan.slots, stride=plan.own)
            lhs = sample_rows(*(self.acc[t, rows, :] for t in range(3))).astype(BF)
            res = dot(lhs, self.kernel[m], dims)
            for t, tile in enumerate(pair_tiles(res[: plan.slots], res[plan.slots :])):
                self.mixed[t, rows, :] = tile

        unroll = 8

        @pl.loop(0, plan.own // unroll)
        def _(j):
            for u in range(unroll):
                one(j * unroll + u)

        result = jnp.concatenate([self.mixed[t, : plan.crow, :] for t in range(3)], axis=1)
        self.res[lax.div(self.me, 2), self.core, pl.ds(c * plan.crow, plan.crow), :] = (
            result.astype(BF)
        )
        for h in range(2):
            self.gather(c, h, 0, 0).start()
            self.forward(c, h, 0).start()

    def spread(self, c, u):
        for h in range(2):
            got = 1 << (u - 1)
            for idx in range(got):
                self.gather(c, h, u - 1, idx).wait_recv()
            if u < self.plan.levels:
                for idx in reversed(range(2 * got)):
                    self.gather(c, h, u, idx).start()
            for idx in range(got, 2 * got):
                self.forward(c, h, idx).start()

    def close(self, c):
        for h in range(2):
            for idx in range(self.plan.chips):
                self.forward(c, h, idx).wait_recv()
        self.store(c).start()

    def drain(self):
        plan = self.plan
        for c in range(plan.chunks):
            self.to_sibling(c).wait_send()
            for h in range(2):
                for t in range(plan.levels):
                    self.level(c, h, t).wait_send()
                for u in range(plan.levels):
                    for idx in range(1 << u):
                        self.gather(c, h, u, idx).wait_send()
                for idx in range(plan.chips):
                    self.forward(c, h, idx).wait_send()
            self.store(c).wait()

    def clear(self):
        plan = self.plan
        if plan.acc_rows > plan.crow:
            rest = plan.acc_rows - plan.crow
            self.acc[:, plan.crow :, :] = jnp.zeros((3, rest, 128), F32)

    def waves(self, total):
        plan = self.plan
        todo = []
        for c in range(plan.chunks):
            chain = [lambda c=c, t=t: self.next_level(c, t) for t in range(1, plan.levels)]
            chain += [lambda c=c: total(c)]
            chain += [lambda c=c, u=u: self.spread(c, u) for u in range(1, plan.levels + 1)]
            chain += [lambda c=c: self.close(c)]
            todo.append(chain)
        waves = []
        for w in range(len(todo[0]) + plan.chunks - 1):
            at = [(c, w - c) for c in reversed(range(plan.chunks))]
            waves.append([todo[c][k] for c, k in at if 0 <= k < len(todo[c])])
        return waves


def greet(devices):
    barrier = pltpu.get_barrier_semaphore()
    for device in devices:
        pl.semaphore_signal(barrier, inc=1, device_id=device)
    pl.semaphore_wait(barrier, len(devices))


def build_modes(plan, place, weights, kernel):
    flat = jnp.concatenate([weights[:, p].reshape(-1, C) for p in range(4)], axis=1)
    for q in range(4):
        rows = dot(flat, place[:, 256 * q : 256 * q + 256])
        kernel[:, C * q : C * q + C, :] = rows.astype(BF).reshape(plan.own, C, 256)
    kernel[:, W:, :] = kernel[:, 128:W, :]


def build_lin(place, weight):
    flat = jnp.concatenate([weight[p] for p in range(4)], axis=1)
    rows = [dot(flat, place[:, 256 * q : 256 * q + 256]) for q in range(4)]
    return jnp.concatenate(rows, axis=0).astype(BF)


def half_tables():
    rows = np.zeros((192, 384), np.float32)
    rows[:128, :128] = 0.5 * np.eye(128)
    rows[128:, 192:256] = 0.5 * np.eye(64)
    rows[128:, 256:320] = 0.5 * np.eye(64)
    line = np.zeros((128, C), np.float32)
    line[MX :: 2 * MX] = 0.5
    return low(rows), low(line), low(np.eye(C, dtype=np.float32))


def plain_fields(plan):
    big, small = plan.big, plan.small
    last = plan.steps - 1
    return [
        pl.BlockSpec((2 * plan.per, 4, C, big.cells), lambda i: (wide(i, last), 0, 0, 0)),
        pl.BlockSpec((plan.nsmall, 4, C, small.cells), lambda i: (0, 0, 0, 0)),
    ]


def fixed(shape):
    return pl.BlockSpec(shape, lambda i: (0,) * len(shape))


ANYWHERE = pl.BlockSpec(memory_space=pl.ANY)


def forward_kernel(plan, x_big, x_small, spec_weight):
    big, small = plan.big, plan.small
    last = plan.wide_steps

    def kernel(x_hbm, xs, fb, fs, place, weights, sb_all, ss_all, out, kernel_out, spectrum,
               part, sb, ss, table_sem, ring, ring_sem, *refs):
        i = pl.program_id(0)
        stream = Stream(x_hbm, ring, ring_sem, 2 * plan.wide_per)
        ex = Exchange(plan, part, out, refs)
        loads = [
            pltpu.make_async_copy(sb_all.at[ex.me], sb, table_sem.at[0]),
            pltpu.make_async_copy(ss_all.at[ex.me], ss, table_sem.at[1]),
        ]
        keep = pltpu.make_async_copy(ex.kernel, kernel_out, table_sem.at[2])

        @pl.when(i == 0)
        def _():
            for load in loads:
                load.start()
            greet([{"rows": d} for d in ex.partners()])
            ex.clear()
            for load in loads:
                load.wait()

        def run(x, geo, first, second, count, per):
            def get(start, width):
                v = x[: 2 * count, :, :, start : start + width]
                return v.reshape(2 * count * W, width)

            zs = forward_grids(geo, get, first[...], second[...], 1.0 / geo.side)
            parts = [z.reshape(plan.chips, 2, plan.own, 2 * W) for z in zs]
            parts += [jnp.zeros_like(parts[0])] * (per - count)
            z = jnp.concatenate(parts, axis=2) if per > 1 else parts[0]
            rows = pl.ds(pl.multiple_of(i * plan.wide_per * plan.own, 16), per * plan.own)
            part[:, :, rows, :] = z.astype(BF)

        @pl.when(i < last)
        def _():
            run(stream.read(i, last), big, fb, sb, plan.wide_per, plan.wide_per)
            stream.ahead(i, last)

        @pl.when(i == last)
        def _():
            run(xs, small, fs, ss, plan.nsmall // 2, plan.per)

        def total(c):
            ex.finish_sum(c, 1.0)
            spectrum[pl.ds(c * plan.crow, plan.crow), :] = jnp.concatenate(
                [ex.acc[t, : plan.crow, :] for t in range(3)], axis=1
            ).astype(BF)
            ex.mix(c, ((1,), (0,)))

        def prepare():
            build_modes(plan, place, weights, ex.kernel)
            keep.start()

        waves = ex.waves(total)
        items = []
        for c in range(plan.chunks):
            pairs = (c + 1) * plan.span * plan.per
            end = min(-(-pairs // plan.wide_per) - 1, last)
            items.append((end, lambda c=c: ex.begin(c)))
            if c == plan.chunks - 1:
                items.append((last, prepare))
                items += [(last, task) for task in waves.pop(0)]
            items.append((min(end + 1, last), lambda c=c: ex.add_sibling(c)))
        items += [(last, task) for wave in waves for task in wave]
        schedule(last, i, items)

        @pl.when(i == last)
        def _():
            ex.drain()
            keep.wait()

    return pl.pallas_call(
        kernel,
        grid=(last + 1,),
        in_specs=[
            ANYWHERE,
            plain_fields(plan)[1],
            fixed(big.first.shape),
            fixed(small.first.shape),
            fixed((W, 1024)),
            fixed(spec_weight.shape),
            ANYWHERE,
            ANYWHERE,
        ],
        out_specs=[ANYWHERE, ANYWHERE, fixed((plan.total, 2 * W))],
        out_shape=[
            jax.ShapeDtypeStruct((plan.chips, 2, plan.total, 2 * W), BF),
            jax.ShapeDtypeStruct((plan.own, 256, 256), BF),
            jax.ShapeDtypeStruct((plan.total, 2 * W), BF),
        ],
        scratch_shapes=[
            pltpu.VMEM((plan.chips, 2, plan.total, 2 * W), BF),
            pltpu.VMEM(big.second.shape[1:], BF),
            pltpu.VMEM(small.second.shape[1:], BF),
            pltpu.SemaphoreType.DMA((3,)),
            *Stream.scratch(min(4, last), 2 * plan.wide_per, big.cells),
            *Exchange.scratch(plan),
        ],
        compiler_params=params(collective_id=1, has_side_effects=True),
        name="mode_forward",
    )(x_big, x_small, big.first, small.first, expand_tables(), spec_weight,
      big.second, small.second)


def schedule(last, i, items):
    for step in range(last + 1):
        now = [task for when, task in items if min(when, last) == step]
        if now:
            @pl.when(i == step)
            def _(now=now):
                for task in now:
                    task()


def cells_pass(plan, rank, x_big, x_small, g_big, g_small, modes, lin_weight,
               lin_bias):
    k0 = math.sqrt(2.0 / math.pi)
    k1 = k0 * 0.044715

    def low_of(value):
        return jnp.asarray(value, BF)

    per, steps = plan.wide_per, plan.wide_steps
    last = steps - 1

    def body(r, xb, xs, gb, gs, m, ms, fb, sb, vb, eb, fs, ss, vs, es,
             place, rows_table, line, eye, lw, lb, ob, os_, pb, ps, z, lin_acc, y_acc,
             kt, bias_ref):
        i = pl.program_id(0)

        @pl.when(i == 0)
        def _():
            full = build_lin(place[...], lw)[:, :W]
            kt[...] = dot(full, rows_table[...], ((0,), (0,))).astype(BF)
            for q in range(4):
                bias_ref[C * q : C * q + C, :] = dot(
                    eye[...], line[...] * lb[q : q + 1, :], ((1,), (1,))
                ).astype(BF)
            lin_acc[...] = jnp.zeros_like(lin_acc)
            y_acc[...] = jnp.zeros_like(y_acc)

        def run(x, g, o, d, m, z, geo, first, second, inverse, spread, count):
            wide_cells = 2 * geo.side
            lane = lax.broadcasted_iota(jnp.int32, (W, 128), 1)
            held, groups = {}, {}

            def rows_back(pair):
                qs = inverse_pair(geo, load_modes(plan, m, pair), inverse[...], 0.5 / MX)
                line = jnp.concatenate([bias_ref[...]] * (geo.qlanes // 128), axis=1)
                for s in range(2):
                    held[2 * pair + s] = qs[s] + line

            def main(at, p):
                lo = p * wide_cells
                cells = slice(lo, lo + wide_cells)
                q = held[at][:, 128 * (p // 2) : 128 * (p // 2) + 128]
                xv = x[at, :, :, cells].reshape(W, wide_cells)
                if p % 2 == 0:
                    tail = jnp.where(lane < 64, q, kt[:, 128:256])
                    rhs = [xv[:128], spread[...], xv[128:]]
                else:
                    tail = jnp.where(lane >= 64, q, kt[:, 256:384])
                    rhs = [xv[:128], xv[128:], spread[...]]
                lhs = jnp.concatenate([kt[:, :128], tail], axis=1)
                b = dot(lhs, jnp.concatenate(rhs, axis=0))
                b = b.astype(BF)
                b2 = b * b
                e = low_of(1.0) + jnp.tanh(b * (low_of(2.0 * k0) + low_of(8.0 * k1) * b2))
                o[at, :, :, cells] = (xv + b * e).reshape(4, C, wide_cells)
                rise = b * (low_of(k0) + low_of(12.0 * k1) * b2)
                slope = e * (low_of(0.5) + rise * (low_of(2.0) - e))
                gv = g[at, :, :, cells].reshape(W, wide_cells)
                d[at, :, :, cells] = (gv * slope).reshape(4, C, wide_cells)

            def weight_grad(at, part):
                span = geo.cells // 2
                xa = x[at, :, :, part * span : part * span + span].reshape(W, span)
                pa = d[at, :, :, part * span : part * span + span].reshape(W, span)
                lin_acc[...] += dot(xa, pa, ((1,), (1,)))

            def keep(y):
                y_acc[...] += y

            def columns(pair, k):
                width = geo.group * geo.side
                v = d[2 * pair : 2 * pair + 2, :, :, k * width : k * width + width]
                cols = forward_group(v.reshape(2 * W, width), first[...], 1.0, keep)
                groups.setdefault(pair, []).append(cols)

            def rows_out(pair):
                store_modes(plan, z, pair, forward_rows(groups[pair], second[...]))

            side = []
            rows_back(0)
            for at in range(2 * count):
                pair = at // 2
                if at % 2 == 0 and pair + 1 < count:
                    side.append(lambda pair=pair: rows_back(pair + 1))
                for p in range(geo.npairs):
                    main(at, p)
                    if side:
                        side.pop(0)()
                side += [lambda at=at, k=k: weight_grad(at, k) for k in range(2)]
                if at % 2 == 1:
                    side += [lambda pair=pair, k=k: columns(pair, k) for k in range(geo.ngroups)]
                    side.append(lambda pair=pair: rows_out(pair))
            for task in side:
                task()

        @pl.when(i < steps)
        def _():
            run(xb, gb, ob, pb, m, z, plan.big, fb, sb, vb, eb, per)

        @pl.when(i == steps)
        def _():
            if plan.nsmall // 2 < per:
                z[...] = jnp.zeros_like(z)
            run(xs, gs, os_, ps, ms, z, plan.small, fs, ss, vs, es, plan.nsmall // 2)

    big, small = plan.big, plan.small
    tables = []
    specs = []
    for geo in (big, small):
        tables += [geo.first, geo.second, geo.inverse, geo.pair_spread]
        specs += [
            const_spec(geo.first.shape),
            device_spec(geo.second.shape[1:]),
            device_spec(geo.inverse.shape[1:]),
            const_spec(geo.pair_spread.shape),
        ]
    extra = [expand_tables(), *half_tables(), lin_weight, lin_bias]
    small_field = field_specs(plan)[1]
    big_field = pl.BlockSpec((2 * per, 4, C, big.cells), lambda i, r: (wide(i, last), 0, 0, 0))
    rows = per * plan.own
    return pl.pallas_call(
        body,
        grid_spec=pltpu.PrefetchScalarGridSpec(
            num_scalar_prefetch=1,
            grid=(steps + 1,),
            in_specs=[
                big_field,
                small_field,
                big_field,
                small_field,
                pl.BlockSpec((plan.n, rows, 2 * W), lambda i, r: (0, wide(i, last), 0)),
                pl.BlockSpec((plan.n, plan.block, 2 * W), lambda i, r: (0, plan.steps, 0)),
                *specs,
                *[const_spec(v.shape) for v in extra],
            ],
            out_specs=[
                big_field,
                small_field,
                big_field,
                small_field,
                pl.BlockSpec((plan.n, rows, 2 * W), lambda i, r: (0, i, 0)),
                const_spec((W, W)),
                const_spec((W, 128)),
            ],
            scratch_shapes=[pltpu.VMEM((W, 2 * W), BF), pltpu.VMEM((W, 128), BF)],
        ),
        out_shape=[
            jax.ShapeDtypeStruct(x_big.shape, BF),
            jax.ShapeDtypeStruct(x_small.shape, BF),
            jax.ShapeDtypeStruct(x_big.shape, BF),
            jax.ShapeDtypeStruct(x_small.shape, BF),
            jax.ShapeDtypeStruct((plan.n, (steps + 1) * rows, 2 * W), BF),
            jax.ShapeDtypeStruct((W, W), F32),
            jax.ShapeDtypeStruct((W, 128), F32),
        ],
        compiler_params=params(),
        name="cells",
    )(rank, x_big, x_small, g_big, g_small, modes, modes, *tables, *extra)


def backward_kernel(plan, part, p_big, p_small, g_big, g_small, kernel_all, spectrum,
                    lin_weight, lin_grad, columns):
    big, small = plan.big, plan.small
    stages = plan.n.bit_length() - 1 + plan.nz.bit_length() - 1
    rows_bits = plan.n.bit_length() - 1
    pick_all, move_all, move_lin = fold_tables()
    zero_lanes = np.zeros((8, 128), np.float32)
    zero_lanes[0, ::MX] = 1.0

    def kernel(pb, ps, gb, gs, place, lw, spec, lin_in, col_in, pick, move, shift, line, part_in, kernel_in,
               db, ds, out, weight_out, lin_out,
               part, kk, sa, mb, dacc, send_z, recv_z, lin_buf, lin_recv,
               in_sem, zs, zr, ls, lr, p_ring, p_sem, g_ring, g_sem, d_ring, d_sem, *refs):
        i = pl.program_id(0)
        p_stream = Stream(pb, p_ring, p_sem, 2 * plan.per)
        g_stream = Stream(gb, g_ring, g_sem, 2 * plan.per)
        d_stream = Stream(db, d_ring, d_sem, 2 * plan.per)
        ex = Exchange(plan, part, out, refs, part_in)
        here = lax.axis_index("samples")
        loads = [
            pltpu.make_async_copy(
                part_in.at[:, :, pl.ds(0, plan.total), :], part, in_sem.at[0]
            ),
            pltpu.make_async_copy(kernel_in, ex.kernel, in_sem.at[1]),
        ]

        def z_peer(d):
            return lax.rem(here + d, plan.nz)

        def to_z(d):
            return remote(
                send_z.at[z_peer(d)], recv_z.at[d], zs.at[d], zr.at[d], {"samples": z_peer(d)}
            )

        def lin_partner(k):
            if k < rows_bits:
                return {"rows": flip(ex.me, 1 << k)}
            return {"samples": flip(here, 1 << (k - rows_bits))}

        def lin_step(k):
            return remote(lin_buf.at[k], lin_recv.at[k], ls.at[k], lr.at[k], lin_partner(k))

        @pl.when(i == 0)
        def _():
            for load in loads:
                load.start()
            greet([{"rows": d} for d in ex.partners()]
                  + [{"samples": z_peer(d)} for d in range(1, plan.nz)])
            for c in range(plan.chunks):
                ex.begin(c)
            folded = None
            for q in range(4):
                term = lax.dot_general(
                    lin_in[C * q : C * q + C, :], shift[q], (((1,), (0,)), ((), ())),
                    precision=lax.Precision.HIGHEST, preferred_element_type=F32,
                )
                folded = term if folded is None else folded + term
            lin_buf[0, :C, :] = folded
            lin_buf[0, C:, :] = lax.dot_general(
                line[...], col_in[...], (((1,), (1,)), ((), ())),
                precision=lax.Precision.HIGHEST, preferred_element_type=F32,
            )
            lin_step(0).start()
            kk[...] = build_lin(place[...], lw)[:, :W]
            loads[0].wait()
            for c in range(plan.chunks):
                ex.add_sibling(c)
            ex.clear()
            sa[...] = jnp.zeros_like(sa)
            mb[...] = jnp.zeros_like(mb)
            dacc[...] = jnp.zeros_like(dacc)
            send_z[...] = jnp.zeros_like(send_z)
            loads[1].wait()

        def run(p, g, d, geo, count):
            for at in range(2 * count):
                v = dot(kk[...], p[at, :, :, :].reshape(W, geo.cells))
                v = g[at, :, :, :].reshape(W, geo.cells) + v.astype(BF)
                d[at, :, :, :] = v.reshape(4, C, geo.cells)

        @pl.when(i < plan.steps)
        def _():
            p = p_stream.read(i, plan.steps)
            g = g_stream.read(i, plan.steps)
            run(p, g, d_stream.reserve(i), big, plan.per)
            d_stream.copy(i, True).start()
            p_stream.ahead(i, plan.steps)
            g_stream.ahead(i, plan.steps)

        @pl.when(i == plan.steps)
        def _():
            run(ps, gs, ds, small, plan.nsmall // 2)

        def weight_grad(c):
            crow = plan.crow
            grads = sample_rows(*(ex.acc[t, :crow, :] for t in range(3))).astype(BF)
            held = spec[pl.ds(c * crow, crow), :].astype(F32)
            spectra = sample_rows(*tiles(held)).astype(BF)
            for t, tile in enumerate(tiles(dot(spectra, pick[...]))):
                sa[t, 0, :crow, :] = tile[:crow]
                sa[t, 1, :crow, :] = tile[crow:]
            for t, tile in enumerate(tiles(dot(grads, move[...]))):
                mb[t, 0, :crow, :] = tile[:crow]
                mb[t, 1, :crow, :] = tile[crow:]

            def one(m):
                rows = pl.ds(m, plan.slots, stride=plan.own)
                left = [sa[q, s, rows, :] for q in range(4) for s in range(2)]
                right = [
                    jnp.concatenate([mb[2 * q, s, rows, :], mb[2 * q + 1, s, rows, :]], axis=1)
                    for q in range(4) for s in range(2)
                ]
                v = dot(
                    jnp.concatenate(left, axis=0).astype(BF),
                    jnp.concatenate(right, axis=0).astype(BF),
                    ((0,), (0,)),
                )
                dacc[m] += v[:C]

            unroll = 4

            @pl.loop(0, plan.own // unroll)
            def _(j):
                for u in range(unroll):
                    one(j * unroll + u)

        def send_weights():
            pairs = []
            for j in range(plan.own // 2):
                pairs.append(jnp.concatenate(pair_tiles(dacc[2 * j], dacc[2 * j + 1]), axis=1))
            rows = jnp.concatenate(pairs, axis=0).astype(BF)
            for z in range(plan.nz):
                lo = z * plan.zrows
                hi = min(lo + plan.zrows, plan.wrows)
                if hi > lo:
                    send_z[z, : hi - lo, :] = rows[lo:hi]
            for d in range(1, plan.nz):
                to_z(d).start()

        def sum_weights():
            v = send_z[here].astype(F32)
            for d in range(1, plan.nz):
                to_z(d).wait_recv()
                v = v + recv_z[d].astype(F32)
            weight_out[...] = v.astype(BF)

        def lin_next(k):
            lin_step(k).wait_recv()
            v = lin_buf[k] + lin_recv[k]
            if k + 1 < stages:
                lin_buf[k + 1] = v
                lin_step(k + 1).start()
            else:
                lin_out[...] = v

        def chunk_total(c):
            ex.finish_sum(c, 1.0 / MX)
            ex.mix(c, ((1,), (1,)))
            weight_grad(c)
            if c == plan.chunks - 1:
                send_weights()

        last = plan.count - 1
        items = [(2 * k + 1, lambda k=k: lin_next(k)) for k in range(stages)]
        for w, wave in enumerate(ex.waves(chunk_total)):
            items += [(2 + 2 * w, task) for task in wave]
        items.append((last, sum_weights))
        schedule(last, i, items)

        @pl.when(i == last)
        def _():
            ex.drain()
            d_stream.flush(plan.steps)
            for d in range(1, plan.nz):
                to_z(d).wait_send()
            for k in range(stages):
                lin_step(k).wait_send()

    acc = plan.acc_rows
    dma = pltpu.SemaphoreType.DMA
    return pl.pallas_call(
        kernel,
        grid=(plan.count,),
        in_specs=[
            ANYWHERE,
            plain_fields(plan)[1],
            ANYWHERE,
            plain_fields(plan)[1],
            fixed((W, 1024)),
            fixed((4, C, C)),
            fixed((plan.total, 2 * W)),
            fixed((W, W)),
            fixed((W, 128)),
            fixed(pick_all.shape),
            fixed(move_all.shape),
            fixed(move_lin.shape),
            fixed(zero_lanes.shape),
            ANYWHERE,
            ANYWHERE,
        ],
        out_specs=[
            ANYWHERE,
            plain_fields(plan)[1],
            ANYWHERE,
            fixed((plan.zrows, 2 * W)),
            fixed((C + 8, W)),
        ],
        out_shape=[
            jax.ShapeDtypeStruct(p_big.shape, BF),
            jax.ShapeDtypeStruct(p_small.shape, BF),
            jax.ShapeDtypeStruct((plan.chips, 2, plan.total, 2 * W), BF),
            jax.ShapeDtypeStruct((plan.zrows, 2 * W), BF),
            jax.ShapeDtypeStruct((C + 8, W), F32),
        ],
        scratch_shapes=[
            pltpu.VMEM((plan.chips, 2, plan.total, 2 * W), BF),
            pltpu.VMEM((W, W), BF),
            pltpu.VMEM((4, 2, acc, 128), F32),
            pltpu.VMEM((8, 2, acc, 128), F32),
            pltpu.VMEM((plan.own, C, 256), F32),
            pltpu.VMEM((plan.nz, plan.zrows, 2 * W), BF),
            pltpu.VMEM((plan.nz, plan.zrows, 2 * W), BF),
            pltpu.VMEM((stages, C + 8, W), F32),
            pltpu.VMEM((stages, C + 8, W), F32),
            dma((2,)),
            dma((plan.nz,)),
            dma((plan.nz,)),
            dma((stages,)),
            dma((stages,)),
            *Stream.scratch(min(4, plan.steps), 2 * plan.per, big.cells),
            *Stream.scratch(min(4, plan.steps), 2 * plan.per, big.cells),
            *Stream.scratch(min(3, plan.steps), 2 * plan.per, big.cells),
            *Exchange.scratch(plan),
        ],
        compiler_params=params(collective_id=2, has_side_effects=True),
        name="mode_backward",
    )(p_big, p_small, g_big, g_small, expand_tables(), lin_weight, spectrum, lin_grad, columns,
      pick_all, move_all, move_lin, zero_lanes, part, kernel_all)


def input_grads(plan, rank, part_big, part_small, modes, lin_sum):
    big, small = plan.big, plan.small
    per, steps = plan.wide_per, plan.wide_steps
    last = steps - 1

    split = np.zeros((W, 4, 128), np.float32)
    for p in range(4):
        split[p * C : p * C + C, p, :C] = np.eye(C)
    split = split.reshape(W, 512)

    def body(r, pb, ps, mb, ms, vb, eb, vs, es, lin, cut, db, ds, lin_out, bias_out):
        i = pl.program_id(0)

        @pl.when(i == 0)
        def _():
            v = lax.dot_general(
                lin[...], cut[...], (((1,), (0,)), ((), ())),
                precision=lax.Precision.HIGHEST, preferred_element_type=F32,
            )
            for p in range(4):
                lin_out[p] = v[:C, 128 * p : 128 * p + C]
                bias_out[p : p + 1, :] = v[C : C + 1, 128 * p : 128 * p + C]

        def run(part, m, d, geo, inverse, spread, count):
            span = spread.shape[1]
            qs = []
            for pair in range(count):
                qs += inverse_pair(geo, load_modes(plan, m, pair), inverse[...], 1.0)
            q = jnp.concatenate(qs, axis=0) * jnp.asarray(1.0 / geo.side, BF)
            for j in range(geo.cells // span):
                v = dot(q[:, 128 * j : 128 * j + 128], spread[...])
                at = (slice(0, 2 * count), slice(None), slice(None),
                      slice(j * span, (j + 1) * span))
                d[at] = part[at].astype(F32) + v.reshape(2 * count, 4, C, span)

        @pl.when(i < steps)
        def _():
            run(pb, mb, db, big, vb, eb, per)

        @pl.when(i == steps)
        def _():
            run(ps, ms, ds, small, vs, es, plan.nsmall // 2)

    tables = []
    specs = []
    for geo in (big, small):
        tables += [geo.inverse, geo.spread]
        specs += [device_spec(geo.inverse.shape[1:]), const_spec(geo.spread.shape)]
    small_field = field_specs(plan)[1]
    big_field = pl.BlockSpec((2 * per, 4, C, big.cells), lambda i, r: (wide(i, last), 0, 0, 0))
    return pl.pallas_call(
        body,
        grid_spec=pltpu.PrefetchScalarGridSpec(
            num_scalar_prefetch=1,
            grid=(steps + 1,),
            in_specs=[
                big_field,
                small_field,
                pl.BlockSpec((plan.n, per * plan.own, 2 * W), lambda i, r: (0, wide(i, last), 0)),
                pl.BlockSpec((plan.n, plan.block, 2 * W), lambda i, r: (0, plan.steps, 0)),
                *specs,
                const_spec(lin_sum.shape),
                const_spec(split.shape),
            ],
            out_specs=[big_field, small_field, const_spec((4, C, C)), const_spec((4, C))],
        ),
        out_shape=[
            jax.ShapeDtypeStruct(part_big.shape, F32),
            jax.ShapeDtypeStruct(part_small.shape, F32),
            jax.ShapeDtypeStruct((4, C, C), F32),
            jax.ShapeDtypeStruct((4, C), F32),
        ],
        compiler_params=params(),
        name="input_grads",
    )(rank, part_big, part_small, modes, modes, *tables, lin_sum, split)


def collect(plan, here, pieces):
    pick = np.zeros((2, 2 * W, 4, 128), np.float32)
    for odd in range(2):
        for lane in range(W):
            at = lane + 128 * odd if lane < 128 else 128 + 64 * odd + lane
            pick[odd, at, lane // C, lane % C] = 1.0
    pick = low(pick.reshape(2, 2 * W, 512))

    def body(z, pick_ref, *refs):
        pieces, out, rows = refs[: plan.nz], refs[plan.nz], refs[plan.nz + 1]
        for d, piece in enumerate(pieces):
            at = lax.rem(z[0] + plan.nz - d, plan.nz) * plan.zrows
            rows[pl.ds(pl.multiple_of(at, 16), plan.zrows), :] = piece[...]
        for odd in range(2):
            v = dot(rows[: plan.wrows, :], pick_ref[odd])
            for j in range(plan.own // 2):
                for p in range(4):
                    out[2 * j + odd, p] = v[j * C : j * C + C, 128 * p : 128 * p + C]

    vmem = pl.BlockSpec(memory_space=pltpu.VMEM)
    return pl.pallas_call(
        body,
        in_specs=[pl.BlockSpec(memory_space=pltpu.SMEM)] + [vmem] * (1 + plan.nz),
        out_specs=vmem,
        out_shape=jax.ShapeDtypeStruct((plan.own, 4, C, C), F32),
        scratch_shapes=[pltpu.VMEM((plan.nz * plan.zrows, 2 * W), BF)],
        compiler_params=params(),
        name="collect",
    )(here, pick, *pieces)


def on_device(plan, x_big, x_small, spec_weight, lin_weight, lin_bias, grad_big, grad_small):
    rank = lax.axis_index("rows").reshape(1)
    here = lax.axis_index("samples").reshape(1)
    whole = (plan.n, plan.total, 2 * W)
    modes, kernel, spectrum = forward_kernel(plan, x_big, x_small, spec_weight)
    out_big, out_small, pre_big, pre_small, part, lin_grad, columns = cells_pass(
        plan, rank, x_big, x_small, grad_big, grad_small, modes.reshape(whole), lin_weight,
        lin_bias,
    )
    part_big, part_small, modes, weight_part, lin_sum = backward_kernel(
        plan, part.reshape(plan.chips, 2, -1, 2 * W), pre_big, pre_small,
        grad_big, grad_small, kernel, spectrum, lin_weight, lin_grad, columns,
    )
    pieces = [weight_part]
    for d in range(1, plan.nz):
        pairs = [(z, (z + d) % plan.nz) for z in range(plan.nz)]
        pieces.append(lax.ppermute(weight_part, "samples", pairs))
    dx_big, dx_small, lin_weight_grad, lin_bias_grad = input_grads(
        plan, rank, part_big, part_small, modes.reshape(whole), lin_sum
    )
    spec_grad = collect(plan, here, pieces)
    return out_big, out_small, dx_big, dx_small, spec_grad, lin_weight_grad, lin_bias_grad


def solution(mesh):
    fields = P("samples", None, None, "rows")
    spec = P("rows", None, None, None)

    def run(x_big, x_small, *rest):
        count = mesh.shape["samples"]
        plan = Plan(mesh, x_big.shape[0] // count, x_small.shape[0] // count)

        def local(*args):
            return on_device(plan, *args)

        return jax.shard_map(
            local,
            mesh=mesh,
            in_specs=(fields, fields, spec, P(), P(), fields, fields),
            out_specs=(fields, fields, fields, fields, spec, P(), P()),
            check_vma=False,
        )(x_big, x_small, *rest)

    return run
```

```python
import math

import jax
import jax.numpy as jnp
import ml_dtypes
import numpy as np
from jax import lax
from jax.experimental import pallas as pl
from jax.experimental.pallas import tpu as pltpu
from jax.sharding import PartitionSpec as P

C = 48
MX = 16
N1 = 128
N2 = 64
W = 4 * C
MODES = MX * MX
BF = jnp.bfloat16
F32 = jnp.float32


def trig(side):
    a = np.arange(MX)
    freq = np.where(a < MX // 2, a, side - MX + a)
    phase = (np.arange(side)[:, None] * freq[None, :]) % side
    angle = phase.astype(np.float32) * np.float32(2.0 * math.pi / side)
    cos = np.cos(angle).astype(ml_dtypes.bfloat16).astype(np.float32)
    sin = np.sin(angle).astype(ml_dtypes.bfloat16).astype(np.float32)
    return cos, sin


def low(table):
    return table.astype(ml_dtypes.bfloat16)


class Geometry:
    def __init__(self, side, n):
        self.side = side
        self.rows = side // n
        self.cells = self.rows * side
        self.group = min(8, self.rows)
        self.ngroups = self.rows // self.group
        self.npairs = self.rows // 2
        self.qlanes = max(128, self.npairs * 64)
        self.hk = self.ngroups * 128
        cos, sin = trig(side)
        eye = np.eye(MX, dtype=np.float32)

        first = np.zeros((self.group, side, 256), np.float32)
        for h in range(self.group):
            first[h, :, h * MX : (h + 1) * MX] = cos
            first[h, :, 128 + h * MX : 128 + (h + 1) * MX] = sin
        self.first = low(first.reshape(self.group * side, 256))

        second = np.zeros((n, MX, MX, 2, self.ngroups, 128), np.float32)
        inverse = np.zeros((n, MX, MX, 2, self.qlanes), np.float32)
        for r in range(n):
            for h in range(self.rows):
                c, s = cos[r * self.rows + h], sin[r * self.rows + h]
                ce, se = c[:, None, None] * eye, s[:, None, None] * eye
                g, lane = h // self.group, (h % self.group) * MX
                second[r, :, :, 0, g, lane : lane + MX] = ce
                second[r, :, :, 1, g, lane : lane + MX] = se
                lane = h * 2 * MX
                inverse[r, :, :, 0, lane : lane + MX] = ce
                inverse[r, :, :, 0, lane + MX : lane + 2 * MX] = -se
                inverse[r, :, :, 1, lane : lane + MX] = -se
                inverse[r, :, :, 1, lane + MX : lane + 2 * MX] = -ce
        self.second = low(second.reshape(n, MODES, 2 * self.hk))
        inverse[..., MX : self.rows * 2 * MX : 2 * MX] = 0.0
        self.inverse = low(inverse.reshape(n, MODES, 2 * self.qlanes))

        spread = np.zeros((4, 2, MX, 4, side), np.float32)
        for h in range(4):
            spread[h, 0, :, h] = cos.T
            spread[h, 1, :, h] = sin.T
        self.spread = low(spread.reshape(128, 4 * side))
        if self.npairs == 1:
            self.spread = self.spread[:, : 2 * side]
        for h in range(4):
            spread[h, 1, 0, h] = 1.0
        self.pair_spread = low(spread.reshape(128, 4 * side))[:64, : 2 * side]


def turn(v):
    return jnp.concatenate([v[3 * C :], v[2 * C : 3 * C], -v[C : 2 * C], -v[:C]], axis=0)


def dot(a, b, dims=((1,), (0,))):
    return lax.dot_general(a, b, (dims, ((), ())), preferred_element_type=F32)


def forward_group(field, first, scale, keep=None):
    y = dot(field, first)
    grids = range(y.shape[0] // W)
    if keep is not None:
        keep(sum(y[W * s : W * s + W, :128] for s in grids))
    cols = []
    for s in grids:
        col = y[W * s : W * s + W, :128] + turn(y[W * s : W * s + W, 128:])
        cols.append((col * scale).astype(BF))
    return cols


def forward_rows(groups, second):
    stacked = []
    for s in range(2):
        cols = [cols[s] for cols in groups]
        stacked.append(jnp.concatenate(cols + [turn(col) for col in cols], axis=1))
    a, b = stacked
    both = jnp.concatenate([a[:128], b[:128], a[128:], b[128:]], axis=0)
    return dot(second, both, ((1,), (1,)))


def forward_grids(geo, get, first, second, scale):
    width = geo.group * geo.side
    groups = [forward_group(get(g * width, width), first, scale) for g in range(geo.ngroups)]
    return [
        forward_rows([cols[2 * k : 2 * k + 2] for cols in groups], second)
        for k in range(len(groups[0]) // 2)
    ]


def inverse_pair(geo, modes, inverse, scale):
    uv = dot(modes, inverse, ((0,), (0,)))
    result = []
    for s in range(2):
        part = jnp.concatenate(
            [uv[128 * s : 128 * s + 128], uv[256 + 64 * s : 320 + 64 * s]], axis=0
        )
        q = part[:, : geo.qlanes] + turn(part[:, geo.qlanes :])
        result.append((q * scale).astype(BF))
    return result


def fold_tables():
    dup = np.concatenate([np.arange(192), np.arange(128, 192)])
    pick = np.zeros((192, 4, 128), np.float32)
    move = np.zeros((192, 4, 192), np.float32)
    for q in range(4):
        pick[q * C : q * C + C, q, :C] = np.eye(C)
        for p in range(4):
            sign = -1.0 if (p >> 1) & q & 1 else 1.0
            o = p ^ q
            move[o * C : o * C + C, q, p * C : p * C + C] = sign * np.eye(C)
    return (
        low(pick[dup].reshape(256, 512)),
        low(move[dup][:, :, dup].reshape(256, 1024)),
        move.transpose(1, 0, 2).copy(),
    )


def expand_tables():
    dup = np.concatenate([np.arange(192), np.arange(128, 192)])
    place = np.zeros((4, C, 4, 256), np.float32)
    for p in range(4):
        for q in range(4):
            sign = -1.0 if (p >> 1) & q & 1 else 1.0
            full = np.zeros((C, 192), np.float32)
            o = p ^ q
            full[:, o * C : (o + 1) * C] = sign * np.eye(C)
            place[p, :, q] = full[:, dup]
    return low(place.reshape(W, 1024))


class Layout:
    def __init__(self, chunks, pairs, modes, by_mode):
        self.chunks, self.pairs, self.modes, self.by_mode = chunks, pairs, modes, by_mode
        self.crow = pairs * modes
        first = -(-self.crow // 32) * 16
        self.halves = (first, self.crow - first)
        self.slots = -(-pairs // 8) * 8
        self.acc_rows = self.slots * modes
        self.total = chunks * self.crow

    def first_mode(self, c):
        return c * self.modes if self.by_mode else 0


class Plan:
    def __init__(self, mesh, nbig, nsmall):
        self.n = mesh.shape["rows"]
        self.nz = mesh.shape["samples"]
        self.own = MODES // self.n
        self.per = max(1, 16 // self.own)
        self.big = Geometry(N1, self.n)
        self.small = Geometry(N2, self.n)
        self.nbig, self.nsmall = nbig, nsmall
        assert nbig % (2 * self.per) == 0 and nsmall % 2 == 0 and nsmall // 2 <= self.per
        self.steps = nbig // (2 * self.per)
        self.count = self.steps + 1
        self.wide_per = 2 * self.per if self.steps % 2 == 0 else self.per
        self.wide_steps = nbig // (2 * self.wide_per)
        self.block = self.per * self.own
        self.total = self.count * self.block
        pairs = self.count * self.per
        parts = next(c for c in (3, 2, 1) if self.count % c == 0)
        self.by_pairs = Layout(parts, pairs // parts, self.own, False)
        parts = max(1, self.own // 16)
        self.by_modes = Layout(parts, pairs, self.own // parts, True)
        self.chips = self.n // 2
        bits = list(range(1, self.n.bit_length() - 1))
        self.orders = (bits, bits[::-1])
        self.levels = len(bits)
        self.wrows = self.by_modes.modes // 2 * C
        self.pieces = 2
        self.zrows = self.wrows // self.pieces
        assert self.nz % 2 == 0 and self.zrows % 16 == 0

    def mask(self, h, idx):
        m = 0
        for t, b in enumerate(self.orders[h]):
            if idx >> (self.levels - 1 - t) & 1:
                m |= 1 << b
        return m


def wide(i, last):
    return jnp.minimum(i, last)


def params(**kw):
    return pltpu.CompilerParams(vmem_limit_bytes=56 * 1024 * 1024, **kw)


def const_spec(shape):
    return pl.BlockSpec(shape, lambda i, r: (0,) * len(shape))


def device_spec(shape):
    return pl.BlockSpec((None,) + shape, lambda i, r: (r[0],) + (0,) * len(shape))


def field_specs(plan):
    big, small = plan.big, plan.small
    last = plan.steps - 1
    return (
        pl.BlockSpec((2 * plan.per, 4, C, big.cells), lambda i, r: (wide(i, last), 0, 0, 0)),
        pl.BlockSpec((plan.nsmall, 4, C, small.cells), lambda i, r: (0, 0, 0, 0)),
    )


def mode_spec(plan):
    return pl.BlockSpec((plan.n, plan.block, 2 * W), lambda i, r: (0, i, 0))


def store_by_modes(plan, ref, pair, z):
    lay = plan.by_modes
    z = z.reshape(plan.n, lay.chunks, lay.modes, 2 * W).astype(BF)
    ref[:, :, pair * lay.modes : (pair + 1) * lay.modes, :] = z


def load_by_modes(plan, ref, pair):
    lay = plan.by_modes
    return ref[:, :, pair * lay.modes : (pair + 1) * lay.modes, :].reshape(MODES, 2 * W)


def load_modes(plan, ref, pair):
    return ref[:, pair * plan.own : (pair + 1) * plan.own, :].reshape(MODES, 2 * W)


def flip(index, mask):
    result = index
    for b in range(mask.bit_length()):
        if mask >> b & 1:
            bit = lax.rem(lax.div(index, 1 << b), 2)
            result = result + (1 - 2 * bit) * (1 << b)
    return result


def tiles(v):
    return [v[:, 128 * t : 128 * t + 128] for t in range(v.shape[1] // 128)]


def sample_rows(first, second, third):
    lane = lax.broadcasted_iota(jnp.int32, third.shape, 1)
    a = jnp.concatenate([first, jnp.where(lane < 64, third, 0.0)], axis=1)
    b = jnp.concatenate([second, jnp.where(lane < 64, 0.0, third)], axis=1)
    return jnp.concatenate([a, b], axis=0)


def pair_tiles(a, b):
    lane = lax.broadcasted_iota(jnp.int32, (a.shape[0], 128), 1)
    return a[:, :128], b[:, :128], jnp.where(lane < 64, a[:, 128:], b[:, 128:])


def remote(src, dst, send, recv, device):
    return pltpu.make_async_remote_copy(
        src_ref=src, dst_ref=dst, send_sem=send, recv_sem=recv, device_id=device
    )


class Stream:
    def __init__(self, field, ring, sems, grids):
        self.field, self.ring, self.sems, self.grids = field, ring, sems, grids
        self.depth = ring.shape[0]

    @staticmethod
    def scratch(depth, grids, cells):
        return [pltpu.VMEM((depth, grids, 4, C, cells), BF), pltpu.SemaphoreType.DMA((depth,))]

    def slot(self, i):
        return self.ring.at[lax.rem(i, self.depth)]

    def copy(self, i, out=False):
        block = self.field.at[pl.ds(i * self.grids, self.grids)]
        sem = self.sems.at[lax.rem(i, self.depth)]
        if out:
            return pltpu.make_async_copy(self.slot(i), block, sem)
        return pltpu.make_async_copy(block, self.slot(i), sem)

    def read(self, i, count):
        @pl.when(i == 0)
        def _():
            for k in range(min(self.depth, count)):
                self.copy(jnp.int32(k)).start()

        self.copy(i).wait()
        return self.slot(i)

    def ahead(self, i, count):
        @pl.when(i + self.depth < count)
        def _():
            self.copy(i + self.depth).start()

    def reserve(self, i):
        @pl.when(i >= self.depth)
        def _():
            self.copy(i - self.depth, True).wait()

        return self.slot(i)

    def flush(self, count):
        for k in range(max(0, count - self.depth), count):
            self.copy(jnp.int32(k), True).wait()


class Exchange:
    @staticmethod
    def scratch(plan, lay):
        chips, width = plan.chips, 2 * W
        dma = pltpu.SemaphoreType.DMA
        part = (lay.chunks, 2)
        moving = (2, chips, lay.chunks * lay.halves[0], width)
        return [
            pltpu.VMEM((chips, lay.total, width), BF),
            pltpu.VMEM(moving, BF),
            pltpu.VMEM(moving, BF),
            pltpu.VMEM((chips, 2, lay.total, width), BF),
            pltpu.VMEM((3, lay.acc_rows, 128), F32),
            pltpu.VMEM((3, lay.acc_rows, 128), F32),
            dma((lay.chunks,)),
            dma((lay.chunks,)),
            dma(part + (plan.levels,)),
            dma(part + (plan.levels,)),
            dma(part + (chips,)),
            dma(part + (chips,)),
            dma(part + (chips,)),
            dma(part + (chips,)),
            dma((lay.chunks,)),
            pltpu.VMEM((plan.own, 256, 256), BF),
        ]

    def __init__(self, plan, lay, part, out, refs, origin):
        self.plan, self.lay, self.part, self.out, self.origin = plan, lay, part, out, origin
        (self.sib, self.sums, self.lev, self.res, self.acc, self.mixed,
         self.sib_s, self.sib_r, self.lev_s, self.lev_r, self.ag_s, self.ag_r,
         self.fw_s, self.fw_r, self.out_s, self.kernel) = refs
        self.me = lax.axis_index("rows")
        self.core = lax.rem(self.me, 2)

    def partners(self):
        return [flip(self.me, 1 << b) for b in range(self.plan.n.bit_length() - 1)]

    def chunk(self, c):
        return pl.ds(c * self.lay.crow, self.lay.crow)

    def rows(self, c, h):
        return pl.ds(c * self.lay.crow + h * self.lay.halves[0], self.lay.halves[h])

    def moving(self, c, h):
        return pl.ds(c * self.lay.halves[0], self.lay.halves[h])

    def to_sibling(self, c):
        return remote(
            self.origin(c, 1 - self.core), self.sib.at[:, self.chunk(c), :],
            self.sib_s.at[c], self.sib_r.at[c], {"rows": flip(self.me, 1)},
        )

    def level(self, c, h, t):
        plan = self.plan
        count = plan.chips >> (t + 1)
        rows = self.moving(c, h)
        at = plan.chips - 2 * count
        return remote(
            self.sums.at[h, pl.ds(count, count), rows, :],
            self.lev.at[h, pl.ds(at, count), rows, :],
            self.lev_s.at[c, h, t], self.lev_r.at[c, h, t],
            {"rows": flip(self.me, 1 << plan.orders[h][t])},
        )

    def block(self, c, h, owner):
        return self.res.at[lax.div(owner, 2), lax.rem(owner, 2), self.rows(c, h), :]

    def gather(self, c, h, u, idx):
        plan = self.plan
        sem = (1 << u) - 1 + idx
        ref = self.block(c, h, flip(self.me, plan.mask(h, idx)))
        return remote(
            ref, ref, self.ag_s.at[c, h, sem], self.ag_r.at[c, h, sem],
            {"rows": flip(self.me, 1 << plan.orders[h][plan.levels - 1 - u])},
        )

    def forward(self, c, h, idx):
        ref = self.block(c, h, flip(self.me, self.plan.mask(h, idx)))
        return remote(
            ref, ref, self.fw_s.at[c, h, idx], self.fw_r.at[c, h, idx],
            {"rows": flip(self.me, 1)},
        )

    def store(self, c):
        rows = self.chunk(c)
        return pltpu.make_async_copy(
            self.res.at[:, :, rows, :], self.out.at[:, :, rows, :], self.out_s.at[c]
        )

    def begin(self, c):
        self.to_sibling(c).start()

    def add_sibling(self, c):
        plan = self.plan
        self.to_sibling(c).wait_recv()
        for far in (1, 0):
            for h in range(2):
                span = plan.chips // 2
                for idx in range(far * span, far * span + span):
                    owner = flip(self.me, plan.mask(h, idx))
                    chip = lax.div(owner, 2)
                    rows = self.rows(c, h)
                    v = self.part[chip, self.core, rows, :].astype(F32)
                    v = v + self.sib[chip, rows, :].astype(F32)
                    self.sums[h, idx, self.moving(c, h), :] = v.astype(BF)
                if far:
                    self.level(c, h, 0).start()

    def next_level(self, c, t):
        plan = self.plan
        count = plan.chips >> t
        at = plan.chips - 2 * count
        for h in range(2):
            rows = self.moving(c, h)
            self.level(c, h, t - 1).wait_recv()
            for idx in reversed(range(count)):
                v = self.sums[h, idx, rows, :].astype(F32)
                v = v + self.lev[h, at + idx, rows, :].astype(F32)
                self.sums[h, idx, rows, :] = v.astype(BF)
                if idx == count // 2:
                    self.level(c, h, t).start()

    def finish_sum(self, c, scale):
        plan, lay = self.plan, self.lay
        for h in range(2):
            rows = self.moving(c, h)
            self.level(c, h, plan.levels - 1).wait_recv()
            v = self.sums[h, 0, rows, :].astype(F32)
            v = (v + self.lev[h, plan.chips - 2, rows, :].astype(F32)) * scale
            at = h * lay.halves[0]
            for t, tile in enumerate(tiles(v)):
                self.acc[t, at : at + lay.halves[h], :] = tile

    def mix(self, c, dims):
        lay = self.lay

        def one(m):
            rows = pl.ds(m, lay.slots, stride=lay.modes)
            lhs = sample_rows(*(self.acc[t, rows, :] for t in range(3))).astype(BF)
            res = dot(lhs, self.kernel[lay.first_mode(c) + m], dims)
            for t, tile in enumerate(pair_tiles(res[: lay.slots], res[lay.slots :])):
                self.mixed[t, rows, :] = tile

        unroll = 8

        @pl.loop(0, lay.modes // unroll)
        def _(j):
            for u in range(unroll):
                one(j * unroll + u)

        result = jnp.concatenate([self.mixed[t, : lay.crow, :] for t in range(3)], axis=1)
        self.res[lax.div(self.me, 2), self.core, self.chunk(c), :] = result.astype(BF)
        for h in range(2):
            self.gather(c, h, 0, 0).start()
            self.forward(c, h, 0).start()

    def spread(self, c, u):
        for h in range(2):
            got = 1 << (u - 1)
            for idx in range(got):
                self.gather(c, h, u - 1, idx).wait_recv()
            if u < self.plan.levels:
                for idx in reversed(range(2 * got)):
                    self.gather(c, h, u, idx).start()
            for idx in range(got, 2 * got):
                self.forward(c, h, idx).start()

    def close(self, c):
        for h in range(2):
            for idx in range(self.plan.chips):
                self.forward(c, h, idx).wait_recv()
        self.store(c).start()

    def drain(self):
        plan = self.plan
        for c in range(self.lay.chunks):
            self.to_sibling(c).wait_send()
            for h in range(2):
                for t in range(plan.levels):
                    self.level(c, h, t).wait_send()
                for u in range(plan.levels):
                    for idx in range(1 << u):
                        self.gather(c, h, u, idx).wait_send()
                for idx in range(plan.chips):
                    self.forward(c, h, idx).wait_send()
            self.store(c).wait()

    def clear(self):
        lay = self.lay
        if lay.acc_rows > lay.crow:
            self.acc[:, lay.crow :, :] = jnp.zeros((3, lay.acc_rows - lay.crow, 128), F32)

    def waves(self, total):
        plan, chunks = self.plan, self.lay.chunks
        todo = []
        for c in range(chunks):
            chain = [lambda c=c, t=t: self.next_level(c, t) for t in range(1, plan.levels)]
            chain += [lambda c=c: total(c)]
            chain += [lambda c=c, u=u: self.spread(c, u) for u in range(1, plan.levels + 1)]
            chain += [lambda c=c: self.close(c)]
            todo.append(chain)
        waves = []
        for w in range(len(todo[0]) + chunks - 1):
            at = [(c, w - c) for c in reversed(range(chunks))]
            waves.append([todo[c][k] for c, k in at if 0 <= k < len(todo[c])])
        return waves


def greet(devices):
    barrier = pltpu.get_barrier_semaphore()
    for device in devices:
        pl.semaphore_signal(barrier, inc=1, device_id=device)
    pl.semaphore_wait(barrier, len(devices))


def build_modes(plan, place, weights, kernel):
    flat = jnp.concatenate([weights[:, p].reshape(-1, C) for p in range(4)], axis=1)
    for q in range(4):
        rows = dot(flat, place[:, 256 * q : 256 * q + 256])
        kernel[:, C * q : C * q + C, :] = rows.astype(BF).reshape(plan.own, C, 256)
    kernel[:, W:, :] = kernel[:, 128:W, :]


def build_lin(place, weight):
    flat = jnp.concatenate([weight[p] for p in range(4)], axis=1)
    rows = [dot(flat, place[:, 256 * q : 256 * q + 256]) for q in range(4)]
    return jnp.concatenate(rows, axis=0).astype(BF)


def half_tables():
    rows = np.zeros((192, 384), np.float32)
    rows[:128, :128] = 0.5 * np.eye(128)
    rows[128:, 192:256] = 0.5 * np.eye(64)
    rows[128:, 256:320] = 0.5 * np.eye(64)
    line = np.zeros((128, C), np.float32)
    line[MX :: 2 * MX] = 0.5
    return low(rows), low(line), low(np.eye(C, dtype=np.float32))


def plain_fields(plan):
    big, small = plan.big, plan.small
    last = plan.steps - 1
    return [
        pl.BlockSpec((2 * plan.per, 4, C, big.cells), lambda i: (wide(i, last), 0, 0, 0)),
        pl.BlockSpec((plan.nsmall, 4, C, small.cells), lambda i: (0, 0, 0, 0)),
    ]


def fixed(shape):
    return pl.BlockSpec(shape, lambda i: (0,) * len(shape))


ANYWHERE = pl.BlockSpec(memory_space=pl.ANY)


def forward_kernel(plan, x_big, x_small, spec_weight):
    big, small = plan.big, plan.small
    lay = plan.by_pairs
    last = plan.wide_steps

    def kernel(x_hbm, xs, fb, fs, place, weights, sb_all, ss_all, out, kernel_out, spectrum,
               part, sb, ss, table_sem, ring, ring_sem, *refs):
        i = pl.program_id(0)
        stream = Stream(x_hbm, ring, ring_sem, 2 * plan.wide_per)
        ex = Exchange(plan, lay, part, out, refs, lambda c, core: part.at[
            :, core, pl.ds(c * lay.crow, lay.crow), :
        ])
        loads = [
            pltpu.make_async_copy(sb_all.at[ex.me], sb, table_sem.at[0]),
            pltpu.make_async_copy(ss_all.at[ex.me], ss, table_sem.at[1]),
        ]
        keep = pltpu.make_async_copy(ex.kernel, kernel_out, table_sem.at[2])

        @pl.when(i == 0)
        def _():
            for load in loads:
                load.start()
            greet([{"rows": d} for d in ex.partners()])
            ex.clear()
            for load in loads:
                load.wait()

        def run(x, geo, first, second, count, per):
            def get(start, width):
                v = x[: 2 * count, :, :, start : start + width]
                return v.reshape(2 * count * W, width)

            zs = forward_grids(geo, get, first[...], second[...], 1.0 / geo.side)
            parts = [z.reshape(plan.chips, 2, plan.own, 2 * W) for z in zs]
            parts += [jnp.zeros_like(parts[0])] * (per - count)
            z = jnp.concatenate(parts, axis=2) if per > 1 else parts[0]
            rows = pl.ds(pl.multiple_of(i * plan.wide_per * plan.own, 16), per * plan.own)
            part[:, :, rows, :] = z.astype(BF)

        @pl.when(i < last)
        def _():
            run(stream.read(i, last), big, fb, sb, plan.wide_per, plan.wide_per)
            stream.ahead(i, last)

        @pl.when(i == last)
        def _():
            run(xs, small, fs, ss, plan.nsmall // 2, plan.per)

        def total(c):
            ex.finish_sum(c, 1.0)
            spectrum[ex.chunk(c), :] = jnp.concatenate(
                [ex.acc[t, : lay.crow, :] for t in range(3)], axis=1
            ).astype(BF)
            ex.mix(c, ((1,), (0,)))

        def prepare():
            build_modes(plan, place, weights, ex.kernel)
            keep.start()

        waves = ex.waves(total)
        items = []
        for c in range(lay.chunks):
            pairs = (c + 1) * lay.pairs
            end = min(-(-pairs // plan.wide_per) - 1, last)
            items.append((end, lambda c=c: ex.begin(c)))
            if c == lay.chunks - 1:
                items.append((last, prepare))
                items += [(last, task) for task in waves.pop(0)]
            items.append((min(end + 1, last), lambda c=c: ex.add_sibling(c)))
        items += [(last, task) for wave in waves for task in wave]
        schedule(last, i, items)

        @pl.when(i == last)
        def _():
            ex.drain()
            keep.wait()

    return pl.pallas_call(
        kernel,
        grid=(last + 1,),
        in_specs=[
            ANYWHERE,
            plain_fields(plan)[1],
            fixed(big.first.shape),
            fixed(small.first.shape),
            fixed((W, 1024)),
            fixed(spec_weight.shape),
            ANYWHERE,
            ANYWHERE,
        ],
        out_specs=[ANYWHERE, ANYWHERE, fixed((plan.by_pairs.total, 2 * W))],
        out_shape=[
            jax.ShapeDtypeStruct((plan.chips, 2, plan.by_pairs.total, 2 * W), BF),
            jax.ShapeDtypeStruct((plan.own, 256, 256), BF),
            jax.ShapeDtypeStruct((plan.by_pairs.total, 2 * W), BF),
        ],
        scratch_shapes=[
            pltpu.VMEM((plan.chips, 2, plan.by_pairs.total, 2 * W), BF),
            pltpu.VMEM(big.second.shape[1:], BF),
            pltpu.VMEM(small.second.shape[1:], BF),
            pltpu.SemaphoreType.DMA((3,)),
            *Stream.scratch(min(4, last), 2 * plan.wide_per, big.cells),
            *Exchange.scratch(plan, plan.by_pairs),
        ],
        compiler_params=params(collective_id=1, has_side_effects=True),
        name="mode_forward",
    )(x_big, x_small, big.first, small.first, expand_tables(), spec_weight,
      big.second, small.second)


def schedule(last, i, items):
    for step in range(last + 1):
        now = [task for when, task in items if min(when, last) == step]
        if now:
            @pl.when(i == step)
            def _(now=now):
                for task in now:
                    task()


def cells_pass(plan, rank, x_big, x_small, g_big, g_small, modes, lin_weight,
               lin_bias):
    k0 = math.sqrt(2.0 / math.pi)
    k1 = k0 * 0.044715

    def low_of(value):
        return jnp.asarray(value, BF)

    per, steps = plan.wide_per, plan.wide_steps
    last = steps - 1

    def body(r, xb, xs, gb, gs, m, ms, fb, sb, vb, eb, fs, ss, vs, es,
             place, rows_table, line, eye, lw, lb, ob, os_, pb, ps, z, lin_acc, y_acc,
             kt, bias_ref):
        i = pl.program_id(0)

        @pl.when(i == 0)
        def _():
            full = build_lin(place[...], lw)[:, :W]
            kt[...] = dot(full, rows_table[...], ((0,), (0,))).astype(BF)
            for q in range(4):
                bias_ref[C * q : C * q + C, :] = dot(
                    eye[...], line[...] * lb[q : q + 1, :], ((1,), (1,))
                ).astype(BF)
            lin_acc[...] = jnp.zeros_like(lin_acc)
            y_acc[...] = jnp.zeros_like(y_acc)

        def run(x, g, o, d, m, z, geo, first, second, inverse, spread, count):
            wide_cells = 2 * geo.side
            lane = lax.broadcasted_iota(jnp.int32, (W, 128), 1)
            held, groups = {}, {}

            def rows_back(pair):
                qs = inverse_pair(geo, load_modes(plan, m, pair), inverse[...], 0.5 / MX)
                line = jnp.concatenate([bias_ref[...]] * (geo.qlanes // 128), axis=1)
                for s in range(2):
                    held[2 * pair + s] = qs[s] + line

            def main(at, p):
                lo = p * wide_cells
                cells = slice(lo, lo + wide_cells)
                q = held[at][:, 128 * (p // 2) : 128 * (p // 2) + 128]
                xv = x[at, :, :, cells].reshape(W, wide_cells)
                if p % 2 == 0:
                    tail = jnp.where(lane < 64, q, kt[:, 128:256])
                    rhs = [xv[:128], spread[...], xv[128:]]
                else:
                    tail = jnp.where(lane >= 64, q, kt[:, 256:384])
                    rhs = [xv[:128], xv[128:], spread[...]]
                lhs = jnp.concatenate([kt[:, :128], tail], axis=1)
                b = dot(lhs, jnp.concatenate(rhs, axis=0))
                b = b.astype(BF)
                b2 = b * b
                e = low_of(1.0) + jnp.tanh(b * (low_of(2.0 * k0) + low_of(8.0 * k1) * b2))
                o[at, :, :, cells] = (xv + b * e).reshape(4, C, wide_cells)
                rise = b * (low_of(k0) + low_of(12.0 * k1) * b2)
                slope = e * (low_of(0.5) + rise * (low_of(2.0) - e))
                gv = g[at, :, :, cells].reshape(W, wide_cells)
                d[at, :, :, cells] = (gv * slope).reshape(4, C, wide_cells)

            def weight_grad(at, part):
                span = geo.cells // 2
                xa = x[at, :, :, part * span : part * span + span].reshape(W, span)
                pa = d[at, :, :, part * span : part * span + span].reshape(W, span)
                lin_acc[...] += dot(xa, pa, ((1,), (1,)))

            def keep(y):
                y_acc[...] += y

            def columns(pair, k):
                width = geo.group * geo.side
                v = d[2 * pair : 2 * pair + 2, :, :, k * width : k * width + width]
                cols = forward_group(v.reshape(2 * W, width), first[...], 1.0, keep)
                groups.setdefault(pair, []).append(cols)

            def rows_out(pair):
                store_by_modes(plan, z, pair, forward_rows(groups[pair], second[...]))

            side = []
            rows_back(0)
            for at in range(2 * count):
                pair = at // 2
                if at % 2 == 0 and pair + 1 < count:
                    side.append(lambda pair=pair: rows_back(pair + 1))
                for p in range(geo.npairs):
                    main(at, p)
                    if side:
                        side.pop(0)()
                side += [lambda at=at, k=k: weight_grad(at, k) for k in range(2)]
                if at % 2 == 1:
                    side += [lambda pair=pair, k=k: columns(pair, k) for k in range(geo.ngroups)]
                    side.append(lambda pair=pair: rows_out(pair))
            for task in side:
                task()

        @pl.when(i < steps)
        def _():
            run(xb, gb, ob, pb, m, z, plan.big, fb, sb, vb, eb, per)

        @pl.when(i == steps)
        def _():
            if plan.nsmall // 2 < per:
                z[...] = jnp.zeros_like(z)
            run(xs, gs, os_, ps, ms, z, plan.small, fs, ss, vs, es, plan.nsmall // 2)

    big, small = plan.big, plan.small
    tables = []
    specs = []
    for geo in (big, small):
        tables += [geo.first, geo.second, geo.inverse, geo.pair_spread]
        specs += [
            const_spec(geo.first.shape),
            device_spec(geo.second.shape[1:]),
            device_spec(geo.inverse.shape[1:]),
            const_spec(geo.pair_spread.shape),
        ]
    extra = [expand_tables(), *half_tables(), lin_weight, lin_bias]
    small_field = field_specs(plan)[1]
    big_field = pl.BlockSpec((2 * per, 4, C, big.cells), lambda i, r: (wide(i, last), 0, 0, 0))
    rows = per * plan.own
    lay = plan.by_modes
    return pl.pallas_call(
        body,
        grid_spec=pltpu.PrefetchScalarGridSpec(
            num_scalar_prefetch=1,
            grid=(steps + 1,),
            in_specs=[
                big_field,
                small_field,
                big_field,
                small_field,
                pl.BlockSpec((plan.n, rows, 2 * W), lambda i, r: (0, wide(i, last), 0)),
                pl.BlockSpec((plan.n, plan.block, 2 * W), lambda i, r: (0, plan.steps, 0)),
                *specs,
                *[const_spec(v.shape) for v in extra],
            ],
            out_specs=[
                big_field,
                small_field,
                big_field,
                small_field,
                pl.BlockSpec(
                    (plan.n, lay.chunks, per * lay.modes, 2 * W), lambda i, r: (0, 0, i, 0)
                ),
                const_spec((W, W)),
                const_spec((W, 128)),
            ],
            scratch_shapes=[pltpu.VMEM((W, 2 * W), BF), pltpu.VMEM((W, 128), BF)],
        ),
        out_shape=[
            jax.ShapeDtypeStruct(x_big.shape, BF),
            jax.ShapeDtypeStruct(x_small.shape, BF),
            jax.ShapeDtypeStruct(x_big.shape, BF),
            jax.ShapeDtypeStruct(x_small.shape, BF),
            jax.ShapeDtypeStruct(
                (plan.n, lay.chunks, (steps + 1) * per * lay.modes, 2 * W), BF
            ),
            jax.ShapeDtypeStruct((W, W), F32),
            jax.ShapeDtypeStruct((W, 128), F32),
        ],
        compiler_params=params(),
        name="cells",
    )(rank, x_big, x_small, g_big, g_small, modes, modes, *tables, *extra)


def backward_kernel(plan, part, p_big, p_small, g_big, g_small, kernel_all, spectrum,
                    lin_weight, lin_grad, columns):
    big, small = plan.big, plan.small
    lay = plan.by_modes
    stages = plan.n.bit_length() - 1 + plan.nz.bit_length() - 1
    z_bits = plan.nz.bit_length() - 1
    pick_all, move_all, move_lin = fold_tables()
    zero_lanes = np.zeros((8, 128), np.float32)
    zero_lanes[0, ::MX] = 1.0

    def kernel(pb, ps, gb, gs, place, lw, spec, lin_in, col_in, pick, move, shift, line, part_in, kernel_in,
               db, ds, out, weight_out, lin_out,
               part, kk, sa, mb, w_rows, w_part, w_sum, w_recv, w_cross, w_full, lin_buf, lin_recv,
               in_sem, zs, zr, zc, zos, zor, ls, lr, p_ring, p_sem, g_ring, g_sem, d_ring, d_sem, *refs):
        i = pl.program_id(0)
        p_stream = Stream(pb, p_ring, p_sem, 2 * plan.per)
        g_stream = Stream(gb, g_ring, g_sem, 2 * plan.per)
        d_stream = Stream(db, d_ring, d_sem, 2 * plan.per)
        ex = Exchange(plan, lay, part, out, refs, lambda c, core: part_in.at[
            :, core, c, pl.ds(0, lay.crow), :
        ])
        here = lax.axis_index("samples")
        loads = [
            pltpu.make_async_copy(
                part_in.at[:, :, c, pl.ds(0, lay.crow), :], part.at[:, :, ex.chunk(c), :],
                in_sem.at[1 + c],
            )
            for c in range(lay.chunks)
        ]
        load_kernel = pltpu.make_async_copy(kernel_in, ex.kernel, in_sem.at[0])

        left = here < plan.nz // 2
        place_z = jnp.where(left, here, plan.nz - 1 - here)
        at_end = place_z == 0
        at_middle = place_z == plan.nz // 2 - 1
        inward = {"samples": jnp.where(left, here + 1, here - 1)}
        outward = {"samples": jnp.where(left, here - 1, here + 1)}

        def to_inner(p):
            return remote(w_sum.at[p], w_recv.at[p], zs.at[p], zr.at[p], inward)

        def across(p):
            return remote(w_sum.at[p], w_cross.at[p], zs.at[p], zc.at[p], inward)

        def to_outer(p):
            return remote(w_full.at[p], w_full.at[p], zos.at[p], zor.at[p], outward)

        def send_inward(p):
            @pl.when(at_middle)
            def _():
                across(p).start()

            @pl.when(jnp.logical_not(at_middle))
            def _():
                to_inner(p).start()

        def lin_partner(k):
            if k < z_bits:
                return {"samples": flip(here, 1 << k)}
            return {"rows": flip(ex.me, 1 << (k - z_bits))}

        def lin_step(k):
            return remote(lin_buf.at[k], lin_recv.at[k], ls.at[k], lr.at[k], lin_partner(k))

        @pl.when(i == 0)
        def _():
            for load in loads:
                load.start()
            load_kernel.start()
            greet([{"rows": d} for d in ex.partners()]
                  + [{"samples": lax.rem(here + d, plan.nz)} for d in range(1, plan.nz)])
            for c in range(lay.chunks):
                ex.begin(c)
            folded = None
            for q in range(4):
                term = lax.dot_general(
                    lin_in[C * q : C * q + C, :], shift[q], (((1,), (0,)), ((), ())),
                    precision=lax.Precision.HIGHEST, preferred_element_type=F32,
                )
                folded = term if folded is None else folded + term
            lin_buf[0, :C, :] = folded
            lin_buf[0, C:, :] = lax.dot_general(
                line[...], col_in[...], (((1,), (1,)), ((), ())),
                precision=lax.Precision.HIGHEST, preferred_element_type=F32,
            )
            lin_step(0).start()
            kk[...] = build_lin(place[...], lw)[:, :W]
            for c, load in enumerate(loads):
                load.wait()
                ex.add_sibling(c)
            ex.clear()
            if lay.acc_rows > lay.crow:
                rest = lay.acc_rows - lay.crow
                sa[:, :, lay.crow :, :] = jnp.zeros((4, 2, rest, 128), F32)
                mb[:, :, lay.crow :, :] = jnp.zeros((8, 2, rest, 128), F32)
            load_kernel.wait()

        def run(p, g, d, geo, count):
            for at in range(2 * count):
                v = dot(kk[...], p[at, :, :, :].reshape(W, geo.cells))
                v = g[at, :, :, :].reshape(W, geo.cells) + v.astype(BF)
                d[at, :, :, :] = v.reshape(4, C, geo.cells)

        @pl.when(i < plan.steps)
        def _():
            p = p_stream.read(i, plan.steps)
            g = g_stream.read(i, plan.steps)
            run(p, g, d_stream.reserve(i), big, plan.per)
            d_stream.copy(i, True).start()
            p_stream.ahead(i, plan.steps)
            g_stream.ahead(i, plan.steps)

        @pl.when(i == plan.steps)
        def _():
            run(ps, gs, ds, small, plan.nsmall // 2)

        def weight_grad(c):
            crow, modes = lay.crow, lay.modes
            grads = sample_rows(*(ex.acc[t, :crow, :] for t in range(3))).astype(BF)
            held = spec[:, lay.first_mode(c) : lay.first_mode(c) + modes, :]
            spectra = sample_rows(*tiles(held.reshape(crow, 2 * W).astype(F32))).astype(BF)
            for t, tile in enumerate(tiles(dot(spectra, pick[...]))):
                sa[t, 0, :crow, :] = tile[:crow]
                sa[t, 1, :crow, :] = tile[crow:]
            for t, tile in enumerate(tiles(dot(grads, move[...]))):
                mb[t, 0, :crow, :] = tile[:crow]
                mb[t, 1, :crow, :] = tile[crow:]

            def one(m):
                rows = pl.ds(m, lay.slots, stride=modes)
                left = [sa[q, s, rows, :] for q in range(4) for s in range(2)]
                right = [
                    jnp.concatenate([mb[2 * q, s, rows, :], mb[2 * q + 1, s, rows, :]], axis=1)
                    for q in range(4) for s in range(2)
                ]
                v = dot(
                    jnp.concatenate(left, axis=0).astype(BF),
                    jnp.concatenate(right, axis=0).astype(BF),
                    ((0,), (0,)),
                )
                return v[:C]

            unroll = 2

            @pl.loop(0, modes // (2 * unroll))
            def _(j):
                for u in range(unroll):
                    pair = j * unroll + u
                    v = pair_tiles(one(2 * pair), one(2 * pair + 1))
                    v = jnp.concatenate(v, axis=1).astype(BF)
                    w_rows[pl.ds(pl.multiple_of(pair * C, 16), C), :] = v

            for k in range(plan.pieces):
                p = c * plan.pieces + k
                w_part[p] = w_rows[k * plan.zrows : (k + 1) * plan.zrows, :]

                @pl.when(at_end)
                def _(p=p):
                    w_sum[p] = w_part[p]
                    send_inward(p)

        def sum_weights(c):
            for p in range(c * plan.pieces, (c + 1) * plan.pieces):
                @pl.when(jnp.logical_not(at_end))
                def _(p=p):
                    to_inner(p).wait_recv()
                    w_sum[p] = (w_part[p].astype(F32) + w_recv[p].astype(F32)).astype(BF)
                    send_inward(p)

        def cross_weights(c):
            for p in range(c * plan.pieces, (c + 1) * plan.pieces):
                @pl.when(at_middle)
                def _(p=p):
                    across(p).wait_recv()
                    w_full[p] = (w_sum[p].astype(F32) + w_cross[p].astype(F32)).astype(BF)

                    @pl.when(jnp.logical_not(at_end))
                    def _():
                        to_outer(p).start()

        def finish_weights(c):
            for p in range(c * plan.pieces, (c + 1) * plan.pieces):
                @pl.when(jnp.logical_not(at_middle))
                def _(p=p):
                    to_outer(p).wait_recv()

                    @pl.when(jnp.logical_not(at_end))
                    def _():
                        to_outer(p).start()

                weight_out[p * plan.zrows : (p + 1) * plan.zrows, :] = w_full[p]

        def lin_next(k):
            lin_step(k).wait_recv()
            v = lin_buf[k] + lin_recv[k]
            if k + 1 < stages:
                lin_buf[k + 1] = v
                lin_step(k + 1).start()
            else:
                lin_out[...] = v

        def chunk_total(c):
            ex.finish_sum(c, 1.0 / MX)
            ex.mix(c, ((1,), (1,)))

        last = plan.count - 1
        items = [(1 + k, lambda k=k: lin_next(k)) for k in range(z_bits)]
        waves = ex.waves(chunk_total)
        first = plan.levels - 1
        for w, wave in enumerate(waves):
            step = 2 + 2 * w
            items += [(step, task) for task in wave]
            for lag, task in enumerate((weight_grad, sum_weights, cross_weights)):
                if 0 <= w - first - lag < lay.chunks:
                    at = len(items) if lag < 2 else len(items) - len(wave)
                    items.insert(at, (step, lambda task=task, c=w - first - lag: task(c)))
            if w >= 3 and z_bits + w -3 < stages:
                items.append((step, lambda k=z_bits + w -3: lin_next(k)))
        for lag, task in ((1, sum_weights), (2, cross_weights)):
            items += [(last, lambda task=task, c=c: task(c))
                      for c in range(max(0, len(waves) - first - lag), lay.chunks)]
        items += [(last, lambda c=c: finish_weights(c)) for c in range(lay.chunks)]
        schedule(last, i, items)

        @pl.when(i == last)
        def _():
            ex.drain()
            d_stream.flush(plan.steps)
            for p in range(lay.chunks * plan.pieces):
                to_inner(p).wait_send()

                @pl.when(jnp.logical_not(at_end))
                def _(p=p):
                    to_outer(p).wait_send()

            for k in range(stages):
                lin_step(k).wait_send()

    acc = lay.acc_rows
    dma = pltpu.SemaphoreType.DMA
    return pl.pallas_call(
        kernel,
        grid=(plan.count,),
        in_specs=[
            ANYWHERE,
            plain_fields(plan)[1],
            ANYWHERE,
            plain_fields(plan)[1],
            fixed((W, 1024)),
            fixed((4, C, C)),
            fixed(spectrum.shape),
            fixed((W, W)),
            fixed((W, 128)),
            fixed(pick_all.shape),
            fixed(move_all.shape),
            fixed(move_lin.shape),
            fixed(zero_lanes.shape),
            ANYWHERE,
            ANYWHERE,
        ],
        out_specs=[
            ANYWHERE,
            plain_fields(plan)[1],
            ANYWHERE,
            fixed((lay.chunks * plan.wrows, 2 * W)),
            fixed((C + 8, W)),
        ],
        out_shape=[
            jax.ShapeDtypeStruct(p_big.shape, BF),
            jax.ShapeDtypeStruct(p_small.shape, BF),
            jax.ShapeDtypeStruct((plan.chips, 2, plan.by_pairs.total, 2 * W), BF),
            jax.ShapeDtypeStruct((lay.chunks * plan.wrows, 2 * W), BF),
            jax.ShapeDtypeStruct((C + 8, W), F32),
        ],
        scratch_shapes=[
            pltpu.VMEM((plan.chips, 2, plan.by_pairs.total, 2 * W), BF),
            pltpu.VMEM((W, W), BF),
            pltpu.VMEM((4, 2, acc, 128), F32),
            pltpu.VMEM((8, 2, acc, 128), F32),
            pltpu.VMEM((plan.wrows, 2 * W), BF),
            *[pltpu.VMEM((lay.chunks * plan.pieces, plan.zrows, 2 * W), BF)] * 5,
            pltpu.VMEM((stages, C + 8, W), F32),
            pltpu.VMEM((stages, C + 8, W), F32),
            dma((1 + lay.chunks,)),
            *[dma((lay.chunks * plan.pieces,))] * 5,
            dma((stages,)),
            dma((stages,)),
            *Stream.scratch(min(4, plan.steps), 2 * plan.per, big.cells),
            *Stream.scratch(min(4, plan.steps), 2 * plan.per, big.cells),
            *Stream.scratch(min(3, plan.steps), 2 * plan.per, big.cells),
            *Exchange.scratch(plan, lay),
        ],
        compiler_params=params(collective_id=2, has_side_effects=True),
        name="mode_backward",
    )(p_big, p_small, g_big, g_small, expand_tables(), lin_weight, spectrum, lin_grad, columns,
      pick_all, move_all, move_lin, zero_lanes, part, kernel_all)


def input_grads(plan, rank, part_big, part_small, modes, lin_sum, weights):
    big, small = plan.big, plan.small
    per, steps = plan.wide_per, plan.wide_steps
    last = steps - 1

    split = np.zeros((W, 4, 128), np.float32)
    for p in range(4):
        split[p * C : p * C + C, p, :C] = np.eye(C)
    split = split.reshape(W, 512)
    blades = np.zeros((2, 2 * W, 4, 128), np.float32)
    for odd in range(2):
        for lane in range(W):
            at = lane + 128 * odd if lane < 128 else 128 + 64 * odd + lane
            blades[odd, at, lane // C, lane % C] = 1.0
    blades = low(blades.reshape(2, 2 * W, 512))
    lay = plan.by_modes

    def body(r, pb, ps, mb, ms, vb, eb, vs, es, lin, cut, w_in, blade,
             db, ds, lin_out, bias_out, w_out, w_held, w_sem):
        i = pl.program_id(0)
        put = pltpu.make_async_copy(w_held, w_out, w_sem.at[0])

        @pl.when(i == 0)
        def _():
            v = lax.dot_general(
                lin[...], cut[...], (((1,), (0,)), ((), ())),
                precision=lax.Precision.HIGHEST, preferred_element_type=F32,
            )
            for p in range(4):
                lin_out[p] = v[:C, 128 * p : 128 * p + C]
                bias_out[p : p + 1, :] = v[C : C + 1, 128 * p : 128 * p + C]
            for c in range(lay.chunks):
                rows = w_in[c * plan.wrows : (c + 1) * plan.wrows, :]
                for odd in range(2):
                    v = dot(rows, blade[odd])
                    for j in range(lay.modes // 2):
                        for p in range(4):
                            w_held[lay.first_mode(c) + 2 * j + odd, p] = (
                                v[j * C : j * C + C, 128 * p : 128 * p + C]
                            )
            put.start()

        @pl.when(i == steps)
        def _():
            put.wait()

        def run(part, m, d, geo, inverse, spread, count):
            span = spread.shape[1]
            qs = []
            for pair in range(count):
                qs += inverse_pair(geo, load_by_modes(plan, m, pair), inverse[...], 1.0)
            q = jnp.concatenate(qs, axis=0) * jnp.asarray(1.0 / geo.side, BF)
            for j in range(geo.cells // span):
                v = dot(q[:, 128 * j : 128 * j + 128], spread[...])
                at = (slice(0, 2 * count), slice(None), slice(None),
                      slice(j * span, (j + 1) * span))
                d[at] = part[at].astype(F32) + v.reshape(2 * count, 4, C, span)

        @pl.when(i < steps)
        def _():
            run(pb, mb, db, big, vb, eb, per)

        @pl.when(i == steps)
        def _():
            run(ps, ms, ds, small, vs, es, plan.nsmall // 2)

    extra = [lin_sum, split, weights, blades]
    tables = []
    specs = []
    for geo in (big, small):
        tables += [geo.inverse, geo.spread]
        specs += [device_spec(geo.inverse.shape[1:]), const_spec(geo.spread.shape)]
    small_field = field_specs(plan)[1]
    big_field = pl.BlockSpec((2 * per, 4, C, big.cells), lambda i, r: (wide(i, last), 0, 0, 0))
    return pl.pallas_call(
        body,
        grid_spec=pltpu.PrefetchScalarGridSpec(
            num_scalar_prefetch=1,
            grid=(steps + 1,),
            in_specs=[
                big_field,
                small_field,
                pl.BlockSpec(
                    (plan.n, lay.chunks, per * lay.modes, 2 * W),
                    lambda i, r: (0, 0, wide(i, last), 0),
                ),
                pl.BlockSpec(
                    (plan.n, lay.chunks, plan.per * lay.modes, 2 * W),
                    lambda i, r: (0, 0, plan.steps, 0),
                ),
                *specs,
                *[const_spec(v.shape) for v in extra],
            ],
            out_specs=[big_field, small_field, const_spec((4, C, C)), const_spec((4, C)),
                       ANYWHERE],
            scratch_shapes=[
                pltpu.VMEM((plan.own, 4, C, C), F32), pltpu.SemaphoreType.DMA((1,))
            ],
        ),
        out_shape=[
            jax.ShapeDtypeStruct(part_big.shape, F32),
            jax.ShapeDtypeStruct(part_small.shape, F32),
            jax.ShapeDtypeStruct((4, C, C), F32),
            jax.ShapeDtypeStruct((4, C), F32),
            jax.ShapeDtypeStruct((plan.own, 4, C, C), F32),
        ],
        compiler_params=params(),
        name="input_grads",
    )(rank, part_big, part_small, modes, modes, *tables, *extra)


def on_device(plan, x_big, x_small, spec_weight, lin_weight, lin_bias, grad_big, grad_small):
    rank = lax.axis_index("rows").reshape(1)
    width = 2 * W
    modes, kernel, spectrum = forward_kernel(plan, x_big, x_small, spec_weight)
    out_big, out_small, pre_big, pre_small, part, lin_grad, columns = cells_pass(
        plan, rank, x_big, x_small, grad_big, grad_small, modes.reshape(plan.n, -1, width),
        lin_weight, lin_bias,
    )
    lay = plan.by_modes
    part_big, part_small, modes, weights, lin_sum = backward_kernel(
        plan, part.reshape((plan.chips, 2) + part.shape[1:]), pre_big, pre_small,
        grad_big, grad_small, kernel, spectrum.reshape(-1, plan.own, width), lin_weight,
        lin_grad, columns,
    )
    dx_big, dx_small, lin_weight_grad, lin_bias_grad, spec_grad = input_grads(
        plan, rank, part_big, part_small, modes.reshape(plan.n, lay.chunks, -1, width),
        lin_sum, weights,
    )
    return out_big, out_small, dx_big, dx_small, spec_grad, lin_weight_grad, lin_bias_grad


def solution(mesh):
    fields = P("samples", None, None, "rows")
    spec = P("rows", None, None, None)

    def run(x_big, x_small, *rest):
        count = mesh.shape["samples"]
        plan = Plan(mesh, x_big.shape[0] // count, x_small.shape[0] // count)

        def local(*args):
            return on_device(plan, *args)

        return jax.shard_map(
            local,
            mesh=mesh,
            in_specs=(fields, fields, spec, P(), P(), fields, fields),
            out_specs=(fields, fields, fields, fields, spec, P(), P()),
            check_vma=False,
        )(x_big, x_small, *rest)

    return run
```

```python
import math

import jax
import jax.numpy as jnp
import ml_dtypes
import numpy as np
from jax import lax
from jax.experimental import pallas as pl
from jax.experimental.pallas import tpu as pltpu
from jax.sharding import PartitionSpec as P

C = 48
MX = 16
N1 = 128
N2 = 64
W = 4 * C
MODES = MX * MX
BF = jnp.bfloat16
F32 = jnp.float32


def trig(side):
    a = np.arange(MX)
    freq = np.where(a < MX // 2, a, side - MX + a)
    phase = (np.arange(side)[:, None] * freq[None, :]) % side
    angle = phase.astype(np.float32) * np.float32(2.0 * math.pi / side)
    cos = np.cos(angle).astype(ml_dtypes.bfloat16).astype(np.float32)
    sin = np.sin(angle).astype(ml_dtypes.bfloat16).astype(np.float32)
    return cos, sin


def low(table):
    return table.astype(ml_dtypes.bfloat16)


class Geometry:
    def __init__(self, side, n):
        self.side = side
        self.rows = side // n
        self.cells = self.rows * side
        self.group = min(8, self.rows)
        self.ngroups = self.rows // self.group
        self.npairs = self.rows // 2
        self.qlanes = max(128, self.npairs * 64)
        self.hk = self.ngroups * 128
        cos, sin = trig(side)
        eye = np.eye(MX, dtype=np.float32)

        first = np.zeros((self.group, side, 256), np.float32)
        for h in range(self.group):
            first[h, :, h * MX : (h + 1) * MX] = cos
            first[h, :, 128 + h * MX : 128 + (h + 1) * MX] = sin
        self.first = low(first.reshape(self.group * side, 256))

        second = np.zeros((n, MX, MX, 2, self.ngroups, 128), np.float32)
        inverse = np.zeros((n, MX, MX, 2, self.qlanes), np.float32)
        for r in range(n):
            for h in range(self.rows):
                c, s = cos[r * self.rows + h], sin[r * self.rows + h]
                ce, se = c[:, None, None] * eye, s[:, None, None] * eye
                g, lane = h // self.group, (h % self.group) * MX
                second[r, :, :, 0, g, lane : lane + MX] = ce
                second[r, :, :, 1, g, lane : lane + MX] = se
                lane = h * 2 * MX
                inverse[r, :, :, 0, lane : lane + MX] = ce
                inverse[r, :, :, 0, lane + MX : lane + 2 * MX] = -se
                inverse[r, :, :, 1, lane : lane + MX] = -se
                inverse[r, :, :, 1, lane + MX : lane + 2 * MX] = -ce
        self.second = low(second.reshape(n, MODES, 2 * self.hk))
        inverse[..., MX : self.rows * 2 * MX : 2 * MX] = 0.0
        self.inverse = low(inverse.reshape(n, MODES, 2 * self.qlanes))

        spread = np.zeros((4, 2, MX, 4, side), np.float32)
        for h in range(4):
            spread[h, 0, :, h] = cos.T
            spread[h, 1, :, h] = sin.T
        self.spread = low(spread.reshape(128, 4 * side))
        if self.npairs == 1:
            self.spread = self.spread[:, : 2 * side]
        for h in range(4):
            spread[h, 1, 0, h] = 1.0
        self.pair_spread = low(spread.reshape(128, 4 * side))[:64, : 2 * side]


def turn(v):
    return jnp.concatenate([v[3 * C :], v[2 * C : 3 * C], -v[C : 2 * C], -v[:C]], axis=0)


def dot(a, b, dims=((1,), (0,))):
    return lax.dot_general(a, b, (dims, ((), ())), preferred_element_type=F32)


def forward_group(field, first, scale, keep=None):
    y = dot(field, first)
    grids = range(y.shape[0] // W)
    if keep is not None:
        keep(sum(y[W * s : W * s + W, :128] for s in grids))
    cols = []
    for s in grids:
        col = y[W * s : W * s + W, :128] + turn(y[W * s : W * s + W, 128:])
        cols.append((col * scale).astype(BF))
    return cols


def forward_rows(groups, second):
    stacked = []
    for s in range(2):
        cols = [cols[s] for cols in groups]
        stacked.append(jnp.concatenate(cols + [turn(col) for col in cols], axis=1))
    a, b = stacked
    both = jnp.concatenate([a[:128], b[:128], a[128:], b[128:]], axis=0)
    return dot(second, both, ((1,), (1,)))


def forward_grids(geo, get, first, second, scale):
    width = geo.group * geo.side
    groups = [forward_group(get(g * width, width), first, scale) for g in range(geo.ngroups)]
    return [
        forward_rows([cols[2 * k : 2 * k + 2] for cols in groups], second)
        for k in range(len(groups[0]) // 2)
    ]


def inverse_pair(geo, modes, inverse, scale):
    uv = dot(modes, inverse, ((0,), (0,)))
    result = []
    for s in range(2):
        part = jnp.concatenate(
            [uv[128 * s : 128 * s + 128], uv[256 + 64 * s : 320 + 64 * s]], axis=0
        )
        q = part[:, : geo.qlanes] + turn(part[:, geo.qlanes :])
        result.append((q * scale).astype(BF))
    return result


def fold_tables():
    dup = np.concatenate([np.arange(192), np.arange(128, 192)])
    pick = np.zeros((192, 4, 128), np.float32)
    move = np.zeros((192, 4, 192), np.float32)
    for q in range(4):
        pick[q * C : q * C + C, q, :C] = np.eye(C)
        for p in range(4):
            sign = -1.0 if (p >> 1) & q & 1 else 1.0
            o = p ^ q
            move[o * C : o * C + C, q, p * C : p * C + C] = sign * np.eye(C)
    return (
        low(pick[dup].reshape(256, 512)),
        low(move[dup][:, :, dup].reshape(256, 1024)),
        move.transpose(1, 0, 2).copy(),
    )


def expand_tables():
    dup = np.concatenate([np.arange(192), np.arange(128, 192)])
    place = np.zeros((4, C, 4, 256), np.float32)
    for p in range(4):
        for q in range(4):
            sign = -1.0 if (p >> 1) & q & 1 else 1.0
            full = np.zeros((C, 192), np.float32)
            o = p ^ q
            full[:, o * C : (o + 1) * C] = sign * np.eye(C)
            place[p, :, q] = full[:, dup]
    return low(place.reshape(W, 1024))


class Layout:
    def __init__(self, chunks, pairs, modes, by_mode):
        self.chunks, self.pairs, self.modes, self.by_mode = chunks, pairs, modes, by_mode
        self.crow = pairs * modes
        first = -(-self.crow // 32) * 16
        self.halves = (first, self.crow - first)
        self.slots = -(-pairs // 8) * 8
        self.acc_rows = self.slots * modes
        self.total = chunks * self.crow

    def first_mode(self, c):
        return c * self.modes if self.by_mode else 0


class Plan:
    def __init__(self, mesh, nbig, nsmall):
        self.n = mesh.shape["rows"]
        self.nz = mesh.shape["samples"]
        self.own = MODES // self.n
        self.per = max(1, 16 // self.own)
        self.big = Geometry(N1, self.n)
        self.small = Geometry(N2, self.n)
        self.nbig, self.nsmall = nbig, nsmall
        assert nbig % (2 * self.per) == 0 and nsmall % 2 == 0 and nsmall // 2 <= self.per
        self.steps = nbig // (2 * self.per)
        self.count = self.steps + 1
        self.wide_per = 2 * self.per if self.steps % 2 == 0 else self.per
        self.wide_steps = nbig // (2 * self.wide_per)
        self.block = self.per * self.own
        self.total = self.count * self.block
        pairs = self.count * self.per
        parts = next(c for c in (3, 2, 1) if self.count % c == 0)
        self.by_pairs = Layout(parts, pairs // parts, self.own, False)
        parts = max(1, self.own // 16)
        self.by_modes = Layout(parts, pairs, self.own // parts, True)
        self.chips = self.n // 2
        bits = list(range(1, self.n.bit_length() - 1))
        self.orders = (bits, bits[::-1])
        self.levels = len(bits)
        self.wrows = self.by_modes.modes // 2 * C
        self.pieces = 4
        self.zrows = self.wrows // self.pieces
        assert self.nz % 2 == 0 and self.zrows % 16 == 0

    def mask(self, h, idx):
        m = 0
        for t, b in enumerate(self.orders[h]):
            if idx >> (self.levels - 1 - t) & 1:
                m |= 1 << b
        return m


def wide(i, last):
    return jnp.minimum(i, last)


def params(**kw):
    return pltpu.CompilerParams(vmem_limit_bytes=56 * 1024 * 1024, **kw)


def const_spec(shape):
    return pl.BlockSpec(shape, lambda i, r: (0,) * len(shape))


def device_spec(shape):
    return pl.BlockSpec((None,) + shape, lambda i, r: (r[0],) + (0,) * len(shape))


def field_specs(plan):
    big, small = plan.big, plan.small
    last = plan.steps - 1
    return (
        pl.BlockSpec((2 * plan.per, 4, C, big.cells), lambda i, r: (wide(i, last), 0, 0, 0)),
        pl.BlockSpec((plan.nsmall, 4, C, small.cells), lambda i, r: (0, 0, 0, 0)),
    )


def mode_spec(plan):
    return pl.BlockSpec((plan.n, plan.block, 2 * W), lambda i, r: (0, i, 0))


def store_by_modes(plan, ref, pair, z):
    lay = plan.by_modes
    z = z.reshape(plan.n, lay.chunks, lay.modes, 2 * W).astype(BF)
    ref[:, :, pair * lay.modes : (pair + 1) * lay.modes, :] = z


def load_by_modes(plan, ref, pair):
    lay = plan.by_modes
    return ref[:, :, pair * lay.modes : (pair + 1) * lay.modes, :].reshape(MODES, 2 * W)


def load_modes(plan, ref, pair):
    return ref[:, pair * plan.own : (pair + 1) * plan.own, :].reshape(MODES, 2 * W)


def flip(index, mask):
    result = index
    for b in range(mask.bit_length()):
        if mask >> b & 1:
            bit = lax.rem(lax.div(index, 1 << b), 2)
            result = result + (1 - 2 * bit) * (1 << b)
    return result


def tiles(v):
    return [v[:, 128 * t : 128 * t + 128] for t in range(v.shape[1] // 128)]


def sample_rows(first, second, third):
    lane = lax.broadcasted_iota(jnp.int32, third.shape, 1)
    a = jnp.concatenate([first, jnp.where(lane < 64, third, 0.0)], axis=1)
    b = jnp.concatenate([second, jnp.where(lane < 64, 0.0, third)], axis=1)
    return jnp.concatenate([a, b], axis=0)


def pair_tiles(a, b):
    lane = lax.broadcasted_iota(jnp.int32, (a.shape[0], 128), 1)
    return a[:, :128], b[:, :128], jnp.where(lane < 64, a[:, 128:], b[:, 128:])


def remote(src, dst, send, recv, device):
    return pltpu.make_async_remote_copy(
        src_ref=src, dst_ref=dst, send_sem=send, recv_sem=recv, device_id=device
    )


class Stream:
    def __init__(self, field, ring, sems, grids):
        self.field, self.ring, self.sems, self.grids = field, ring, sems, grids
        self.depth = ring.shape[0]

    @staticmethod
    def scratch(depth, grids, cells):
        return [pltpu.VMEM((depth, grids, 4, C, cells), BF), pltpu.SemaphoreType.DMA((depth,))]

    def slot(self, i):
        return self.ring.at[lax.rem(i, self.depth)]

    def copy(self, i, out=False):
        block = self.field.at[pl.ds(i * self.grids, self.grids)]
        sem = self.sems.at[lax.rem(i, self.depth)]
        if out:
            return pltpu.make_async_copy(self.slot(i), block, sem)
        return pltpu.make_async_copy(block, self.slot(i), sem)

    def read(self, i, count):
        @pl.when(i == 0)
        def _():
            for k in range(min(self.depth, count)):
                self.copy(jnp.int32(k)).start()

        self.copy(i).wait()
        return self.slot(i)

    def ahead(self, i, count):
        @pl.when(i + self.depth < count)
        def _():
            self.copy(i + self.depth).start()

    def reserve(self, i):
        @pl.when(i >= self.depth)
        def _():
            self.copy(i - self.depth, True).wait()

        return self.slot(i)

    def flush(self, count):
        for k in range(max(0, count - self.depth), count):
            self.copy(jnp.int32(k), True).wait()


class Exchange:
    @staticmethod
    def scratch(plan, lay):
        chips, width = plan.chips, 2 * W
        dma = pltpu.SemaphoreType.DMA
        part = (lay.chunks, 2)
        moving = (2, chips, lay.chunks * lay.halves[0], width)
        return [
            pltpu.VMEM((chips, lay.total, width), BF),
            pltpu.VMEM(moving, BF),
            pltpu.VMEM(moving, BF),
            pltpu.VMEM((chips, 2, lay.total, width), BF),
            pltpu.VMEM((3, lay.acc_rows, 128), F32),
            pltpu.VMEM((3, lay.acc_rows, 128), F32),
            dma((lay.chunks,)),
            dma((lay.chunks,)),
            dma(part + (plan.levels,)),
            dma(part + (plan.levels,)),
            dma(part + (chips,)),
            dma(part + (chips,)),
            dma(part + (chips,)),
            dma(part + (chips,)),
            dma((lay.chunks,)),
            pltpu.VMEM((plan.own, 256, 256), BF),
        ]

    def __init__(self, plan, lay, part, out, refs, origin):
        self.plan, self.lay, self.part, self.out, self.origin = plan, lay, part, out, origin
        (self.sib, self.sums, self.lev, self.res, self.acc, self.mixed,
         self.sib_s, self.sib_r, self.lev_s, self.lev_r, self.ag_s, self.ag_r,
         self.fw_s, self.fw_r, self.out_s, self.kernel) = refs
        self.me = lax.axis_index("rows")
        self.core = lax.rem(self.me, 2)

    def partners(self):
        return [flip(self.me, 1 << b) for b in range(self.plan.n.bit_length() - 1)]

    def chunk(self, c):
        return pl.ds(c * self.lay.crow, self.lay.crow)

    def rows(self, c, h):
        return pl.ds(c * self.lay.crow + h * self.lay.halves[0], self.lay.halves[h])

    def moving(self, c, h):
        return pl.ds(c * self.lay.halves[0], self.lay.halves[h])

    def to_sibling(self, c):
        return remote(
            self.origin(c, 1 - self.core), self.sib.at[:, self.chunk(c), :],
            self.sib_s.at[c], self.sib_r.at[c], {"rows": flip(self.me, 1)},
        )

    def level(self, c, h, t):
        plan = self.plan
        count = plan.chips >> (t + 1)
        rows = self.moving(c, h)
        at = plan.chips - 2 * count
        return remote(
            self.sums.at[h, pl.ds(count, count), rows, :],
            self.lev.at[h, pl.ds(at, count), rows, :],
            self.lev_s.at[c, h, t], self.lev_r.at[c, h, t],
            {"rows": flip(self.me, 1 << plan.orders[h][t])},
        )

    def block(self, c, h, owner):
        return self.res.at[lax.div(owner, 2), lax.rem(owner, 2), self.rows(c, h), :]

    def gather(self, c, h, u, idx):
        plan = self.plan
        sem = (1 << u) - 1 + idx
        ref = self.block(c, h, flip(self.me, plan.mask(h, idx)))
        return remote(
            ref, ref, self.ag_s.at[c, h, sem], self.ag_r.at[c, h, sem],
            {"rows": flip(self.me, 1 << plan.orders[h][plan.levels - 1 - u])},
        )

    def forward(self, c, h, idx):
        ref = self.block(c, h, flip(self.me, self.plan.mask(h, idx)))
        return remote(
            ref, ref, self.fw_s.at[c, h, idx], self.fw_r.at[c, h, idx],
            {"rows": flip(self.me, 1)},
        )

    def store(self, c):
        rows = self.chunk(c)
        return pltpu.make_async_copy(
            self.res.at[:, :, rows, :], self.out.at[:, :, rows, :], self.out_s.at[c]
        )

    def begin(self, c):
        self.to_sibling(c).start()

    def add_sibling(self, c):
        plan = self.plan
        self.to_sibling(c).wait_recv()
        for far in (1, 0):
            for h in range(2):
                span = plan.chips // 2
                for idx in range(far * span, far * span + span):
                    owner = flip(self.me, plan.mask(h, idx))
                    chip = lax.div(owner, 2)
                    rows = self.rows(c, h)
                    v = self.part[chip, self.core, rows, :].astype(F32)
                    v = v + self.sib[chip, rows, :].astype(F32)
                    self.sums[h, idx, self.moving(c, h), :] = v.astype(BF)
                if far:
                    self.level(c, h, 0).start()

    def next_level(self, c, t):
        plan = self.plan
        count = plan.chips >> t
        at = plan.chips - 2 * count
        for h in range(2):
            rows = self.moving(c, h)
            self.level(c, h, t - 1).wait_recv()
            for idx in reversed(range(count)):
                v = self.sums[h, idx, rows, :].astype(F32)
                v = v + self.lev[h, at + idx, rows, :].astype(F32)
                self.sums[h, idx, rows, :] = v.astype(BF)
                if idx == count // 2:
                    self.level(c, h, t).start()

    def finish_sum(self, c, scale):
        plan, lay = self.plan, self.lay
        for h in range(2):
            rows = self.moving(c, h)
            self.level(c, h, plan.levels - 1).wait_recv()
            v = self.sums[h, 0, rows, :].astype(F32)
            v = (v + self.lev[h, plan.chips - 2, rows, :].astype(F32)) * scale
            at = h * lay.halves[0]
            for t, tile in enumerate(tiles(v)):
                self.acc[t, at : at + lay.halves[h], :] = tile

    def mix(self, c, dims):
        lay = self.lay

        def one(m):
            rows = pl.ds(m, lay.slots, stride=lay.modes)
            lhs = sample_rows(*(self.acc[t, rows, :] for t in range(3))).astype(BF)
            res = dot(lhs, self.kernel[lay.first_mode(c) + m], dims)
            for t, tile in enumerate(pair_tiles(res[: lay.slots], res[lay.slots :])):
                self.mixed[t, rows, :] = tile

        unroll = 8

        @pl.loop(0, lay.modes // unroll)
        def _(j):
            for u in range(unroll):
                one(j * unroll + u)

        result = jnp.concatenate([self.mixed[t, : lay.crow, :] for t in range(3)], axis=1)
        self.res[lax.div(self.me, 2), self.core, self.chunk(c), :] = result.astype(BF)
        for h in range(2):
            self.gather(c, h, 0, 0).start()
            self.forward(c, h, 0).start()

    def spread(self, c, u):
        for h in range(2):
            got = 1 << (u - 1)
            for idx in range(got):
                self.gather(c, h, u - 1, idx).wait_recv()
            if u < self.plan.levels:
                for idx in reversed(range(2 * got)):
                    self.gather(c, h, u, idx).start()
            for idx in range(got, 2 * got):
                self.forward(c, h, idx).start()

    def close(self, c):
        for h in range(2):
            for idx in range(self.plan.chips):
                self.forward(c, h, idx).wait_recv()
        self.store(c).start()

    def drain(self):
        plan = self.plan
        for c in range(self.lay.chunks):
            self.to_sibling(c).wait_send()
            for h in range(2):
                for t in range(plan.levels):
                    self.level(c, h, t).wait_send()
                for u in range(plan.levels):
                    for idx in range(1 << u):
                        self.gather(c, h, u, idx).wait_send()
                for idx in range(plan.chips):
                    self.forward(c, h, idx).wait_send()
            self.store(c).wait()

    def clear(self):
        lay = self.lay
        if lay.acc_rows > lay.crow:
            self.acc[:, lay.crow :, :] = jnp.zeros((3, lay.acc_rows - lay.crow, 128), F32)

    def waves(self, total):
        plan, chunks = self.plan, self.lay.chunks
        todo = []
        for c in range(chunks):
            chain = [lambda c=c, t=t: self.next_level(c, t) for t in range(1, plan.levels)]
            chain += [lambda c=c: total(c)]
            chain += [lambda c=c, u=u: self.spread(c, u) for u in range(1, plan.levels + 1)]
            chain += [lambda c=c: self.close(c)]
            todo.append(chain)
        waves = []
        for w in range(len(todo[0]) + chunks - 1):
            at = [(c, w - c) for c in reversed(range(chunks))]
            waves.append([todo[c][k] for c, k in at if 0 <= k < len(todo[c])])
        return waves


def greet(devices):
    barrier = pltpu.get_barrier_semaphore()
    for device in devices:
        pl.semaphore_signal(barrier, inc=1, device_id=device)
    pl.semaphore_wait(barrier, len(devices))


def build_modes(plan, place, weights, kernel):
    flat = jnp.concatenate([weights[:, p].reshape(-1, C) for p in range(4)], axis=1)
    for q in range(4):
        rows = dot(flat, place[:, 256 * q : 256 * q + 256])
        kernel[:, C * q : C * q + C, :] = rows.astype(BF).reshape(plan.own, C, 256)
    kernel[:, W:, :] = kernel[:, 128:W, :]


def build_lin(place, weight):
    flat = jnp.concatenate([weight[p] for p in range(4)], axis=1)
    rows = [dot(flat, place[:, 256 * q : 256 * q + 256]) for q in range(4)]
    return jnp.concatenate(rows, axis=0).astype(BF)


def half_tables():
    rows = np.zeros((192, 384), np.float32)
    rows[:128, :128] = 0.5 * np.eye(128)
    rows[128:, 192:256] = 0.5 * np.eye(64)
    rows[128:, 256:320] = 0.5 * np.eye(64)
    line = np.zeros((128, C), np.float32)
    line[MX :: 2 * MX] = 0.5
    return low(rows), low(line), low(np.eye(C, dtype=np.float32))


def plain_fields(plan):
    big, small = plan.big, plan.small
    last = plan.steps - 1
    return [
        pl.BlockSpec((2 * plan.per, 4, C, big.cells), lambda i: (wide(i, last), 0, 0, 0)),
        pl.BlockSpec((plan.nsmall, 4, C, small.cells), lambda i: (0, 0, 0, 0)),
    ]


def fixed(shape):
    return pl.BlockSpec(shape, lambda i: (0,) * len(shape))


ANYWHERE = pl.BlockSpec(memory_space=pl.ANY)


def forward_kernel(plan, x_big, x_small, spec_weight):
    big, small = plan.big, plan.small
    lay = plan.by_pairs
    last = plan.wide_steps

    def kernel(x_hbm, xs, fb, fs, place, weights, sb_all, ss_all, out, kernel_out, spectrum,
               part, sb, ss, table_sem, ring, ring_sem, *refs):
        i = pl.program_id(0)
        stream = Stream(x_hbm, ring, ring_sem, 2 * plan.wide_per)
        ex = Exchange(plan, lay, part, out, refs, lambda c, core: part.at[
            :, core, pl.ds(c * lay.crow, lay.crow), :
        ])
        loads = [
            pltpu.make_async_copy(sb_all.at[ex.me], sb, table_sem.at[0]),
            pltpu.make_async_copy(ss_all.at[ex.me], ss, table_sem.at[1]),
        ]
        keep = pltpu.make_async_copy(ex.kernel, kernel_out, table_sem.at[2])

        @pl.when(i == 0)
        def _():
            for load in loads:
                load.start()
            greet([{"rows": d} for d in ex.partners()])
            ex.clear()
            for load in loads:
                load.wait()

        def run(x, geo, first, second, count, per):
            def get(start, width):
                v = x[: 2 * count, :, :, start : start + width]
                return v.reshape(2 * count * W, width)

            zs = forward_grids(geo, get, first[...], second[...], 1.0 / geo.side)
            parts = [z.reshape(plan.chips, 2, plan.own, 2 * W) for z in zs]
            parts += [jnp.zeros_like(parts[0])] * (per - count)
            z = jnp.concatenate(parts, axis=2) if per > 1 else parts[0]
            rows = pl.ds(pl.multiple_of(i * plan.wide_per * plan.own, 16), per * plan.own)
            part[:, :, rows, :] = z.astype(BF)

        @pl.when(i < last)
        def _():
            run(stream.read(i, last), big, fb, sb, plan.wide_per, plan.wide_per)
            stream.ahead(i, last)

        @pl.when(i == last)
        def _():
            run(xs, small, fs, ss, plan.nsmall // 2, plan.per)

        def total(c):
            ex.finish_sum(c, 1.0)
            spectrum[ex.chunk(c), :] = jnp.concatenate(
                [ex.acc[t, : lay.crow, :] for t in range(3)], axis=1
            ).astype(BF)
            ex.mix(c, ((1,), (0,)))

        def prepare():
            build_modes(plan, place, weights, ex.kernel)
            keep.start()

        waves = ex.waves(total)
        items = []
        for c in range(lay.chunks):
            pairs = (c + 1) * lay.pairs
            end = min(-(-pairs // plan.wide_per) - 1, last)
            items.append((end, lambda c=c: ex.begin(c)))
            if c == lay.chunks - 1:
                items.append((last, prepare))
                items += [(last, task) for task in waves.pop(0)]
            items.append((min(end + 1, last), lambda c=c: ex.add_sibling(c)))
        items += [(last, task) for wave in waves for task in wave]
        schedule(last, i, items)

        @pl.when(i == last)
        def _():
            ex.drain()
            keep.wait()

    return pl.pallas_call(
        kernel,
        grid=(last + 1,),
        in_specs=[
            ANYWHERE,
            plain_fields(plan)[1],
            fixed(big.first.shape),
            fixed(small.first.shape),
            fixed((W, 1024)),
            fixed(spec_weight.shape),
            ANYWHERE,
            ANYWHERE,
        ],
        out_specs=[ANYWHERE, ANYWHERE, fixed((plan.by_pairs.total, 2 * W))],
        out_shape=[
            jax.ShapeDtypeStruct((plan.chips, 2, plan.by_pairs.total, 2 * W), BF),
            jax.ShapeDtypeStruct((plan.own, 256, 256), BF),
            jax.ShapeDtypeStruct((plan.by_pairs.total, 2 * W), BF),
        ],
        scratch_shapes=[
            pltpu.VMEM((plan.chips, 2, plan.by_pairs.total, 2 * W), BF),
            pltpu.VMEM(big.second.shape[1:], BF),
            pltpu.VMEM(small.second.shape[1:], BF),
            pltpu.SemaphoreType.DMA((3,)),
            *Stream.scratch(min(4, last), 2 * plan.wide_per, big.cells),
            *Exchange.scratch(plan, plan.by_pairs),
        ],
        compiler_params=params(collective_id=1, has_side_effects=True),
        name="mode_forward",
    )(x_big, x_small, big.first, small.first, expand_tables(), spec_weight,
      big.second, small.second)


def schedule(last, i, items):
    for step in range(last + 1):
        now = [task for when, task in items if min(when, last) == step]
        if now:
            @pl.when(i == step)
            def _(now=now):
                for task in now:
                    task()


def cells_pass(plan, rank, x_big, x_small, g_big, g_small, modes, lin_weight,
               lin_bias):
    k0 = math.sqrt(2.0 / math.pi)
    k1 = k0 * 0.044715

    def low_of(value):
        return jnp.asarray(value, BF)

    per, steps = plan.wide_per, plan.wide_steps
    last = steps - 1

    def body(r, xb, xs, gb, gs, m, m_next, ms, fb, sb, vb, eb, fs, ss, vs, es,
             place, rows_table, line, eye, lw, lb, ob, os_, pb, ps, z, lin_acc, y_acc,
             kt, bias_ref, q_next):
        i = pl.program_id(0)

        @pl.when(i == 0)
        def _():
            full = build_lin(place[...], lw)[:, :W]
            kt[...] = dot(full, rows_table[...], ((0,), (0,))).astype(BF)
            for q in range(4):
                bias_ref[C * q : C * q + C, :] = dot(
                    eye[...], line[...] * lb[q : q + 1, :], ((1,), (1,))
                ).astype(BF)
            lin_acc[...] = jnp.zeros_like(lin_acc)
            y_acc[...] = jnp.zeros_like(y_acc)

        def coefficients(geo, m, pair, inverse):
            qs = inverse_pair(geo, load_modes(plan, m, pair), inverse[...], 0.5 / MX)
            line = jnp.concatenate([bias_ref[...]] * (geo.qlanes // 128), axis=1)
            return [q + line for q in qs]

        def prepare(m):
            for s, q in enumerate(coefficients(plan.big, m, 0, vb)):
                q_next[s] = q

        @pl.when(i == 0)
        def _():
            prepare(m)

        def run(x, g, o, d, m, z, geo, first, second, inverse, spread, count, following=None):
            wide_cells = 2 * geo.side
            lane = lax.broadcasted_iota(jnp.int32, (W, 128), 1)
            held, groups = {}, {}

            def rows_back(pair):
                held[2 * pair], held[2 * pair + 1] = coefficients(geo, m, pair, inverse)

            def main(at, p):
                lo = p * wide_cells
                cells = slice(lo, lo + wide_cells)
                q = held[at][:, 128 * (p // 2) : 128 * (p // 2) + 128]
                xv = x[at, :, :, cells].reshape(W, wide_cells)
                if p % 2 == 0:
                    tail = jnp.where(lane < 64, q, kt[:, 128:256])
                    rhs = [xv[:128], spread[...], xv[128:]]
                else:
                    tail = jnp.where(lane >= 64, q, kt[:, 256:384])
                    rhs = [xv[:128], xv[128:], spread[...]]
                lhs = jnp.concatenate([kt[:, :128], tail], axis=1)
                b = dot(lhs, jnp.concatenate(rhs, axis=0))
                b = b.astype(BF)
                b2 = b * b
                e = low_of(1.0) + jnp.tanh(b * (low_of(2.0 * k0) + low_of(8.0 * k1) * b2))
                o[at, :, :, cells] = (xv + b * e).reshape(4, C, wide_cells)
                rise = b * (low_of(k0) + low_of(12.0 * k1) * b2)
                slope = e * (low_of(0.5) + rise * (low_of(2.0) - e))
                gv = g[at, :, :, cells].reshape(W, wide_cells)
                d[at, :, :, cells] = (gv * slope).reshape(4, C, wide_cells)

            def weight_grad(at, part):
                span = geo.cells // 2
                xa = x[at, :, :, part * span : part * span + span].reshape(W, span)
                pa = d[at, :, :, part * span : part * span + span].reshape(W, span)
                lin_acc[...] += dot(xa, pa, ((1,), (1,)))

            def keep(y):
                y_acc[...] += y

            def columns(pair, k):
                width = geo.group * geo.side
                v = d[2 * pair : 2 * pair + 2, :, :, k * width : k * width + width]
                cols = forward_group(v.reshape(2 * W, width), first[...], 1.0, keep)
                groups.setdefault(pair, []).append(cols)

            def rows_out(pair):
                store_by_modes(plan, z, pair, forward_rows(groups[pair], second[...]))

            side = []
            if following is None:
                rows_back(0)
            else:
                for s in range(2):
                    held[s] = q_next.at[s]
            for at in range(2 * count):
                pair = at // 2
                if at % 2 == 0 and pair + 1 < count:
                    side.append(lambda pair=pair: rows_back(pair + 1))
                if at == 2 and following is not None:
                    side.append(following)
                done = 0
                for p in range(geo.npairs):
                    main(at, p)
                    if side:
                        side.pop(0)()
                    if 2 * (p + 1) == geo.npairs:
                        side.append(lambda at=at: weight_grad(at, 0))
                    if at % 2 == 1 and (p + 1) * geo.ngroups // geo.npairs > done:
                        side.append(lambda pair=pair, k=done: columns(pair, k))
                        done += 1
                if geo.npairs == 1:
                    side.append(lambda at=at: weight_grad(at, 0))
                side.append(lambda at=at: weight_grad(at, 1))
                if at % 2 == 1:
                    side.append(lambda pair=pair: rows_out(pair))
            for task in side:
                task()

        @pl.when(i < steps)
        def _():
            run(xb, gb, ob, pb, m, z, plan.big, fb, sb, vb, eb, per,
                lambda: prepare(m_next))

        @pl.when(i == steps)
        def _():
            if plan.nsmall // 2 < per:
                z[...] = jnp.zeros_like(z)
            run(xs, gs, os_, ps, ms, z, plan.small, fs, ss, vs, es, plan.nsmall // 2)

    big, small = plan.big, plan.small
    tables = []
    specs = []
    for geo in (big, small):
        tables += [geo.first, geo.second, geo.inverse, geo.pair_spread]
        specs += [
            const_spec(geo.first.shape),
            device_spec(geo.second.shape[1:]),
            device_spec(geo.inverse.shape[1:]),
            const_spec(geo.pair_spread.shape),
        ]
    extra = [expand_tables(), *half_tables(), lin_weight, lin_bias]
    small_field = field_specs(plan)[1]
    big_field = pl.BlockSpec((2 * per, 4, C, big.cells), lambda i, r: (wide(i, last), 0, 0, 0))
    rows = per * plan.own
    lay = plan.by_modes
    return pl.pallas_call(
        body,
        grid_spec=pltpu.PrefetchScalarGridSpec(
            num_scalar_prefetch=1,
            grid=(steps + 1,),
            in_specs=[
                big_field,
                small_field,
                big_field,
                small_field,
                pl.BlockSpec((plan.n, rows, 2 * W), lambda i, r: (0, wide(i, last), 0)),
                pl.BlockSpec(
                    (plan.n, plan.own, 2 * W), lambda i, r: (0, wide(i + 1, last) * per, 0)
                ),
                pl.BlockSpec((plan.n, plan.block, 2 * W), lambda i, r: (0, plan.steps, 0)),
                *specs,
                *[const_spec(v.shape) for v in extra],
            ],
            out_specs=[
                big_field,
                small_field,
                big_field,
                small_field,
                pl.BlockSpec(
                    (plan.n, lay.chunks, per * lay.modes, 2 * W), lambda i, r: (0, 0, i, 0)
                ),
                const_spec((W, W)),
                const_spec((W, 128)),
            ],
            scratch_shapes=[
                pltpu.VMEM((W, 2 * W), BF),
                pltpu.VMEM((W, 128), BF),
                pltpu.VMEM((2, W, big.qlanes), BF),
            ],
        ),
        out_shape=[
            jax.ShapeDtypeStruct(x_big.shape, BF),
            jax.ShapeDtypeStruct(x_small.shape, BF),
            jax.ShapeDtypeStruct(x_big.shape, BF),
            jax.ShapeDtypeStruct(x_small.shape, BF),
            jax.ShapeDtypeStruct(
                (plan.n, lay.chunks, (steps + 1) * per * lay.modes, 2 * W), BF
            ),
            jax.ShapeDtypeStruct((W, W), F32),
            jax.ShapeDtypeStruct((W, 128), F32),
        ],
        compiler_params=params(),
        name="cells",
    )(rank, x_big, x_small, g_big, g_small, modes, modes, modes, *tables, *extra)


def backward_kernel(plan, part, p_big, p_small, g_big, g_small, kernel_all, spectrum,
                    lin_weight, lin_grad, columns):
    big, small = plan.big, plan.small
    lay = plan.by_modes
    stages = plan.n.bit_length() - 1 + plan.nz.bit_length() - 1
    z_bits = plan.nz.bit_length() - 1
    pick_all, move_all, move_lin = fold_tables()
    zero_lanes = np.zeros((8, 128), np.float32)
    zero_lanes[0, ::MX] = 1.0

    def kernel(pb, ps, gb, gs, place, lw, spec, lin_in, col_in, pick, move, shift, line, part_in, kernel_in,
               db, ds, out, weight_out, lin_out,
               part, kk, sa, mb, w_rows, w_part, w_sum, w_recv, w_cross, w_full, lin_buf, lin_recv,
               in_sem, zs, zr, zc, zos, zor, ls, lr, p_ring, p_sem, g_ring, g_sem, d_ring, d_sem, *refs):
        i = pl.program_id(0)
        p_stream = Stream(pb, p_ring, p_sem, 2 * plan.per)
        g_stream = Stream(gb, g_ring, g_sem, 2 * plan.per)
        d_stream = Stream(db, d_ring, d_sem, 2 * plan.per)
        ex = Exchange(plan, lay, part, out, refs, lambda c, core: part_in.at[
            :, core, c, pl.ds(0, lay.crow), :
        ])
        here = lax.axis_index("samples")
        loads = [
            pltpu.make_async_copy(
                part_in.at[:, :, c, pl.ds(0, lay.crow), :], part.at[:, :, ex.chunk(c), :],
                in_sem.at[1 + c],
            )
            for c in range(lay.chunks)
        ]
        load_kernel = pltpu.make_async_copy(kernel_in, ex.kernel, in_sem.at[0])

        left = here < plan.nz // 2
        place_z = jnp.where(left, here, plan.nz - 1 - here)
        at_end = place_z == 0
        at_middle = place_z == plan.nz // 2 - 1
        inward = {"samples": jnp.where(left, here + 1, here - 1)}
        outward = {"samples": jnp.where(left, here - 1, here + 1)}

        def to_inner(p):
            return remote(w_sum.at[p], w_recv.at[p], zs.at[p], zr.at[p], inward)

        def across(p):
            return remote(w_sum.at[p], w_cross.at[p], zs.at[p], zc.at[p], inward)

        def to_outer(p):
            return remote(w_full.at[p], w_full.at[p], zos.at[p], zor.at[p], outward)

        def send_inward(p):
            @pl.when(at_middle)
            def _():
                across(p).start()

            @pl.when(jnp.logical_not(at_middle))
            def _():
                to_inner(p).start()

        def lin_partner(k):
            if k < z_bits:
                return {"samples": flip(here, 1 << k)}
            return {"rows": flip(ex.me, 1 << (k - z_bits))}

        def lin_step(k):
            return remote(lin_buf.at[k], lin_recv.at[k], ls.at[k], lr.at[k], lin_partner(k))

        @pl.when(i == 0)
        def _():
            for load in loads:
                load.start()
            load_kernel.start()
            greet([{"rows": d} for d in ex.partners()]
                  + [{"samples": lax.rem(here + d, plan.nz)} for d in range(1, plan.nz)])
            for c in range(lay.chunks):
                ex.begin(c)
            folded = None
            for q in range(4):
                term = lax.dot_general(
                    lin_in[C * q : C * q + C, :], shift[q], (((1,), (0,)), ((), ())),
                    precision=lax.Precision.HIGHEST, preferred_element_type=F32,
                )
                folded = term if folded is None else folded + term
            lin_buf[0, :C, :] = folded
            lin_buf[0, C:, :] = lax.dot_general(
                line[...], col_in[...], (((1,), (1,)), ((), ())),
                precision=lax.Precision.HIGHEST, preferred_element_type=F32,
            )
            lin_step(0).start()
            kk[...] = build_lin(place[...], lw)[:, :W]
            for c, load in enumerate(loads):
                load.wait()
                ex.add_sibling(c)
            ex.clear()
            if lay.acc_rows > lay.crow:
                rest = lay.acc_rows - lay.crow
                sa[:, :, lay.crow :, :] = jnp.zeros((4, 2, rest, 128), F32)
                mb[:, :, lay.crow :, :] = jnp.zeros((8, 2, rest, 128), F32)
            load_kernel.wait()

        def run(p, g, d, geo, count):
            for at in range(2 * count):
                v = dot(kk[...], p[at, :, :, :].reshape(W, geo.cells))
                v = g[at, :, :, :].reshape(W, geo.cells) + v.astype(BF)
                d[at, :, :, :] = v.reshape(4, C, geo.cells)

        @pl.when(i < plan.steps)
        def _():
            p = p_stream.read(i, plan.steps)
            g = g_stream.read(i, plan.steps)
            run(p, g, d_stream.reserve(i), big, plan.per)
            d_stream.copy(i, True).start()
            p_stream.ahead(i, plan.steps)
            g_stream.ahead(i, plan.steps)

        @pl.when(i == plan.steps)
        def _():
            run(ps, gs, ds, small, plan.nsmall // 2)

        def weight_grad(c):
            crow, modes = lay.crow, lay.modes
            grads = sample_rows(*(ex.acc[t, :crow, :] for t in range(3))).astype(BF)
            held = spec[:, lay.first_mode(c) : lay.first_mode(c) + modes, :]
            spectra = sample_rows(*tiles(held.reshape(crow, 2 * W).astype(F32))).astype(BF)
            for t, tile in enumerate(tiles(dot(spectra, pick[...]))):
                sa[t, 0, :crow, :] = tile[:crow]
                sa[t, 1, :crow, :] = tile[crow:]
            for t, tile in enumerate(tiles(dot(grads, move[...]))):
                mb[t, 0, :crow, :] = tile[:crow]
                mb[t, 1, :crow, :] = tile[crow:]

            def one(m):
                rows = pl.ds(m, lay.slots, stride=modes)
                left = [sa[q, s, rows, :] for q in range(4) for s in range(2)]
                right = [
                    jnp.concatenate([mb[2 * q, s, rows, :], mb[2 * q + 1, s, rows, :]], axis=1)
                    for q in range(4) for s in range(2)
                ]
                v = dot(
                    jnp.concatenate(left, axis=0).astype(BF),
                    jnp.concatenate(right, axis=0).astype(BF),
                    ((0,), (0,)),
                )
                return v[:C]

            unroll = 2

            @pl.loop(0, modes // (2 * unroll))
            def _(j):
                for u in range(unroll):
                    pair = j * unroll + u
                    v = pair_tiles(one(2 * pair), one(2 * pair + 1))
                    v = jnp.concatenate(v, axis=1).astype(BF)
                    w_rows[pl.ds(pl.multiple_of(pair * C, 16), C), :] = v

            for k in range(plan.pieces):
                p = c * plan.pieces + k
                w_part[p] = w_rows[k * plan.zrows : (k + 1) * plan.zrows, :]

                @pl.when(at_end)
                def _(p=p):
                    w_sum[p] = w_part[p]
                    send_inward(p)

        def sum_weights(c):
            for p in range(c * plan.pieces, (c + 1) * plan.pieces):
                @pl.when(jnp.logical_not(at_end))
                def _(p=p):
                    to_inner(p).wait_recv()
                    w_sum[p] = (w_part[p].astype(F32) + w_recv[p].astype(F32)).astype(BF)
                    send_inward(p)

        def cross_weights(c):
            for p in range(c * plan.pieces, (c + 1) * plan.pieces):
                @pl.when(at_middle)
                def _(p=p):
                    across(p).wait_recv()
                    w_full[p] = (w_sum[p].astype(F32) + w_cross[p].astype(F32)).astype(BF)

                    @pl.when(jnp.logical_not(at_end))
                    def _():
                        to_outer(p).start()

        def finish_weights(c):
            for p in range(c * plan.pieces, (c + 1) * plan.pieces):
                @pl.when(jnp.logical_not(at_middle))
                def _(p=p):
                    to_outer(p).wait_recv()

                    @pl.when(jnp.logical_not(at_end))
                    def _():
                        to_outer(p).start()

                weight_out[p * plan.zrows : (p + 1) * plan.zrows, :] = w_full[p]

        def lin_next(k):
            lin_step(k).wait_recv()
            v = lin_buf[k] + lin_recv[k]
            if k + 1 < stages:
                lin_buf[k + 1] = v
                lin_step(k + 1).start()
            else:
                lin_out[...] = v

        def chunk_total(c):
            ex.finish_sum(c, 1.0 / MX)
            weight_grad(c)
            ex.mix(c, ((1,), (1,)))

        last = plan.count - 1
        items = [(1 + k, lambda k=k: lin_next(k)) for k in range(z_bits)]
        waves = ex.waves(chunk_total)
        first = plan.levels - 1
        for w, wave in enumerate(waves):
            step = 2 + 2 * w
            items += [(step, task) for task in wave]
            for lag, task in enumerate((weight_grad, sum_weights, cross_weights)):
                if lag and 0 <= w - first - lag < lay.chunks:
                    at = len(items) if lag < 2 else len(items) - len(wave)
                    items.insert(at, (step, lambda task=task, c=w - first - lag: task(c)))
            if w >= 3 and z_bits + w -3 < stages:
                items.append((step, lambda k=z_bits + w -3: lin_next(k)))
        for lag, task in ((1, sum_weights), (2, cross_weights)):
            items += [(last, lambda task=task, c=c: task(c))
                      for c in range(max(0, len(waves) - first - lag), lay.chunks)]
        items += [(last, lambda c=c: finish_weights(c)) for c in range(lay.chunks)]
        schedule(last, i, items)

        @pl.when(i == last)
        def _():
            ex.drain()
            d_stream.flush(plan.steps)
            for p in range(lay.chunks * plan.pieces):
                to_inner(p).wait_send()

                @pl.when(jnp.logical_not(at_end))
                def _(p=p):
                    to_outer(p).wait_send()

            for k in range(stages):
                lin_step(k).wait_send()

    acc = lay.acc_rows
    dma = pltpu.SemaphoreType.DMA
    return pl.pallas_call(
        kernel,
        grid=(plan.count,),
        in_specs=[
            ANYWHERE,
            plain_fields(plan)[1],
            ANYWHERE,
            plain_fields(plan)[1],
            fixed((W, 1024)),
            fixed((4, C, C)),
            fixed(spectrum.shape),
            fixed((W, W)),
            fixed((W, 128)),
            fixed(pick_all.shape),
            fixed(move_all.shape),
            fixed(move_lin.shape),
            fixed(zero_lanes.shape),
            ANYWHERE,
            ANYWHERE,
        ],
        out_specs=[
            ANYWHERE,
            plain_fields(plan)[1],
            ANYWHERE,
            fixed((lay.chunks * plan.wrows, 2 * W)),
            fixed((C + 8, W)),
        ],
        out_shape=[
            jax.ShapeDtypeStruct(p_big.shape, BF),
            jax.ShapeDtypeStruct(p_small.shape, BF),
            jax.ShapeDtypeStruct((plan.chips, 2, plan.by_pairs.total, 2 * W), BF),
            jax.ShapeDtypeStruct((lay.chunks * plan.wrows, 2 * W), BF),
            jax.ShapeDtypeStruct((C + 8, W), F32),
        ],
        scratch_shapes=[
            pltpu.VMEM((plan.chips, 2, plan.by_pairs.total, 2 * W), BF),
            pltpu.VMEM((W, W), BF),
            pltpu.VMEM((4, 2, acc, 128), F32),
            pltpu.VMEM((8, 2, acc, 128), F32),
            pltpu.VMEM((plan.wrows, 2 * W), BF),
            *[pltpu.VMEM((lay.chunks * plan.pieces, plan.zrows, 2 * W), BF)] * 5,
            pltpu.VMEM((stages, C + 8, W), F32),
            pltpu.VMEM((stages, C + 8, W), F32),
            dma((1 + lay.chunks,)),
            *[dma((lay.chunks * plan.pieces,))] * 5,
            dma((stages,)),
            dma((stages,)),
            *Stream.scratch(min(4, plan.steps), 2 * plan.per, big.cells),
            *Stream.scratch(min(4, plan.steps), 2 * plan.per, big.cells),
            *Stream.scratch(min(3, plan.steps), 2 * plan.per, big.cells),
            *Exchange.scratch(plan, lay),
        ],
        compiler_params=params(collective_id=2, has_side_effects=True),
        name="mode_backward",
    )(p_big, p_small, g_big, g_small, expand_tables(), lin_weight, spectrum, lin_grad, columns,
      pick_all, move_all, move_lin, zero_lanes, part, kernel_all)


def input_grads(plan, rank, part_big, part_small, modes, lin_sum, weights):
    big, small = plan.big, plan.small
    per, steps = plan.wide_per, plan.wide_steps
    last = steps - 1

    split = np.zeros((W, 4, 128), np.float32)
    for p in range(4):
        split[p * C : p * C + C, p, :C] = np.eye(C)
    split = split.reshape(W, 512)
    blades = np.zeros((2, 2 * W, 4, 128), np.float32)
    for odd in range(2):
        for lane in range(W):
            at = lane + 128 * odd if lane < 128 else 128 + 64 * odd + lane
            blades[odd, at, lane // C, lane % C] = 1.0
    blades = low(blades.reshape(2, 2 * W, 512))
    lay = plan.by_modes

    def body(r, pb, ps, mb, ms, vb, eb, vs, es, lin, cut, w_in, blade,
             db, ds, lin_out, bias_out, w_out, w_held, w_sem):
        i = pl.program_id(0)
        put = pltpu.make_async_copy(w_held, w_out, w_sem.at[0])

        @pl.when(i == 0)
        def _():
            v = lax.dot_general(
                lin[...], cut[...], (((1,), (0,)), ((), ())),
                precision=lax.Precision.HIGHEST, preferred_element_type=F32,
            )
            for p in range(4):
                lin_out[p] = v[:C, 128 * p : 128 * p + C]
                bias_out[p : p + 1, :] = v[C : C + 1, 128 * p : 128 * p + C]
            for c in range(lay.chunks):
                rows = w_in[c * plan.wrows : (c + 1) * plan.wrows, :]
                for odd in range(2):
                    v = dot(rows, blade[odd])
                    for j in range(lay.modes // 2):
                        for p in range(4):
                            w_held[lay.first_mode(c) + 2 * j + odd, p] = (
                                v[j * C : j * C + C, 128 * p : 128 * p + C]
                            )
            put.start()

        @pl.when(i == steps)
        def _():
            put.wait()

        def run(part, m, d, geo, inverse, spread, count):
            span = spread.shape[1]
            qs = []
            for pair in range(count):
                qs += inverse_pair(geo, load_by_modes(plan, m, pair), inverse[...], 1.0)
            q = jnp.concatenate(qs, axis=0) * jnp.asarray(1.0 / geo.side, BF)
            for j in range(geo.cells // span):
                v = dot(q[:, 128 * j : 128 * j + 128], spread[...])
                at = (slice(0, 2 * count), slice(None), slice(None),
                      slice(j * span, (j + 1) * span))
                d[at] = part[at].astype(F32) + v.reshape(2 * count, 4, C, span)

        @pl.when(i < steps)
        def _():
            run(pb, mb, db, big, vb, eb, per)

        @pl.when(i == steps)
        def _():
            run(ps, ms, ds, small, vs, es, plan.nsmall // 2)

    extra = [lin_sum, split, weights, blades]
    tables = []
    specs = []
    for geo in (big, small):
        tables += [geo.inverse, geo.spread]
        specs += [device_spec(geo.inverse.shape[1:]), const_spec(geo.spread.shape)]
    small_field = field_specs(plan)[1]
    big_field = pl.BlockSpec((2 * per, 4, C, big.cells), lambda i, r: (wide(i, last), 0, 0, 0))
    return pl.pallas_call(
        body,
        grid_spec=pltpu.PrefetchScalarGridSpec(
            num_scalar_prefetch=1,
            grid=(steps + 1,),
            in_specs=[
                big_field,
                small_field,
                pl.BlockSpec(
                    (plan.n, lay.chunks, per * lay.modes, 2 * W),
                    lambda i, r: (0, 0, wide(i, last), 0),
                ),
                pl.BlockSpec(
                    (plan.n, lay.chunks, plan.per * lay.modes, 2 * W),
                    lambda i, r: (0, 0, plan.steps, 0),
                ),
                *specs,
                *[const_spec(v.shape) for v in extra],
            ],
            out_specs=[big_field, small_field, const_spec((4, C, C)), const_spec((4, C)),
                       ANYWHERE],
            scratch_shapes=[
                pltpu.VMEM((plan.own, 4, C, C), F32), pltpu.SemaphoreType.DMA((1,))
            ],
        ),
        out_shape=[
            jax.ShapeDtypeStruct(part_big.shape, F32),
            jax.ShapeDtypeStruct(part_small.shape, F32),
            jax.ShapeDtypeStruct((4, C, C), F32),
            jax.ShapeDtypeStruct((4, C), F32),
            jax.ShapeDtypeStruct((plan.own, 4, C, C), F32),
        ],
        compiler_params=params(),
        name="input_grads",
    )(rank, part_big, part_small, modes, modes, *tables, *extra)


def on_device(plan, x_big, x_small, spec_weight, lin_weight, lin_bias, grad_big, grad_small):
    rank = lax.axis_index("rows").reshape(1)
    width = 2 * W
    modes, kernel, spectrum = forward_kernel(plan, x_big, x_small, spec_weight)
    out_big, out_small, pre_big, pre_small, part, lin_grad, columns = cells_pass(
        plan, rank, x_big, x_small, grad_big, grad_small, modes.reshape(plan.n, -1, width),
        lin_weight, lin_bias,
    )
    lay = plan.by_modes
    part_big, part_small, modes, weights, lin_sum = backward_kernel(
        plan, part.reshape((plan.chips, 2) + part.shape[1:]), pre_big, pre_small,
        grad_big, grad_small, kernel, spectrum.reshape(-1, plan.own, width), lin_weight,
        lin_grad, columns,
    )
    dx_big, dx_small, lin_weight_grad, lin_bias_grad, spec_grad = input_grads(
        plan, rank, part_big, part_small, modes.reshape(plan.n, lay.chunks, -1, width),
        lin_sum, weights,
    )
    return out_big, out_small, dx_big, dx_small, spec_grad, lin_weight_grad, lin_bias_grad


def solution(mesh):
    fields = P("samples", None, None, "rows")
    spec = P("rows", None, None, None)

    def run(x_big, x_small, *rest):
        count = mesh.shape["samples"]
        plan = Plan(mesh, x_big.shape[0] // count, x_small.shape[0] // count)

        def local(*args):
            return on_device(plan, *args)

        return jax.shard_map(
            local,
            mesh=mesh,
            in_specs=(fields, fields, spec, P(), P(), fields, fields),
            out_specs=(fields, fields, fields, fields, spec, P(), P()),
            check_vma=False,
        )(x_big, x_small, *rest)

    return run
```

```python
import math

import jax
import jax.numpy as jnp
import ml_dtypes
import numpy as np
from jax import lax
from jax.experimental import pallas as pl
from jax.experimental.pallas import tpu as pltpu
from jax.sharding import PartitionSpec as P

C = 48
MX = 16
N1 = 128
N2 = 64
W = 4 * C
MODES = MX * MX
BF = jnp.bfloat16
F32 = jnp.float32


def trig(side):
    a = np.arange(MX)
    freq = np.where(a < MX // 2, a, side - MX + a)
    phase = (np.arange(side)[:, None] * freq[None, :]) % side
    angle = phase.astype(np.float32) * np.float32(2.0 * math.pi / side)
    cos = np.cos(angle).astype(ml_dtypes.bfloat16).astype(np.float32)
    sin = np.sin(angle).astype(ml_dtypes.bfloat16).astype(np.float32)
    return cos, sin


def low(table):
    return table.astype(ml_dtypes.bfloat16)


class Geometry:
    def __init__(self, side, n):
        self.side = side
        self.rows = side // n
        self.cells = self.rows * side
        self.group = min(8, self.rows)
        self.ngroups = self.rows // self.group
        self.npairs = self.rows // 2
        self.qlanes = max(128, self.npairs * 64)
        self.hk = self.ngroups * 128
        cos, sin = trig(side)
        eye = np.eye(MX, dtype=np.float32)

        first = np.zeros((self.group, side, 256), np.float32)
        for h in range(self.group):
            first[h, :, h * MX : (h + 1) * MX] = cos
            first[h, :, 128 + h * MX : 128 + (h + 1) * MX] = sin
        self.first = low(first.reshape(self.group * side, 256))

        second = np.zeros((n, MX, MX, 2, self.ngroups, 128), np.float32)
        inverse = np.zeros((n, MX, MX, 2, self.qlanes), np.float32)
        for r in range(n):
            for h in range(self.rows):
                c, s = cos[r * self.rows + h], sin[r * self.rows + h]
                ce, se = c[:, None, None] * eye, s[:, None, None] * eye
                g, lane = h // self.group, (h % self.group) * MX
                second[r, :, :, 0, g, lane : lane + MX] = ce
                second[r, :, :, 1, g, lane : lane + MX] = se
                lane = h * 2 * MX
                inverse[r, :, :, 0, lane : lane + MX] = ce
                inverse[r, :, :, 0, lane + MX : lane + 2 * MX] = -se
                inverse[r, :, :, 1, lane : lane + MX] = -se
                inverse[r, :, :, 1, lane + MX : lane + 2 * MX] = -ce
        self.second = low(second.reshape(n, MODES, 2 * self.hk))
        inverse[..., MX : self.rows * 2 * MX : 2 * MX] = 0.0
        self.inverse = low(inverse.reshape(n, MODES, 2 * self.qlanes))

        spread = np.zeros((4, 2, MX, 4, side), np.float32)
        for h in range(4):
            spread[h, 0, :, h] = cos.T
            spread[h, 1, :, h] = sin.T
        self.spread = low(spread.reshape(128, 4 * side))
        if self.npairs == 1:
            self.spread = self.spread[:, : 2 * side]
        for h in range(4):
            spread[h, 1, 0, h] = 1.0
        self.pair_spread = low(spread.reshape(128, 4 * side))[:64, : 2 * side]


def turn(v):
    return jnp.concatenate([v[3 * C :], v[2 * C : 3 * C], -v[C : 2 * C], -v[:C]], axis=0)


def dot(a, b, dims=((1,), (0,))):
    return lax.dot_general(a, b, (dims, ((), ())), preferred_element_type=F32)


def forward_group(field, first, scale, keep=None):
    y = dot(field, first)
    grids = range(y.shape[0] // W)
    if keep is not None:
        keep(sum(y[W * s : W * s + W, :128] for s in grids))
    cols = []
    for s in grids:
        col = y[W * s : W * s + W, :128] + turn(y[W * s : W * s + W, 128:])
        cols.append((col * scale).astype(BF))
    return cols


def forward_rows(groups, second):
    stacked = []
    for s in range(2):
        cols = [cols[s] for cols in groups]
        stacked.append(jnp.concatenate(cols + [turn(col) for col in cols], axis=1))
    a, b = stacked
    both = jnp.concatenate([a[:128], b[:128], a[128:], b[128:]], axis=0)
    return dot(second, both, ((1,), (1,)))


def forward_grids(geo, get, first, second, scale):
    width = geo.group * geo.side
    groups = [forward_group(get(g * width, width), first, scale) for g in range(geo.ngroups)]
    return [
        forward_rows([cols[2 * k : 2 * k + 2] for cols in groups], second)
        for k in range(len(groups[0]) // 2)
    ]


def inverse_pair(geo, modes, inverse, scale):
    uv = dot(modes, inverse, ((0,), (0,)))
    result = []
    for s in range(2):
        part = jnp.concatenate(
            [uv[128 * s : 128 * s + 128], uv[256 + 64 * s : 320 + 64 * s]], axis=0
        )
        q = part[:, : geo.qlanes] + turn(part[:, geo.qlanes :])
        result.append((q * scale).astype(BF))
    return result


def fold_tables():
    dup = np.concatenate([np.arange(192), np.arange(128, 192)])
    pick = np.zeros((192, 4, 128), np.float32)
    move = np.zeros((192, 4, 192), np.float32)
    for q in range(4):
        pick[q * C : q * C + C, q, :C] = np.eye(C)
        for p in range(4):
            sign = -1.0 if (p >> 1) & q & 1 else 1.0
            o = p ^ q
            move[o * C : o * C + C, q, p * C : p * C + C] = sign * np.eye(C)
    return (
        low(pick[dup].reshape(256, 512)),
        low(move[dup][:, :, dup].reshape(256, 1024)),
        move.transpose(1, 0, 2).copy(),
    )


def expand_tables():
    dup = np.concatenate([np.arange(192), np.arange(128, 192)])
    place = np.zeros((4, C, 4, 256), np.float32)
    for p in range(4):
        for q in range(4):
            sign = -1.0 if (p >> 1) & q & 1 else 1.0
            full = np.zeros((C, 192), np.float32)
            o = p ^ q
            full[:, o * C : (o + 1) * C] = sign * np.eye(C)
            place[p, :, q] = full[:, dup]
    return low(place.reshape(W, 1024))


class Layout:
    def __init__(self, chunks, pairs, modes, by_mode):
        self.chunks, self.pairs, self.modes, self.by_mode = chunks, pairs, modes, by_mode
        self.crow = pairs * modes
        first = -(-self.crow // 32) * 16
        self.halves = (first, self.crow - first)
        self.slots = -(-pairs // 8) * 8
        self.acc_rows = self.slots * modes
        self.total = chunks * self.crow

    def first_mode(self, c):
        return c * self.modes if self.by_mode else 0


class Plan:
    def __init__(self, mesh, nbig, nsmall):
        self.n = mesh.shape["rows"]
        self.nz = mesh.shape["samples"]
        self.own = MODES // self.n
        self.per = max(1, 16 // self.own)
        self.big = Geometry(N1, self.n)
        self.small = Geometry(N2, self.n)
        self.nbig, self.nsmall = nbig, nsmall
        assert nbig % (2 * self.per) == 0 and nsmall % 2 == 0 and nsmall // 2 <= self.per
        self.steps = nbig // (2 * self.per)
        self.count = self.steps + 1
        self.wide_per = 2 * self.per if self.steps % 2 == 0 else self.per
        self.wide_steps = nbig // (2 * self.wide_per)
        self.block = self.per * self.own
        self.total = self.count * self.block
        pairs = self.count * self.per
        parts = next(c for c in (3, 2, 1) if self.count % c == 0)
        self.by_pairs = Layout(parts, pairs // parts, self.own, False)
        parts = max(1, self.own // 16)
        self.by_modes = Layout(parts, pairs, self.own // parts, True)
        self.chips = self.n // 2
        bits = list(range(1, self.n.bit_length() - 1))
        self.orders = (bits, bits[::-1])
        self.levels = len(bits)
        self.wrows = self.by_modes.modes // 2 * C
        self.pieces = 6
        self.zrows = self.wrows // self.pieces
        assert self.nz % 2 == 0 and self.zrows % 16 == 0

    def mask(self, h, idx):
        m = 0
        for t, b in enumerate(self.orders[h]):
            if idx >> (self.levels - 1 - t) & 1:
                m |= 1 << b
        return m


def wide(i, last):
    return jnp.minimum(i, last)


def params(**kw):
    return pltpu.CompilerParams(vmem_limit_bytes=56 * 1024 * 1024, **kw)


def const_spec(shape):
    return pl.BlockSpec(shape, lambda i, r: (0,) * len(shape))


def device_spec(shape):
    return pl.BlockSpec((None,) + shape, lambda i, r: (r[0],) + (0,) * len(shape))


def field_specs(plan):
    big, small = plan.big, plan.small
    last = plan.steps - 1
    return (
        pl.BlockSpec((2 * plan.per, 4, C, big.cells), lambda i, r: (wide(i, last), 0, 0, 0)),
        pl.BlockSpec((plan.nsmall, 4, C, small.cells), lambda i, r: (0, 0, 0, 0)),
    )


def mode_spec(plan):
    return pl.BlockSpec((plan.n, plan.block, 2 * W), lambda i, r: (0, i, 0))


def store_by_modes(plan, ref, pair, z):
    lay = plan.by_modes
    z = z.reshape(plan.n, lay.chunks, lay.modes, 2 * W).astype(BF)
    ref[:, :, pair * lay.modes : (pair + 1) * lay.modes, :] = z


def load_by_modes(plan, ref, pair):
    lay = plan.by_modes
    return ref[:, :, pair * lay.modes : (pair + 1) * lay.modes, :].reshape(MODES, 2 * W)


def load_modes(plan, ref, pair):
    return ref[:, pair * plan.own : (pair + 1) * plan.own, :].reshape(MODES, 2 * W)


def flip(index, mask):
    result = index
    for b in range(mask.bit_length()):
        if mask >> b & 1:
            bit = lax.rem(lax.div(index, 1 << b), 2)
            result = result + (1 - 2 * bit) * (1 << b)
    return result


def tiles(v):
    return [v[:, 128 * t : 128 * t + 128] for t in range(v.shape[1] // 128)]


def sample_rows(first, second, third):
    lane = lax.broadcasted_iota(jnp.int32, third.shape, 1)
    a = jnp.concatenate([first, jnp.where(lane < 64, third, 0.0)], axis=1)
    b = jnp.concatenate([second, jnp.where(lane < 64, 0.0, third)], axis=1)
    return jnp.concatenate([a, b], axis=0)


def pair_tiles(a, b):
    lane = lax.broadcasted_iota(jnp.int32, (a.shape[0], 128), 1)
    return a[:, :128], b[:, :128], jnp.where(lane < 64, a[:, 128:], b[:, 128:])


def remote(src, dst, send, recv, device):
    return pltpu.make_async_remote_copy(
        src_ref=src, dst_ref=dst, send_sem=send, recv_sem=recv, device_id=device
    )


class Stream:
    def __init__(self, field, ring, sems, grids):
        self.field, self.ring, self.sems, self.grids = field, ring, sems, grids
        self.depth = ring.shape[0]

    @staticmethod
    def scratch(depth, grids, cells):
        return [pltpu.VMEM((depth, grids, 4, C, cells), BF), pltpu.SemaphoreType.DMA((depth,))]

    def slot(self, i):
        return self.ring.at[lax.rem(i, self.depth)]

    def copy(self, i, out=False):
        block = self.field.at[pl.ds(i * self.grids, self.grids)]
        sem = self.sems.at[lax.rem(i, self.depth)]
        if out:
            return pltpu.make_async_copy(self.slot(i), block, sem)
        return pltpu.make_async_copy(block, self.slot(i), sem)

    def read(self, i, count):
        @pl.when(i == 0)
        def _():
            for k in range(min(self.depth, count)):
                self.copy(jnp.int32(k)).start()

        self.copy(i).wait()
        return self.slot(i)

    def ahead(self, i, count):
        @pl.when(i + self.depth < count)
        def _():
            self.copy(i + self.depth).start()

    def reserve(self, i):
        @pl.when(i >= self.depth)
        def _():
            self.copy(i - self.depth, True).wait()

        return self.slot(i)

    def flush(self, count):
        for k in range(max(0, count - self.depth), count):
            self.copy(jnp.int32(k), True).wait()


class Exchange:
    @staticmethod
    def scratch(plan, lay):
        chips, width = plan.chips, 2 * W
        dma = pltpu.SemaphoreType.DMA
        part = (lay.chunks, 2)
        moving = (2, chips, lay.chunks * lay.halves[0], width)
        return [
            pltpu.VMEM((chips, lay.total, width), BF),
            pltpu.VMEM(moving, BF),
            pltpu.VMEM(moving, BF),
            pltpu.VMEM((chips, 2, lay.total, width), BF),
            pltpu.VMEM((3, lay.acc_rows, 128), F32),
            pltpu.VMEM((3, lay.acc_rows, 128), F32),
            dma((lay.chunks,)),
            dma((lay.chunks,)),
            dma(part + (plan.levels,)),
            dma(part + (plan.levels,)),
            dma(part + (chips,)),
            dma(part + (chips,)),
            dma(part + (chips,)),
            dma(part + (chips,)),
            dma((lay.chunks,)),
            pltpu.VMEM((plan.own, 256, 256), BF),
        ]

    def __init__(self, plan, lay, part, out, refs, origin):
        self.plan, self.lay, self.part, self.out, self.origin = plan, lay, part, out, origin
        (self.sib, self.sums, self.lev, self.res, self.acc, self.mixed,
         self.sib_s, self.sib_r, self.lev_s, self.lev_r, self.ag_s, self.ag_r,
         self.fw_s, self.fw_r, self.out_s, self.kernel) = refs
        self.me = lax.axis_index("rows")
        self.core = lax.rem(self.me, 2)

    def partners(self):
        return [flip(self.me, 1 << b) for b in range(self.plan.n.bit_length() - 1)]

    def chunk(self, c):
        return pl.ds(c * self.lay.crow, self.lay.crow)

    def rows(self, c, h):
        return pl.ds(c * self.lay.crow + h * self.lay.halves[0], self.lay.halves[h])

    def moving(self, c, h):
        return pl.ds(c * self.lay.halves[0], self.lay.halves[h])

    def to_sibling(self, c):
        return remote(
            self.origin(c, 1 - self.core), self.sib.at[:, self.chunk(c), :],
            self.sib_s.at[c], self.sib_r.at[c], {"rows": flip(self.me, 1)},
        )

    def level(self, c, h, t):
        plan = self.plan
        count = plan.chips >> (t + 1)
        rows = self.moving(c, h)
        at = plan.chips - 2 * count
        return remote(
            self.sums.at[h, pl.ds(count, count), rows, :],
            self.lev.at[h, pl.ds(at, count), rows, :],
            self.lev_s.at[c, h, t], self.lev_r.at[c, h, t],
            {"rows": flip(self.me, 1 << plan.orders[h][t])},
        )

    def block(self, c, h, owner):
        return self.res.at[lax.div(owner, 2), lax.rem(owner, 2), self.rows(c, h), :]

    def gather(self, c, h, u, idx):
        plan = self.plan
        sem = (1 << u) - 1 + idx
        ref = self.block(c, h, flip(self.me, plan.mask(h, idx)))
        return remote(
            ref, ref, self.ag_s.at[c, h, sem], self.ag_r.at[c, h, sem],
            {"rows": flip(self.me, 1 << plan.orders[h][plan.levels - 1 - u])},
        )

    def forward(self, c, h, idx):
        ref = self.block(c, h, flip(self.me, self.plan.mask(h, idx)))
        return remote(
            ref, ref, self.fw_s.at[c, h, idx], self.fw_r.at[c, h, idx],
            {"rows": flip(self.me, 1)},
        )

    def store(self, c):
        rows = self.chunk(c)
        return pltpu.make_async_copy(
            self.res.at[:, :, rows, :], self.out.at[:, :, rows, :], self.out_s.at[c]
        )

    def begin(self, c):
        self.to_sibling(c).start()

    def add_sibling(self, c):
        plan = self.plan
        self.to_sibling(c).wait_recv()
        for far in (1, 0):
            for h in range(2):
                span = plan.chips // 2
                for idx in range(far * span, far * span + span):
                    owner = flip(self.me, plan.mask(h, idx))
                    chip = lax.div(owner, 2)
                    rows = self.rows(c, h)
                    v = self.part[chip, self.core, rows, :].astype(F32)
                    v = v + self.sib[chip, rows, :].astype(F32)
                    self.sums[h, idx, self.moving(c, h), :] = v.astype(BF)
                if far:
                    self.level(c, h, 0).start()

    def next_level(self, c, t):
        plan = self.plan
        count = plan.chips >> t
        at = plan.chips - 2 * count
        for h in range(2):
            rows = self.moving(c, h)
            self.level(c, h, t - 1).wait_recv()
            for idx in reversed(range(count)):
                v = self.sums[h, idx, rows, :].astype(F32)
                v = v + self.lev[h, at + idx, rows, :].astype(F32)
                self.sums[h, idx, rows, :] = v.astype(BF)
                if idx == count // 2:
                    self.level(c, h, t).start()

    def finish_sum(self, c, scale):
        plan, lay = self.plan, self.lay
        for h in range(2):
            rows = self.moving(c, h)
            self.level(c, h, plan.levels - 1).wait_recv()
            v = self.sums[h, 0, rows, :].astype(F32)
            v = (v + self.lev[h, plan.chips - 2, rows, :].astype(F32)) * scale
            at = h * lay.halves[0]
            for t, tile in enumerate(tiles(v)):
                self.acc[t, at : at + lay.halves[h], :] = tile

    def mix(self, c, dims):
        lay = self.lay

        def one(m):
            rows = pl.ds(m, lay.slots, stride=lay.modes)
            lhs = sample_rows(*(self.acc[t, rows, :] for t in range(3))).astype(BF)
            res = dot(lhs, self.kernel[lay.first_mode(c) + m], dims)
            for t, tile in enumerate(pair_tiles(res[: lay.slots], res[lay.slots :])):
                self.mixed[t, rows, :] = tile

        unroll = 8

        @pl.loop(0, lay.modes // unroll)
        def _(j):
            for u in range(unroll):
                one(j * unroll + u)

        result = jnp.concatenate([self.mixed[t, : lay.crow, :] for t in range(3)], axis=1)
        self.res[lax.div(self.me, 2), self.core, self.chunk(c), :] = result.astype(BF)
        for h in range(2):
            self.gather(c, h, 0, 0).start()
            self.forward(c, h, 0).start()

    def spread(self, c, u):
        for h in range(2):
            got = 1 << (u - 1)
            for idx in range(got):
                self.gather(c, h, u - 1, idx).wait_recv()
            if u < self.plan.levels:
                for idx in reversed(range(2 * got)):
                    self.gather(c, h, u, idx).start()
            for idx in range(got, 2 * got):
                self.forward(c, h, idx).start()

    def close(self, c):
        for h in range(2):
            for idx in range(self.plan.chips):
                self.forward(c, h, idx).wait_recv()
        self.store(c).start()

    def drain(self):
        plan = self.plan
        for c in range(self.lay.chunks):
            self.to_sibling(c).wait_send()
            for h in range(2):
                for t in range(plan.levels):
                    self.level(c, h, t).wait_send()
                for u in range(plan.levels):
                    for idx in range(1 << u):
                        self.gather(c, h, u, idx).wait_send()
                for idx in range(plan.chips):
                    self.forward(c, h, idx).wait_send()
            self.store(c).wait()

    def clear(self):
        lay = self.lay
        if lay.acc_rows > lay.crow:
            self.acc[:, lay.crow :, :] = jnp.zeros((3, lay.acc_rows - lay.crow, 128), F32)

    def waves(self, total):
        plan, chunks = self.plan, self.lay.chunks
        todo = []
        for c in range(chunks):
            chain = [lambda c=c, t=t: self.next_level(c, t) for t in range(1, plan.levels)]
            chain += [lambda c=c: total(c)]
            chain += [lambda c=c, u=u: self.spread(c, u) for u in range(1, plan.levels + 1)]
            chain += [lambda c=c: self.close(c)]
            todo.append(chain)
        waves = []
        for w in range(len(todo[0]) + chunks - 1):
            at = [(c, w - c) for c in reversed(range(chunks))]
            waves.append([todo[c][k] for c, k in at if 0 <= k < len(todo[c])])
        return waves


def greet(devices):
    barrier = pltpu.get_barrier_semaphore()
    for device in devices:
        pl.semaphore_signal(barrier, inc=1, device_id=device)
    pl.semaphore_wait(barrier, len(devices))


def build_modes(plan, place, weights, kernel):
    flat = jnp.concatenate([weights[:, p].reshape(-1, C) for p in range(4)], axis=1)
    for q in range(4):
        rows = dot(flat, place[:, 256 * q : 256 * q + 256])
        kernel[:, C * q : C * q + C, :] = rows.astype(BF).reshape(plan.own, C, 256)
    kernel[:, W:, :] = kernel[:, 128:W, :]


def build_lin(place, weight):
    flat = jnp.concatenate([weight[p] for p in range(4)], axis=1)
    rows = [dot(flat, place[:, 256 * q : 256 * q + 256]) for q in range(4)]
    return jnp.concatenate(rows, axis=0).astype(BF)


def half_tables():
    rows = np.zeros((192, 384), np.float32)
    rows[:128, :128] = 0.5 * np.eye(128)
    rows[128:, 192:256] = 0.5 * np.eye(64)
    rows[128:, 256:320] = 0.5 * np.eye(64)
    line = np.zeros((128, C), np.float32)
    line[MX :: 2 * MX] = 0.5
    return low(rows), low(line), low(np.eye(C, dtype=np.float32))


def plain_fields(plan):
    big, small = plan.big, plan.small
    last = plan.steps - 1
    return [
        pl.BlockSpec((2 * plan.per, 4, C, big.cells), lambda i: (wide(i, last), 0, 0, 0)),
        pl.BlockSpec((plan.nsmall, 4, C, small.cells), lambda i: (0, 0, 0, 0)),
    ]


def fixed(shape):
    return pl.BlockSpec(shape, lambda i: (0,) * len(shape))


ANYWHERE = pl.BlockSpec(memory_space=pl.ANY)


def forward_kernel(plan, x_big, x_small, spec_weight):
    big, small = plan.big, plan.small
    lay = plan.by_pairs
    last = plan.wide_steps

    def kernel(x_hbm, xs, fb, fs, place, weights, sb_all, ss_all, out, kernel_out, spectrum,
               part, sb, ss, table_sem, ring, ring_sem, *refs):
        i = pl.program_id(0)
        stream = Stream(x_hbm, ring, ring_sem, 2 * plan.wide_per)
        ex = Exchange(plan, lay, part, out, refs, lambda c, core: part.at[
            :, core, pl.ds(c * lay.crow, lay.crow), :
        ])
        loads = [
            pltpu.make_async_copy(sb_all.at[ex.me], sb, table_sem.at[0]),
            pltpu.make_async_copy(ss_all.at[ex.me], ss, table_sem.at[1]),
        ]
        keep = pltpu.make_async_copy(ex.kernel, kernel_out, table_sem.at[2])

        @pl.when(i == 0)
        def _():
            for load in loads:
                load.start()
            greet([{"rows": d} for d in ex.partners()])
            ex.clear()
            for load in loads:
                load.wait()

        def run(x, geo, first, second, count, per):
            def get(start, width):
                v = x[: 2 * count, :, :, start : start + width]
                return v.reshape(2 * count * W, width)

            zs = forward_grids(geo, get, first[...], second[...], 1.0 / geo.side)
            parts = [z.reshape(plan.chips, 2, plan.own, 2 * W) for z in zs]
            parts += [jnp.zeros_like(parts[0])] * (per - count)
            z = jnp.concatenate(parts, axis=2) if per > 1 else parts[0]
            rows = pl.ds(pl.multiple_of(i * plan.wide_per * plan.own, 16), per * plan.own)
            part[:, :, rows, :] = z.astype(BF)

        @pl.when(i < last)
        def _():
            run(stream.read(i, last), big, fb, sb, plan.wide_per, plan.wide_per)
            stream.ahead(i, last)

        @pl.when(i == last)
        def _():
            run(xs, small, fs, ss, plan.nsmall // 2, plan.per)

        def total(c):
            ex.finish_sum(c, 1.0)
            spectrum[ex.chunk(c), :] = jnp.concatenate(
                [ex.acc[t, : lay.crow, :] for t in range(3)], axis=1
            ).astype(BF)
            ex.mix(c, ((1,), (0,)))

        def prepare():
            build_modes(plan, place, weights, ex.kernel)
            keep.start()

        waves = ex.waves(total)
        items = []
        for c in range(lay.chunks):
            pairs = (c + 1) * lay.pairs
            end = min(-(-pairs // plan.wide_per) - 1, last)
            items.append((end, lambda c=c: ex.begin(c)))
            if c == lay.chunks - 1:
                items.append((last, prepare))
                items += [(last, task) for task in waves.pop(0)]
            items.append((min(end + 1, last), lambda c=c: ex.add_sibling(c)))
        items += [(last, task) for wave in waves for task in wave]
        schedule(last, i, items)

        @pl.when(i == last)
        def _():
            ex.drain()
            keep.wait()

    return pl.pallas_call(
        kernel,
        grid=(last + 1,),
        in_specs=[
            ANYWHERE,
            plain_fields(plan)[1],
            fixed(big.first.shape),
            fixed(small.first.shape),
            fixed((W, 1024)),
            fixed(spec_weight.shape),
            ANYWHERE,
            ANYWHERE,
        ],
        out_specs=[ANYWHERE, ANYWHERE, fixed((plan.by_pairs.total, 2 * W))],
        out_shape=[
            jax.ShapeDtypeStruct((plan.chips, 2, plan.by_pairs.total, 2 * W), BF),
            jax.ShapeDtypeStruct((plan.own, 256, 256), BF),
            jax.ShapeDtypeStruct((plan.by_pairs.total, 2 * W), BF),
        ],
        scratch_shapes=[
            pltpu.VMEM((plan.chips, 2, plan.by_pairs.total, 2 * W), BF),
            pltpu.VMEM(big.second.shape[1:], BF),
            pltpu.VMEM(small.second.shape[1:], BF),
            pltpu.SemaphoreType.DMA((3,)),
            *Stream.scratch(min(4, last), 2 * plan.wide_per, big.cells),
            *Exchange.scratch(plan, plan.by_pairs),
        ],
        compiler_params=params(collective_id=1, has_side_effects=True),
        name="mode_forward",
    )(x_big, x_small, big.first, small.first, expand_tables(), spec_weight,
      big.second, small.second)


def schedule(last, i, items):
    for step in range(last + 1):
        now = [task for when, task in items if min(when, last) == step]
        if now:
            @pl.when(i == step)
            def _(now=now):
                for task in now:
                    task()


def cells_pass(plan, rank, x_big, x_small, g_big, g_small, modes, lin_weight,
               lin_bias):
    k0 = math.sqrt(2.0 / math.pi)
    k1 = k0 * 0.044715

    def low_of(value):
        return jnp.asarray(value, BF)

    per, steps = plan.wide_per, plan.wide_steps
    last = steps - 1

    def body(r, xb, xs, gb, gs, m, m_next, ms, fb, sb, vb, eb, fs, ss, vs, es,
             place, rows_table, line, eye, lw, lb, ob, os_, pb, ps, z, lin_acc, y_acc,
             kt, bias_ref, q_next):
        i = pl.program_id(0)

        @pl.when(i == 0)
        def _():
            full = build_lin(place[...], lw)[:, :W]
            kt[...] = dot(full, rows_table[...], ((0,), (0,))).astype(BF)
            for q in range(4):
                bias_ref[C * q : C * q + C, :] = dot(
                    eye[...], line[...] * lb[q : q + 1, :], ((1,), (1,))
                ).astype(BF)
            lin_acc[...] = jnp.zeros_like(lin_acc)
            y_acc[...] = jnp.zeros_like(y_acc)

        def coefficients(geo, m, pair, inverse):
            qs = inverse_pair(geo, load_modes(plan, m, pair), inverse[...], 0.5 / MX)
            line = jnp.concatenate([bias_ref[...]] * (geo.qlanes // 128), axis=1)
            return [q + line for q in qs]

        def prepare(m):
            for s, q in enumerate(coefficients(plan.big, m, 0, vb)):
                q_next[s] = q

        @pl.when(i == 0)
        def _():
            prepare(m)

        def run(x, g, o, d, m, z, geo, first, second, inverse, spread, count, following=None):
            wide_cells = 2 * geo.side
            lane = lax.broadcasted_iota(jnp.int32, (W, 128), 1)
            held, groups = {}, {}

            def rows_back(pair):
                held[2 * pair], held[2 * pair + 1] = coefficients(geo, m, pair, inverse)

            def main(at, p):
                lo = p * wide_cells
                cells = slice(lo, lo + wide_cells)
                q = held[at][:, 128 * (p // 2) : 128 * (p // 2) + 128]
                xv = x[at, :, :, cells].reshape(W, wide_cells)
                if p % 2 == 0:
                    tail = jnp.where(lane < 64, q, kt[:, 128:256])
                    rhs = [xv[:128], spread[...], xv[128:]]
                else:
                    tail = jnp.where(lane >= 64, q, kt[:, 256:384])
                    rhs = [xv[:128], xv[128:], spread[...]]
                lhs = jnp.concatenate([kt[:, :128], tail], axis=1)
                b = dot(lhs, jnp.concatenate(rhs, axis=0))
                b = b.astype(BF)
                b2 = b * b
                e = low_of(1.0) + jnp.tanh(b * (low_of(2.0 * k0) + low_of(8.0 * k1) * b2))
                o[at, :, :, cells] = (xv + b * e).reshape(4, C, wide_cells)
                rise = b * (low_of(k0) + low_of(12.0 * k1) * b2)
                slope = e * (low_of(0.5) + rise * (low_of(2.0) - e))
                gv = g[at, :, :, cells].reshape(W, wide_cells)
                d[at, :, :, cells] = (gv * slope).reshape(4, C, wide_cells)

            def weight_grad(at, part):
                span = geo.cells // 2
                xa = x[at, :, :, part * span : part * span + span].reshape(W, span)
                pa = d[at, :, :, part * span : part * span + span].reshape(W, span)
                lin_acc[...] += dot(xa, pa, ((1,), (1,)))

            def keep(y):
                y_acc[...] += y

            def columns(pair, k):
                width = geo.group * geo.side
                v = d[2 * pair : 2 * pair + 2, :, :, k * width : k * width + width]
                cols = forward_group(v.reshape(2 * W, width), first[...], 1.0, keep)
                groups.setdefault(pair, []).append(cols)

            def rows_out(pair):
                store_by_modes(plan, z, pair, forward_rows(groups[pair], second[...]))

            side = []
            if following is None:
                rows_back(0)
            else:
                for s in range(2):
                    held[s] = q_next.at[s]
            for at in range(2 * count):
                pair = at // 2
                if at % 2 == 0 and pair + 1 < count:
                    side.append(lambda pair=pair: rows_back(pair + 1))
                if at == 2 and following is not None:
                    side.append(following)
                done = 0
                for p in range(geo.npairs):
                    main(at, p)
                    if side:
                        side.pop(0)()
                    if 2 * (p + 1) == geo.npairs:
                        side.append(lambda at=at: weight_grad(at, 0))
                    if at % 2 == 1 and (p + 1) * geo.ngroups // geo.npairs > done:
                        side.append(lambda pair=pair, k=done: columns(pair, k))
                        done += 1
                if geo.npairs == 1:
                    side.append(lambda at=at: weight_grad(at, 0))
                side.append(lambda at=at: weight_grad(at, 1))
                if at % 2 == 1:
                    side.append(lambda pair=pair: rows_out(pair))
            for task in side:
                task()

        @pl.when(i < steps)
        def _():
            run(xb, gb, ob, pb, m, z, plan.big, fb, sb, vb, eb, per,
                lambda: prepare(m_next))

        @pl.when(i == steps)
        def _():
            if plan.nsmall // 2 < per:
                z[...] = jnp.zeros_like(z)
            run(xs, gs, os_, ps, ms, z, plan.small, fs, ss, vs, es, plan.nsmall // 2)

    big, small = plan.big, plan.small
    tables = []
    specs = []
    for geo in (big, small):
        tables += [geo.first, geo.second, geo.inverse, geo.pair_spread]
        specs += [
            const_spec(geo.first.shape),
            device_spec(geo.second.shape[1:]),
            device_spec(geo.inverse.shape[1:]),
            const_spec(geo.pair_spread.shape),
        ]
    extra = [expand_tables(), *half_tables(), lin_weight, lin_bias]
    small_field = field_specs(plan)[1]
    big_field = pl.BlockSpec((2 * per, 4, C, big.cells), lambda i, r: (wide(i, last), 0, 0, 0))
    rows = per * plan.own
    lay = plan.by_modes
    return pl.pallas_call(
        body,
        grid_spec=pltpu.PrefetchScalarGridSpec(
            num_scalar_prefetch=1,
            grid=(steps + 1,),
            in_specs=[
                big_field,
                small_field,
                big_field,
                small_field,
                pl.BlockSpec((plan.n, rows, 2 * W), lambda i, r: (0, wide(i, last), 0)),
                pl.BlockSpec(
                    (plan.n, plan.own, 2 * W), lambda i, r: (0, wide(i + 1, last) * per, 0)
                ),
                pl.BlockSpec((plan.n, plan.block, 2 * W), lambda i, r: (0, plan.steps, 0)),
                *specs,
                *[const_spec(v.shape) for v in extra],
            ],
            out_specs=[
                big_field,
                small_field,
                big_field,
                small_field,
                pl.BlockSpec(
                    (plan.n, lay.chunks, per * lay.modes, 2 * W), lambda i, r: (0, 0, i, 0)
                ),
                const_spec((W, W)),
                const_spec((W, 128)),
            ],
            scratch_shapes=[
                pltpu.VMEM((W, 2 * W), BF),
                pltpu.VMEM((W, 128), BF),
                pltpu.VMEM((2, W, big.qlanes), BF),
            ],
        ),
        out_shape=[
            jax.ShapeDtypeStruct(x_big.shape, BF),
            jax.ShapeDtypeStruct(x_small.shape, BF),
            jax.ShapeDtypeStruct(x_big.shape, BF),
            jax.ShapeDtypeStruct(x_small.shape, BF),
            jax.ShapeDtypeStruct(
                (plan.n, lay.chunks, (steps + 1) * per * lay.modes, 2 * W), BF
            ),
            jax.ShapeDtypeStruct((W, W), F32),
            jax.ShapeDtypeStruct((W, 128), F32),
        ],
        compiler_params=params(),
        name="cells",
    )(rank, x_big, x_small, g_big, g_small, modes, modes, modes, *tables, *extra)


def backward_kernel(plan, part, p_big, p_small, g_big, g_small, kernel_all, spectrum,
                    lin_weight, lin_grad, columns):
    big, small = plan.big, plan.small
    lay = plan.by_modes
    stages = plan.n.bit_length() - 1 + plan.nz.bit_length() - 1
    z_bits = plan.nz.bit_length() - 1
    pick_all, move_all, move_lin = fold_tables()
    zero_lanes = np.zeros((8, 128), np.float32)
    zero_lanes[0, ::MX] = 1.0

    def kernel(pb, ps, gb, gs, place, lw, spec, lin_in, col_in, pick, move, shift, line, part_in, kernel_in,
               db, ds, out, weight_out, lin_out,
               part, kk, sa, mb, w_rows, w_part, w_sum, w_recv, w_cross, w_full, lin_buf, lin_recv,
               in_sem, zs, zr, zc, zos, zor, ls, lr, p_ring, p_sem, g_ring, g_sem, d_ring, d_sem, *refs):
        i = pl.program_id(0)
        p_stream = Stream(pb, p_ring, p_sem, 2 * plan.per)
        g_stream = Stream(gb, g_ring, g_sem, 2 * plan.per)
        d_stream = Stream(db, d_ring, d_sem, 2 * plan.per)
        ex = Exchange(plan, lay, part, out, refs, lambda c, core: part_in.at[
            :, core, c, pl.ds(0, lay.crow), :
        ])
        here = lax.axis_index("samples")
        loads = [
            pltpu.make_async_copy(
                part_in.at[:, :, c, pl.ds(0, lay.crow), :], part.at[:, :, ex.chunk(c), :],
                in_sem.at[1 + c],
            )
            for c in range(lay.chunks)
        ]
        load_kernel = pltpu.make_async_copy(kernel_in, ex.kernel, in_sem.at[0])

        left = here < plan.nz // 2
        place_z = jnp.where(left, here, plan.nz - 1 - here)
        at_end = place_z == 0
        at_middle = place_z == plan.nz // 2 - 1
        inward = {"samples": jnp.where(left, here + 1, here - 1)}
        outward = {"samples": jnp.where(left, here - 1, here + 1)}

        def to_inner(p):
            return remote(w_sum.at[p], w_recv.at[p], zs.at[p], zr.at[p], inward)

        def across(p):
            return remote(w_sum.at[p], w_cross.at[p], zs.at[p], zc.at[p], inward)

        def to_outer(p):
            return remote(w_full.at[p], w_full.at[p], zos.at[p], zor.at[p], outward)

        def send_inward(p):
            @pl.when(at_middle)
            def _():
                across(p).start()

            @pl.when(jnp.logical_not(at_middle))
            def _():
                to_inner(p).start()

        def lin_partner(k):
            if k < z_bits:
                return {"samples": flip(here, 1 << k)}
            return {"rows": flip(ex.me, 1 << (k - z_bits))}

        def lin_step(k):
            return remote(lin_buf.at[k], lin_recv.at[k], ls.at[k], lr.at[k], lin_partner(k))

        @pl.when(i == 0)
        def _():
            for load in loads:
                load.start()
            load_kernel.start()
            greet([{"rows": d} for d in ex.partners()]
                  + [{"samples": lax.rem(here + d, plan.nz)} for d in range(1, plan.nz)])
            for c in range(lay.chunks):
                ex.begin(c)
            folded = None
            for q in range(4):
                term = lax.dot_general(
                    lin_in[C * q : C * q + C, :], shift[q], (((1,), (0,)), ((), ())),
                    precision=lax.Precision.HIGHEST, preferred_element_type=F32,
                )
                folded = term if folded is None else folded + term
            lin_buf[0, :C, :] = folded
            lin_buf[0, C:, :] = lax.dot_general(
                line[...], col_in[...], (((1,), (1,)), ((), ())),
                precision=lax.Precision.HIGHEST, preferred_element_type=F32,
            )
            lin_step(0).start()
            kk[...] = build_lin(place[...], lw)[:, :W]
            for c, load in enumerate(loads):
                load.wait()
                ex.add_sibling(c)
            ex.clear()
            if lay.acc_rows > lay.crow:
                rest = lay.acc_rows - lay.crow
                sa[:, :, lay.crow :, :] = jnp.zeros((4, 2, rest, 128), F32)
                mb[:, :, lay.crow :, :] = jnp.zeros((8, 2, rest, 128), F32)
            load_kernel.wait()

        def run(p, g, d, geo, count):
            for at in range(2 * count):
                v = dot(kk[...], p[at, :, :, :].reshape(W, geo.cells))
                v = g[at, :, :, :].reshape(W, geo.cells) + v.astype(BF)
                d[at, :, :, :] = v.reshape(4, C, geo.cells)

        @pl.when(i < plan.steps)
        def _():
            p = p_stream.read(i, plan.steps)
            g = g_stream.read(i, plan.steps)
            run(p, g, d_stream.reserve(i), big, plan.per)
            d_stream.copy(i, True).start()
            p_stream.ahead(i, plan.steps)
            g_stream.ahead(i, plan.steps)

        @pl.when(i == plan.steps)
        def _():
            run(ps, gs, ds, small, plan.nsmall // 2)

        def weight_grad(c):
            crow, modes = lay.crow, lay.modes
            grads = sample_rows(*(ex.acc[t, :crow, :] for t in range(3))).astype(BF)
            held = spec[:, lay.first_mode(c) : lay.first_mode(c) + modes, :]
            spectra = sample_rows(*tiles(held.reshape(crow, 2 * W).astype(F32))).astype(BF)
            for t, tile in enumerate(tiles(dot(spectra, pick[...]))):
                sa[t, 0, :crow, :] = tile[:crow]
                sa[t, 1, :crow, :] = tile[crow:]
            for t, tile in enumerate(tiles(dot(grads, move[...]))):
                mb[t, 0, :crow, :] = tile[:crow]
                mb[t, 1, :crow, :] = tile[crow:]

            def one(m):
                rows = pl.ds(m, lay.slots, stride=modes)
                left = [sa[q, s, rows, :] for q in range(4) for s in range(2)]
                right = [
                    jnp.concatenate([mb[2 * q, s, rows, :], mb[2 * q + 1, s, rows, :]], axis=1)
                    for q in range(4) for s in range(2)
                ]
                v = dot(
                    jnp.concatenate(left, axis=0).astype(BF),
                    jnp.concatenate(right, axis=0).astype(BF),
                    ((0,), (0,)),
                )
                return v[:C]

            unroll = 2

            @pl.loop(0, modes // (2 * unroll))
            def _(j):
                for u in range(unroll):
                    pair = j * unroll + u
                    v = pair_tiles(one(2 * pair), one(2 * pair + 1))
                    v = jnp.concatenate(v, axis=1).astype(BF)
                    w_rows[pl.ds(pl.multiple_of(pair * C, 16), C), :] = v

            for k in range(plan.pieces):
                p = c * plan.pieces + k
                w_part[p] = w_rows[k * plan.zrows : (k + 1) * plan.zrows, :]

                @pl.when(at_end)
                def _(p=p):
                    w_sum[p] = w_part[p]
                    send_inward(p)

        def sum_weights(c):
            for p in range(c * plan.pieces, (c + 1) * plan.pieces):
                @pl.when(jnp.logical_not(at_end))
                def _(p=p):
                    to_inner(p).wait_recv()
                    w_sum[p] = (w_part[p].astype(F32) + w_recv[p].astype(F32)).astype(BF)
                    send_inward(p)

        def cross_weights(c):
            for p in range(c * plan.pieces, (c + 1) * plan.pieces):
                @pl.when(at_middle)
                def _(p=p):
                    across(p).wait_recv()
                    w_full[p] = (w_sum[p].astype(F32) + w_cross[p].astype(F32)).astype(BF)

                    @pl.when(jnp.logical_not(at_end))
                    def _():
                        to_outer(p).start()

        def finish_weights(c):
            for p in range(c * plan.pieces, (c + 1) * plan.pieces):
                @pl.when(jnp.logical_not(at_middle))
                def _(p=p):
                    to_outer(p).wait_recv()

                    @pl.when(jnp.logical_not(at_end))
                    def _():
                        to_outer(p).start()

                weight_out[p * plan.zrows : (p + 1) * plan.zrows, :] = w_full[p]

        def lin_next(k):
            lin_step(k).wait_recv()
            v = lin_buf[k] + lin_recv[k]
            if k + 1 < stages:
                lin_buf[k + 1] = v
                lin_step(k + 1).start()
            else:
                lin_out[...] = v

        def chunk_total(c):
            ex.finish_sum(c, 1.0 / MX)
            weight_grad(c)
            ex.mix(c, ((1,), (1,)))

        last = plan.count - 1
        items = [(1 + k, lambda k=k: lin_next(k)) for k in range(z_bits)]
        waves = ex.waves(chunk_total)
        first = plan.levels - 1
        for w, wave in enumerate(waves):
            step = (2, 3, 4, 6, 9, 12)[w] if w < 6 else last
            items += [(step, task) for task in wave]
            for lag, task in enumerate((weight_grad, sum_weights, cross_weights)):
                if lag and 0 <= w - first - lag < lay.chunks:
                    at = len(items) if lag < 2 else len(items) - len(wave)
                    items.insert(at, (step, lambda task=task, c=w - first - lag: task(c)))
            if w >= 3 and z_bits + w -3 < stages:
                items.append((step, lambda k=z_bits + w -3: lin_next(k)))
        for lag, task in ((1, sum_weights), (2, cross_weights)):
            items += [(last, lambda task=task, c=c: task(c))
                      for c in range(max(0, len(waves) - first - lag), lay.chunks)]
        items += [(last, lambda c=c: finish_weights(c)) for c in range(lay.chunks)]
        schedule(last, i, items)

        @pl.when(i == last)
        def _():
            ex.drain()
            d_stream.flush(plan.steps)
            for p in range(lay.chunks * plan.pieces):
                to_inner(p).wait_send()

                @pl.when(jnp.logical_not(at_end))
                def _(p=p):
                    to_outer(p).wait_send()

            for k in range(stages):
                lin_step(k).wait_send()

    acc = lay.acc_rows
    dma = pltpu.SemaphoreType.DMA
    return pl.pallas_call(
        kernel,
        grid=(plan.count,),
        in_specs=[
            ANYWHERE,
            plain_fields(plan)[1],
            ANYWHERE,
            plain_fields(plan)[1],
            fixed((W, 1024)),
            fixed((4, C, C)),
            fixed(spectrum.shape),
            fixed((W, W)),
            fixed((W, 128)),
            fixed(pick_all.shape),
            fixed(move_all.shape),
            fixed(move_lin.shape),
            fixed(zero_lanes.shape),
            ANYWHERE,
            ANYWHERE,
        ],
        out_specs=[
            ANYWHERE,
            plain_fields(plan)[1],
            ANYWHERE,
            fixed((lay.chunks * plan.wrows, 2 * W)),
            fixed((C + 8, W)),
        ],
        out_shape=[
            jax.ShapeDtypeStruct(p_big.shape, BF),
            jax.ShapeDtypeStruct(p_small.shape, BF),
            jax.ShapeDtypeStruct((plan.chips, 2, plan.by_pairs.total, 2 * W), BF),
            jax.ShapeDtypeStruct((lay.chunks * plan.wrows, 2 * W), BF),
            jax.ShapeDtypeStruct((C + 8, W), F32),
        ],
        scratch_shapes=[
            pltpu.VMEM((plan.chips, 2, plan.by_pairs.total, 2 * W), BF),
            pltpu.VMEM((W, W), BF),
            pltpu.VMEM((4, 2, acc, 128), F32),
            pltpu.VMEM((8, 2, acc, 128), F32),
            pltpu.VMEM((plan.wrows, 2 * W), BF),
            *[pltpu.VMEM((lay.chunks * plan.pieces, plan.zrows, 2 * W), BF)] * 5,
            pltpu.VMEM((stages, C + 8, W), F32),
            pltpu.VMEM((stages, C + 8, W), F32),
            dma((1 + lay.chunks,)),
            *[dma((lay.chunks * plan.pieces,))] * 5,
            dma((stages,)),
            dma((stages,)),
            *Stream.scratch(min(4, plan.steps), 2 * plan.per, big.cells),
            *Stream.scratch(min(4, plan.steps), 2 * plan.per, big.cells),
            *Stream.scratch(min(3, plan.steps), 2 * plan.per, big.cells),
            *Exchange.scratch(plan, lay),
        ],
        compiler_params=params(collective_id=2, has_side_effects=True),
        name="mode_backward",
    )(p_big, p_small, g_big, g_small, expand_tables(), lin_weight, spectrum, lin_grad, columns,
      pick_all, move_all, move_lin, zero_lanes, part, kernel_all)


def input_grads(plan, rank, part_big, part_small, modes, lin_sum, weights):
    big, small = plan.big, plan.small
    per, steps = plan.wide_per, plan.wide_steps
    last = steps - 1

    split = np.zeros((W, 4, 128), np.float32)
    for p in range(4):
        split[p * C : p * C + C, p, :C] = np.eye(C)
    split = split.reshape(W, 512)
    blades = np.zeros((2, 2 * W, 4, 128), np.float32)
    for odd in range(2):
        for lane in range(W):
            at = lane + 128 * odd if lane < 128 else 128 + 64 * odd + lane
            blades[odd, at, lane // C, lane % C] = 1.0
    blades = low(blades.reshape(2, 2 * W, 512))
    lay = plan.by_modes

    def body(r, pb, ps, mb, ms, vb, eb, vs, es, lin, cut, w_in, blade,
             db, ds, lin_out, bias_out, w_out, w_held, w_sem):
        i = pl.program_id(0)
        put = pltpu.make_async_copy(w_held, w_out, w_sem.at[0])

        @pl.when(i == 0)
        def _():
            v = lax.dot_general(
                lin[...], cut[...], (((1,), (0,)), ((), ())),
                precision=lax.Precision.HIGHEST, preferred_element_type=F32,
            )
            for p in range(4):
                lin_out[p] = v[:C, 128 * p : 128 * p + C]
                bias_out[p : p + 1, :] = v[C : C + 1, 128 * p : 128 * p + C]
            for c in range(lay.chunks):
                rows = w_in[c * plan.wrows : (c + 1) * plan.wrows, :]
                for odd in range(2):
                    v = dot(rows, blade[odd])
                    for j in range(lay.modes // 2):
                        for p in range(4):
                            w_held[lay.first_mode(c) + 2 * j + odd, p] = (
                                v[j * C : j * C + C, 128 * p : 128 * p + C]
                            )
            put.start()

        @pl.when(i == steps)
        def _():
            put.wait()

        def run(part, m, d, geo, inverse, spread, count):
            span = spread.shape[1]
            qs = []
            for pair in range(count):
                qs += inverse_pair(geo, load_by_modes(plan, m, pair), inverse[...], 1.0)
            q = jnp.concatenate(qs, axis=0) * jnp.asarray(1.0 / geo.side, BF)
            for j in range(geo.cells // span):
                v = dot(q[:, 128 * j : 128 * j + 128], spread[...])
                at = (slice(0, 2 * count), slice(None), slice(None),
                      slice(j * span, (j + 1) * span))
                d[at] = part[at].astype(F32) + v.reshape(2 * count, 4, C, span)

        @pl.when(i < steps)
        def _():
            run(pb, mb, db, big, vb, eb, per)

        @pl.when(i == steps)
        def _():
            run(ps, ms, ds, small, vs, es, plan.nsmall // 2)

    extra = [lin_sum, split, weights, blades]
    tables = []
    specs = []
    for geo in (big, small):
        tables += [geo.inverse, geo.spread]
        specs += [device_spec(geo.inverse.shape[1:]), const_spec(geo.spread.shape)]
    small_field = field_specs(plan)[1]
    big_field = pl.BlockSpec((2 * per, 4, C, big.cells), lambda i, r: (wide(i, last), 0, 0, 0))
    return pl.pallas_call(
        body,
        grid_spec=pltpu.PrefetchScalarGridSpec(
            num_scalar_prefetch=1,
            grid=(steps + 1,),
            in_specs=[
                big_field,
                small_field,
                pl.BlockSpec(
                    (plan.n, lay.chunks, per * lay.modes, 2 * W),
                    lambda i, r: (0, 0, wide(i, last), 0),
                ),
                pl.BlockSpec(
                    (plan.n, lay.chunks, plan.per * lay.modes, 2 * W),
                    lambda i, r: (0, 0, plan.steps, 0),
                ),
                *specs,
                *[const_spec(v.shape) for v in extra],
            ],
            out_specs=[big_field, small_field, const_spec((4, C, C)), const_spec((4, C)),
                       ANYWHERE],
            scratch_shapes=[
                pltpu.VMEM((plan.own, 4, C, C), F32), pltpu.SemaphoreType.DMA((1,))
            ],
        ),
        out_shape=[
            jax.ShapeDtypeStruct(part_big.shape, F32),
            jax.ShapeDtypeStruct(part_small.shape, F32),
            jax.ShapeDtypeStruct((4, C, C), F32),
            jax.ShapeDtypeStruct((4, C), F32),
            jax.ShapeDtypeStruct((plan.own, 4, C, C), F32),
        ],
        compiler_params=params(),
        name="input_grads",
    )(rank, part_big, part_small, modes, modes, *tables, *extra)


def on_device(plan, x_big, x_small, spec_weight, lin_weight, lin_bias, grad_big, grad_small):
    rank = lax.axis_index("rows").reshape(1)
    width = 2 * W
    modes, kernel, spectrum = forward_kernel(plan, x_big, x_small, spec_weight)
    out_big, out_small, pre_big, pre_small, part, lin_grad, columns = cells_pass(
        plan, rank, x_big, x_small, grad_big, grad_small, modes.reshape(plan.n, -1, width),
        lin_weight, lin_bias,
    )
    lay = plan.by_modes
    part_big, part_small, modes, weights, lin_sum = backward_kernel(
        plan, part.reshape((plan.chips, 2) + part.shape[1:]), pre_big, pre_small,
        grad_big, grad_small, kernel, spectrum.reshape(-1, plan.own, width), lin_weight,
        lin_grad, columns,
    )
    dx_big, dx_small, lin_weight_grad, lin_bias_grad, spec_grad = input_grads(
        plan, rank, part_big, part_small, modes.reshape(plan.n, lay.chunks, -1, width),
        lin_sum, weights,
    )
    return out_big, out_small, dx_big, dx_small, spec_grad, lin_weight_grad, lin_bias_grad


def solution(mesh):
    fields = P("samples", None, None, "rows")
    spec = P("rows", None, None, None)

    def run(x_big, x_small, *rest):
        count = mesh.shape["samples"]
        plan = Plan(mesh, x_big.shape[0] // count, x_small.shape[0] // count)

        def local(*args):
            return on_device(plan, *args)

        return jax.shard_map(
            local,
            mesh=mesh,
            in_specs=(fields, fields, spec, P(), P(), fields, fields),
            out_specs=(fields, fields, fields, fields, spec, P(), P()),
            check_vma=False,
        )(x_big, x_small, *rest)

    return run
```
